256 devices in a mesh: tile: 128 (over y_lo, z, x, core), mode: 2 (over y_hi).
Axes of the slice: x: 4, y: 4 (y_hi: 2, y_lo: 2; y = y_hi * 2 + y_lo), z: 8, core: 2. Of those that a mesh axis runs over, the one named last changes fastest.
Arguments:
- object_tiles: float32 [128, 2, 2, 256, 256], P('tile'), may hold values from -1.5 to 1.5
- probe_modes: float32 [2, 12, 256, 256], P(None, 'mode'), may hold values from -0.9 to 0.9
- propagator: bfloat16 [2, 256, 256], replicated, may hold values from -1.5 to 1.5
- offsets: int32 [128, 2, 2], P('tile'), may hold values from -128 to 127
- counts: int32 [128], P('tile'), may hold values from 1 to 2, as said below
- measured: float32 [128, 2, 256, 256], P('tile'), may hold values from 0.3 to 3
Outputs:
- object_grad: float32 [128, 2, 2, 256, 256], P('tile')
- probe_grad: float32 [128, 2, 12, 256, 256], P('tile', None, 'mode')
The draws below stay inside these ranges and needn't reach their ends.
Inputs may be any that keep to these rules, and one draw needn't show every extreme that they name: `counts`: each tile holds at least one position, and some tile holds 2 in every draw.
All inputs are finite; a program needn't handle non-finite values.
Results may differ from the reference program's by a relative error of at most 0.015.
Values sent between devices are 32-bit elements; how exact they have to be, the bound alone decides.
No kernel may reach another device: no remote copies, remote signals or barrier semaphores. Data moves between devices by JAX's collectives and lax.ppermute only.
A program may use at most 128 MiB of HBM per device.

```python
import math
import jax
import jax.numpy as jnp
from jax import lax

PATCH = 256
MODES = 12
TILE = 256
SLOTS = 2
SLICES = 2
GY = 8
BAND = 16
TILES = 128
GX = 16
NX = 4096
NY = 2048


def draw_object_tiles(key, part):
    key = jax.random.fold_in(key, 11)
    real_key, imag_key = jax.random.split(key)
    shape = (TILES, SLICES, TILE, TILE)
    real_part = jax.random.uniform(real_key, shape, jnp.float32, 0.5, 1.5)
    imag_part = jnp.clip(0.3 * jax.random.normal(imag_key, shape, jnp.float32), -1.0, 1.0)
    return jnp.stack([real_part, imag_part], axis=1)


def draw_propagator(key, part):
    key = jax.random.fold_in(key, 12)
    real_key, imag_key = jax.random.split(key)
    counter = jnp.arange(PATCH)
    within = (jnp.abs(counter[:, None] - counter[None, :]) <= BAND).astype(jnp.float32)
    real_noise = jnp.clip(0.12 * jax.random.normal(real_key, (PATCH, PATCH), jnp.float32), -0.45, 0.45)
    imag_noise = jnp.clip(0.12 * jax.random.normal(imag_key, (PATCH, PATCH), jnp.float32), -0.45, 0.45)
    real_part = jnp.eye(PATCH, dtype=jnp.float32) + within * real_noise
    imag_part = within * imag_noise
    return jnp.stack([real_part, imag_part]).astype(jnp.bfloat16)


def draw_counts(key, part):
    key = jax.random.fold_in(key, 13)
    filled = jax.random.randint(key, (TILES,), 1, SLOTS + 1)
    return filled.at[0].set(SLOTS).astype(jnp.int32)


def with_ends(values, rng, least, high):
    index_at = [jax.random.randint(jax.random.fold_in(rng, axis), (), 0, length) for axis, length in enumerate(values.shape)]
    main_axis = values.shape.index(max(values.shape))
    beside = index_at[:main_axis] + [(index_at[main_axis] + 1) % values.shape[main_axis]] + index_at[main_axis + 1:]
    return values.at[tuple(index_at)].set(least).at[tuple(beside)].set(high)


def block_scale(own_key, shape, cuts, low, largest):
    def one(dim, parts):
        heights = jax.random.uniform(jax.random.fold_in(jax.random.fold_in(own_key, 6), dim), (parts,), jnp.float32, low / len(cuts), largest / len(cuts))
        return jnp.repeat(jnp.exp(heights), shape[dim] // parts).reshape((-1,) + (1,) * (len(shape) - dim - 1))

    level = one(*cuts[0])
    for cut in cuts[1:]:
        level = level * one(*cut)
    return level


def gaussian(rng, dims, spread, most, cuts=(), held_as=jnp.bfloat16):
    result = jax.random.normal(rng, dims, jnp.float32) * spread
    if len(cuts) > 0:
        result = block_scale(rng, dims, cuts, -0.22, 0.18) * result
    return jnp.clip(result, min=-most, max=most).astype(held_as)


def setup_inputs(seed: int = 0) -> dict:
    keys = jax.random.split(jax.random.key(seed), 7)
    return {
        "object_tiles": draw_object_tiles(jax.random.fold_in(keys[6], 71), 0),
        "probe_modes": gaussian(keys[1], (2, MODES, PATCH, PATCH), 0.15, 0.9, ((1, 2),), jnp.float32),
        "propagator": draw_propagator(jax.random.fold_in(keys[6], 71), 0),
        "offsets": with_ends(jax.random.randint(keys[3], (TILES, SLOTS, 2), -(PATCH // 2), TILE - PATCH // 2), jax.random.fold_in(keys[3], 1), -(PATCH // 2), (TILE - PATCH // 2) - 1).astype(jnp.int32),
        "counts": draw_counts(jax.random.fold_in(keys[6], 71), 0),
        "measured": jnp.clip(jnp.exp(math.log(3.0) - 2.3025851 * jax.random.uniform(keys[5], (TILES, SLOTS, PATCH, PATCH), jnp.float32) ** block_scale(keys[5], (TILES, SLOTS, PATCH, PATCH), ((0, 128),), -0.2, 0.2)), 0.3, 3.0),
    }


def complex_product(einsum_form, left_pair, right_pair):

    def single_product(first_op, second_op):
        return jnp.einsum(einsum_form, first_op.astype(jnp.float32), second_op.astype(jnp.float32), precision=lax.Precision.HIGHEST)
    real_part = single_product(left_pair[0], right_pair[0]) - single_product(left_pair[1], right_pair[1])
    imag_part = single_product(left_pair[0], right_pair[1]) + single_product(left_pair[1], right_pair[0])
    return (real_part, imag_part)

def rounded(pair):
    return (pair[0].astype(jnp.bfloat16), pair[1].astype(jnp.bfloat16))

def sandwich(left_form, left_matrix, right_form, right_matrix, wavefield):
    first_pass = complex_product(left_form, left_matrix, rounded(wavefield))
    return complex_product(right_form, rounded(first_pass), right_matrix)

def dft_table(extent):
    counter = jnp.arange(extent, dtype=jnp.int32)
    phase_step = counter[:, None] * counter[None, :] % extent
    phase_angle = -2.0 * math.pi / extent * phase_step.astype(jnp.float32)
    norm_scale = 1.0 / math.sqrt(extent)
    return ((jnp.cos(phase_angle) * norm_scale).astype(jnp.bfloat16), (jnp.sin(phase_angle) * norm_scale).astype(jnp.bfloat16))

def forward(probe_pair, patch_block, kernel_pair, dft_pair):
    wavefield = probe_pair
    fields = []
    layers = patch_block.shape[1]
    farfield = None
    for slice_index in range(layers):
        fields.append(wavefield)
        slab_re = patch_block[0, slice_index]
        slab_im = patch_block[1, slice_index]
        exit_re = wavefield[0] * slab_re - wavefield[1] * slab_im
        exit_im = wavefield[0] * slab_im + wavefield[1] * slab_re
        if slice_index + 1 < layers:
            wavefield = sandwich('ij,mjk->mik', kernel_pair, 'mij,kj->mik', kernel_pair, (exit_re, exit_im))
        else:
            farfield = sandwich('ij,mjk->mik', dft_pair, 'mij,jk->mik', dft_pair, (exit_re, exit_im))
    return (fields, farfield)

def backward(chi_field, fields, patch_block, kernel_pair, dft_pair):
    conj_table = (dft_pair[0], -dft_pair[1])
    conj_kernel = (kernel_pair[0], -kernel_pair[1])
    back_wave = sandwich('ij,mjk->mik', conj_table, 'mij,jk->mik', conj_table, chi_field)
    layers = patch_block.shape[1]
    slice_grads = [None] * layers
    bar_re, bar_im = back_wave
    for slice_index in reversed(range(layers)):
        wavefield = fields[slice_index]
        slab_re = patch_block[0, slice_index]
        slab_im = patch_block[1, slice_index]
        grad_re = lax.optimization_barrier(jnp.sum(wavefield[0] * back_wave[0] + wavefield[1] * back_wave[1], axis=0))
        grad_im = lax.optimization_barrier(jnp.sum(wavefield[0] * back_wave[1] - wavefield[1] * back_wave[0], axis=0))
        slice_grads[slice_index] = (grad_re, grad_im)
        bar_re = slab_re * back_wave[0] + slab_im * back_wave[1]
        bar_im = slab_re * back_wave[1] - slab_im * back_wave[0]
        if slice_index > 0:
            back_wave = sandwich('ji,mjk->mik', conj_kernel, 'mij,jk->mik', conj_kernel, (bar_re, bar_im))
    patch_grad = jnp.stack([jnp.stack([pair[0] for pair in slice_grads]), jnp.stack([pair[1] for pair in slice_grads])])
    return (patch_grad, (bar_re, bar_im))

def reference(object_tiles, probe_modes, propagator, offsets, counts, measured):
    margin = PATCH // 2
    dft_pair = dft_table(PATCH)
    kernel_pair = (propagator[0], propagator[1])
    probe_pair = (probe_modes[0], probe_modes[1])
    object_grid = object_tiles.reshape(GX, GY, 2, SLICES, TILE, TILE)
    object_grid = jnp.transpose(object_grid, (2, 3, 0, 4, 1, 5)).reshape(2, SLICES, NX, NY)
    padded = jnp.pad(object_grid, ((0, 0), (0, 0), (margin, margin), (margin, margin)))
    anchor = jnp.zeros((), jnp.int32)

    def visit_slot(loop_state, position):
        grad_canvas, probe_store = loop_state
        tile_index = position // SLOTS
        slot_index = position % SLOTS
        row_start = (tile_index // GY * TILE + offsets[tile_index, slot_index, 0] + margin).astype(jnp.int32)
        col_start = (tile_index % GY * TILE + offsets[tile_index, slot_index, 1] + margin).astype(jnp.int32)
        corner = (anchor, anchor, row_start, col_start)
        patch_block = lax.dynamic_slice(padded, corner, (2, SLICES, PATCH, PATCH))
        target = measured[tile_index, slot_index]

        def compute(unused):
            fields, farfield = forward(probe_pair, patch_block, kernel_pair, dft_pair)
            intensity = lax.optimization_barrier(jnp.sum(farfield[0] * farfield[0] + farfield[1] * farfield[1], axis=0))
            residual = intensity - target
            chi_field = (2.0 * residual * farfield[0], 2.0 * residual * farfield[1])
            patch_grad, probe_part = backward(chi_field, fields, patch_block, kernel_pair, dft_pair)
            return (patch_grad, jnp.stack(probe_part))

        def no_work(unused):
            return (jnp.zeros((2, SLICES, PATCH, PATCH), jnp.float32), jnp.zeros((2, MODES, PATCH, PATCH), jnp.float32))
        patch_grad, probe_part = lax.cond(slot_index < counts[tile_index], compute, no_work, 0)
        previous = lax.dynamic_slice(grad_canvas, corner, (2, SLICES, PATCH, PATCH))
        grad_canvas = lax.dynamic_update_slice(grad_canvas, previous + patch_grad, corner)
        probe_store = probe_store.at[tile_index].add(probe_part)
        return ((grad_canvas, probe_store), 0)
    start_state = (jnp.zeros(padded.shape, jnp.float32), jnp.zeros((TILES, 2, MODES, PATCH, PATCH), jnp.float32))
    final_state, unused = lax.scan(visit_slot, start_state, jnp.arange(TILES * SLOTS, dtype=jnp.int32))
    grad_canvas, probe_store = final_state
    interior = grad_canvas[:, :, margin:margin + NX, margin:margin + NY]
    interior = interior.reshape(2, SLICES, GX, TILE, GY, TILE)
    object_grad = jnp.transpose(interior, (2, 4, 0, 1, 3, 5)).reshape(TILES, 2, SLICES, TILE, TILE)
    return (object_grad, probe_store)
```

```python
import math

import jax
import jax.numpy as jnp
import ml_dtypes
import numpy as np
from jax import lax
from jax.experimental import pallas as pl
from jax.experimental.pallas import tpu as pltpu
from jax.sharding import PartitionSpec as P

GY = 8
F32 = jnp.float32
BF16 = jnp.bfloat16
VMEM_LIMIT = 40 * 1024 * 1024


def dft_pair(extent):
    counter = np.arange(extent)
    angle = -2.0 * math.pi / extent * (counter[:, None] * counter[None, :] % extent)
    scale = 1.0 / math.sqrt(extent)
    return (
        (np.cos(angle) * scale).astype(ml_dtypes.bfloat16),
        (np.sin(angle) * scale).astype(ml_dtypes.bfloat16),
    )


def left_form(re, im, xp):
    return xp.concatenate(
        [xp.concatenate([re, -im], axis=1), xp.concatenate([im, re], axis=1)], axis=0
    )


def right_form(re, im, xp):
    return xp.concatenate(
        [xp.concatenate([re, im], axis=1), xp.concatenate([-im, re], axis=1)], axis=0
    )


def sandwich(left, stacked, right):
    n = stacked.shape[1]
    half = jnp.dot(left, stacked, preferred_element_type=F32)
    beside = jnp.concatenate([half[:n].astype(BF16), half[n:].astype(BF16)], axis=1)
    both = jnp.dot(beside, right, preferred_element_type=F32)
    return both[:, :n], both[:, n:]


def stack_rounded(re, im):
    return jnp.concatenate([re.astype(BF16), im.astype(BF16)], axis=0)


def extract_kernel(off_ref, own, up, down, left, right, corner_l, corner_r, out, canvas):
    n = own.shape[-1]
    h = n // 2
    canvas[:, :, h : h + n, h : h + n] = own[...]
    canvas[:, :, 0:h, h : h + n] = up[...]
    canvas[:, :, h + n :, h : h + n] = down[...]
    canvas[:, :, h : h + n, 0:h] = left[...]
    canvas[:, :, h : h + n, h + n :] = right[...]
    canvas[:, :, 0:h, 0:h] = corner_l[0]
    canvas[:, :, h + n :, 0:h] = corner_l[1]
    canvas[:, :, 0:h, h + n :] = corner_r[0]
    canvas[:, :, h + n :, h + n :] = corner_r[1]
    for slot in range(out.shape[0]):
        row = off_ref[slot, 0] + h
        col = off_ref[slot, 1] + h
        top = pl.multiple_of((row >> 3) * 8, 8)
        block = pl.multiple_of((col >> 7) * 128, 128)
        row_rest, col_rest = row & 7, col & 127
        row_shift = jnp.where(row_rest == 0, 0, n + 8 - row_rest)
        col_shift = jnp.where(col_rest == 0, 0, n + h - col_rest)
        for part in range(2):
            for layer in range(2):
                window = canvas[part, layer, pl.ds(top, n + 8), pl.ds(block, n + h)]
                window = pltpu.roll(window, col_shift, 1)[:, :n]
                out[slot, part, layer] = pltpu.roll(window, row_shift, 0)[:n]


def forward_kernel(probe, patch, prop_l, prop_r, dft_l, dft_r, wave, far, inten):
    first = pl.program_id(0) == 0
    p_re, p_im = probe[0, 0], probe[1, 0]
    o_re, o_im = patch[0, 0, 0], patch[0, 1, 0]
    e = stack_rounded(p_re * o_re - p_im * o_im, p_re * o_im + p_im * o_re)
    w_re, w_im = sandwich(prop_l[...], e, prop_r[...])
    wave[0, 0] = w_re
    wave[0, 1] = w_im
    o_re, o_im = patch[0, 0, 1], patch[0, 1, 1]
    e = stack_rounded(w_re * o_re - w_im * o_im, w_re * o_im + w_im * o_re)
    f_re, f_im = sandwich(dft_l[...], e, dft_r[...])
    far[0, 0] = f_re
    far[0, 1] = f_im
    part = f_re * f_re + f_im * f_im

    @pl.when(first)
    def _():
        inten[...] = part

    @pl.when(jnp.logical_not(first))
    def _():
        inten[...] += part


def back_last_kernel(
    slot, counts, mine, other, measured, far, wave, patch, cdft_l, cdft_r, grad, bar, resid
):
    first = pl.program_id(0) == 0

    @pl.when(first)
    def _():
        live = jnp.where(slot < counts[0], 2.0, 0.0).astype(F32)
        resid[...] = (mine[...] + other[...] - measured[0]) * live

    r = resid[...]
    c = stack_rounded(r * far[0, 0], r * far[0, 1])
    b_re, b_im = sandwich(cdft_l[...], c, cdft_r[...])
    w_re, w_im = wave[0, 0], wave[0, 1]
    g_re = w_re * b_re + w_im * b_im
    g_im = w_re * b_im - w_im * b_re

    @pl.when(first)
    def _():
        grad[0] = g_re
        grad[1] = g_im

    @pl.when(jnp.logical_not(first))
    def _():
        grad[0] += g_re
        grad[1] += g_im

    o_re, o_im = patch[0, 0, 1], patch[0, 1, 1]
    bar[0] = stack_rounded(o_re * b_re + o_im * b_im, o_re * b_im - o_im * b_re)


def back_first_kernel(bar0, bar1, probe, patches, prop_l, prop_r, grad, probe_grad):
    first = pl.program_id(0) == 0
    p_re, p_im = probe[0, 0], probe[1, 0]
    sum_re = sum_im = None
    for slot, bar in enumerate((bar0, bar1)):
        b_re, b_im = sandwich(prop_l[...], bar[0], prop_r[...])
        g_re = p_re * b_re + p_im * b_im
        g_im = p_re * b_im - p_im * b_re

        @pl.when(first)
        def _():
            grad[slot, 0] = g_re
            grad[slot, 1] = g_im

        @pl.when(jnp.logical_not(first))
        def _():
            grad[slot, 0] += g_re
            grad[slot, 1] += g_im

        o_re, o_im = patches[slot, 0, 0], patches[slot, 1, 0]
        q_re = o_re * b_re + o_im * b_im
        q_im = o_re * b_im - o_im * b_re
        sum_re = q_re if sum_re is None else sum_re + q_re
        sum_im = q_im if sum_im is None else sum_im + q_im
    probe_grad[0, 0, 0] = sum_re
    probe_grad[0, 1, 0] = sum_im


def place_kernel(off_ref, grad0, grad1, out_l, out_c, out_r, canvas):
    n = grad0.shape[-1]
    h = n // 2
    canvas[...] = jnp.zeros_like(canvas)
    for slot, grad in enumerate((grad0, grad1)):
        row = off_ref[slot, 0] + h
        col = off_ref[slot, 1] + h
        top = pl.multiple_of((row >> 3) * 8, 8)
        block = pl.multiple_of((col >> 7) * 128, 128)
        for part in range(2):
            tall = jnp.concatenate([grad[part], jnp.zeros((8, n), F32)], axis=0)
            tall = pltpu.roll(tall, row & 7, 0)
            wide = jnp.concatenate([tall, jnp.zeros((n + 8, h), F32)], axis=1)
            wide = pltpu.roll(wide, col & 127, 1)
            canvas[part, pl.ds(top, n + 8), pl.ds(block, n + h)] += wide
    out_l[...] = canvas[:, :, 0:h]
    out_c[...] = canvas[:, :, h : h + n]
    out_r[...] = canvas[:, :, h + n :]


def rows_by(value, step):
    count = lax.axis_size("tile")
    pairs = [(i, i + GY * step) for i in range(count) if 0 <= i + GY * step < count]
    return lax.ppermute(value, "tile", pairs)


def cols_by(value, step):
    count = lax.axis_size("tile")
    pairs = [(i, i + step) for i in range(count) if 0 <= i % GY + step < GY]
    return lax.ppermute(value, "tile", pairs)


def swap_mode(value):
    return lax.ppermute(value, "mode", [(0, 1), (1, 0)])


def params(grid):
    return pltpu.CompilerParams(
        dimension_semantics=("arbitrary",) * grid, vmem_limit_bytes=VMEM_LIMIT
    )


def whole(shape):
    return pl.BlockSpec(shape, lambda m: (0,) * len(shape))


SMEM = pl.BlockSpec(memory_space=pltpu.SMEM)


def body(object_tiles, probe_modes, propagator, offsets, counts, measured):
    n = probe_modes.shape[-1]
    h = n // 2
    modes = probe_modes.shape[1]
    slots = measured.shape[1]
    own = object_tiles[0]
    off = offsets[0]

    down_strip = rows_by(own[:, :, :h, :], -1)
    up_strip = rows_by(own[:, :, h:, :], 1)
    left_strip = cols_by(own[:, :, :, h:], 1)
    right_strip = cols_by(own[:, :, :, :h], -1)
    corner_l = cols_by(jnp.stack([up_strip[..., h:], down_strip[..., h:]]), 1)
    corner_r = cols_by(jnp.stack([up_strip[..., :h], down_strip[..., :h]]), -1)

    k_re, k_im = propagator[0], propagator[1]
    prop_l = left_form(k_re, k_im, jnp)
    prop_r = right_form(k_re.T, k_im.T, jnp)
    back_prop_l = left_form(k_re.T, -k_im.T, jnp)
    back_prop_r = right_form(k_re, -k_im, jnp)
    f_re, f_im = dft_pair(n)
    dft_l = jnp.asarray(left_form(f_re, f_im, np))
    dft_r = jnp.asarray(right_form(f_re, f_im, np))
    cdft_l = jnp.asarray(left_form(f_re, -f_im, np))
    cdft_r = jnp.asarray(right_form(f_re, -f_im, np))

    vmem = pl.BlockSpec(memory_space=pltpu.VMEM)
    patches = pl.pallas_call(
        extract_kernel,
        out_shape=jax.ShapeDtypeStruct((slots, 2, 2, n, n), F32),
        in_specs=[SMEM] + [vmem] * 7,
        out_specs=vmem,
        scratch_shapes=[pltpu.VMEM((2, 2, 2 * n, 2 * n), F32)],
        compiler_params=pltpu.CompilerParams(vmem_limit_bytes=VMEM_LIMIT),
        name="extract",
    )(off, own, up_strip, down_strip, left_strip, right_strip, corner_l, corner_r)

    mat = whole((2 * n, 2 * n))
    probe_spec = pl.BlockSpec((2, 1, n, n), lambda m: (0, m, 0, 0))
    field_spec = pl.BlockSpec((1, 2, n, n), lambda m: (m, 0, 0, 0))
    field_shape = jax.ShapeDtypeStruct((modes, 2, n, n), F32)
    plane = jax.ShapeDtypeStruct((n, n), F32)

    def patch_spec(slot):
        return pl.BlockSpec((1, 2, 2, n, n), lambda m: (slot, 0, 0, 0, 0))

    waves, fars, intens = [], [], []
    for slot in range(slots):
        wave, far, inten = pl.pallas_call(
            forward_kernel,
            grid=(modes,),
            out_shape=(field_shape, field_shape, plane),
            in_specs=[probe_spec, patch_spec(slot), mat, mat, mat, mat],
            out_specs=(field_spec, field_spec, whole((n, n))),
            compiler_params=params(1),
            name=f"forward_{slot}",
        )(probe_modes, patches, prop_l, prop_r, dft_l, dft_r)
        waves.append(wave)
        fars.append(far)
        intens.append(inten)
    others = [swap_mode(inten) for inten in intens]

    bar_spec = pl.BlockSpec((1, 2 * n, n), lambda m: (m, 0, 0))
    grads_last, bars = [], []
    for slot in range(slots):
        grad, bar = pl.pallas_call(
            lambda *refs, slot=slot: back_last_kernel(slot, *refs),
            grid=(modes,),
            out_shape=(
                jax.ShapeDtypeStruct((2, n, n), F32),
                jax.ShapeDtypeStruct((modes, 2 * n, n), BF16),
            ),
            in_specs=[
                SMEM,
                whole((n, n)),
                whole((n, n)),
                pl.BlockSpec((1, n, n), lambda m, slot=slot: (slot, 0, 0)),
                field_spec,
                field_spec,
                patch_spec(slot),
                mat,
                mat,
            ],
            out_specs=(whole((2, n, n)), bar_spec),
            scratch_shapes=[pltpu.VMEM((n, n), F32)],
            compiler_params=params(1),
            name=f"back_last_{slot}",
        )(counts, intens[slot], others[slot], measured[0], fars[slot], waves[slot], patches,
          cdft_l, cdft_r)
        grads_last.append(grad)
        bars.append(bar)

    def place(grad0, grad1, name):
        return pl.pallas_call(
            place_kernel,
            out_shape=(
                jax.ShapeDtypeStruct((2, 2 * n, h), F32),
                jax.ShapeDtypeStruct((2, 2 * n, n), F32),
                jax.ShapeDtypeStruct((2, 2 * n, h), F32),
            ),
            in_specs=[SMEM, vmem, vmem],
            out_specs=(vmem, vmem, vmem),
            scratch_shapes=[pltpu.VMEM((2, 2 * n, 2 * n), F32)],
            compiler_params=pltpu.CompilerParams(vmem_limit_bytes=VMEM_LIMIT),
            name=name,
        )(off, grad0, grad1)

    def collect(grad0, grad1, name):
        out_l, out_c, out_r = place(grad0, grad1, name)
        from_left = cols_by(out_r, 1)
        from_right = cols_by(out_l, -1)
        tall = out_c + jnp.concatenate([from_left, from_right], axis=2)
        from_up = rows_by(tall[:, n + h :, :], 1)
        from_down = rows_by(tall[:, :h, :], -1)
        mine = tall[:, h : h + n, :] + jnp.concatenate([from_up, from_down], axis=1)
        return mine + swap_mode(mine)

    last = collect(grads_last[0], grads_last[1], "place_last")

    grads_first, probe_grad = pl.pallas_call(
        back_first_kernel,
        grid=(modes,),
        out_shape=(
            jax.ShapeDtypeStruct((slots, 2, n, n), F32),
            jax.ShapeDtypeStruct((1, 2, modes, n, n), F32),
        ),
        in_specs=[bar_spec, bar_spec, probe_spec, whole((slots, 2, 2, n, n)), mat, mat],
        out_specs=(
            whole((slots, 2, n, n)),
            pl.BlockSpec((1, 2, 1, n, n), lambda m: (0, 0, m, 0, 0)),
        ),
        compiler_params=params(1),
        name="back_first",
    )(bars[0], bars[1], probe_modes, patches, back_prop_l, back_prop_r)
    first = collect(grads_first[0], grads_first[1], "place_first")
    object_grad = jnp.stack([first, last], axis=1)
    return (object_grad.reshape(object_tiles.shape), probe_grad)


def solution(mesh):
    placed = (
        P("tile", None, None, None, None),
        P(None, "mode", None, None),
        P(),
        P("tile", None, None),
        P("tile"),
        P("tile", None, None, None),
    )
    return jax.shard_map(
        body,
        mesh=mesh,
        in_specs=placed,
        out_specs=(P("tile", None, None, None, None), P("tile", None, "mode", None, None)),
        check_vma=False,
    )
```

```python
import functools
import math

import jax
import jax.numpy as jnp
import ml_dtypes
import numpy as np
from jax import lax
from jax.experimental import pallas as pl
from jax.experimental.pallas import tpu as pltpu
from jax.sharding import PartitionSpec as P

GY = 8
F32 = jnp.float32
BF16 = jnp.bfloat16
VMEM_LIMIT = 24 * 1024 * 1024


def dft_pair(extent):
    counter = np.arange(extent)
    angle = -2.0 * math.pi / extent * (counter[:, None] * counter[None, :] % extent)
    scale = 1.0 / math.sqrt(extent)
    return (
        (np.cos(angle) * scale).astype(ml_dtypes.bfloat16),
        (np.sin(angle) * scale).astype(ml_dtypes.bfloat16),
    )


def left_form(re, im, xp):
    return xp.concatenate(
        [xp.concatenate([re, -im], axis=1), xp.concatenate([im, re], axis=1)], axis=0
    )


def right_form(re, im, xp):
    return xp.concatenate(
        [xp.concatenate([re, im], axis=1), xp.concatenate([-im, re], axis=1)], axis=0
    )


def dft_tables(extent):
    re, im = dft_pair(extent)
    h = extent // 2

    def tables(re, im, evens_first):
        by_row = [(re[b::2, :h], im[b::2, :h]) for b in range(2)]
        by_col = [(re[:h, b::2], im[:h, b::2]) for b in range(2)]
        lefts, rights = (by_row, by_col) if evens_first else (by_col, by_row)
        return np.stack(
            [left_form(*pair, np) for pair in lefts] + [right_form(*pair, np) for pair in rights]
        )

    return tables(re, im, True), tables(re, -im, False)


def mm(a, b):
    return jnp.dot(a, b, preferred_element_type=F32)


def beside(a, b):
    return jnp.concatenate([a, b], axis=1)


def above(a, b):
    return jnp.concatenate([a, b], axis=0)


def sandwich(left, re, im, right):
    n = re.shape[0]
    half = mm(left, above(re.astype(BF16), im.astype(BF16)))
    both = mm(beside(half[:n].astype(BF16), half[n:].astype(BF16)), right)
    return both[:, :n], both[:, n:]


def dft_sandwich(tabs, re, im):
    h = re.shape[0] // 2
    even = mm(tabs[0], above(re[:h] + re[h:], im[:h] + im[h:]).astype(BF16))
    odd = mm(tabs[1], above(re[:h] - re[h:], im[:h] - im[h:]).astype(BF16))
    re, im = above(even[:h], odd[:h]), above(even[h:], odd[h:])
    e = mm(beside(re[:, :h] + re[:, h:], im[:, :h] + im[:, h:]).astype(BF16), tabs[2])
    o = mm(beside(re[:, :h] - re[:, h:], im[:, :h] - im[:, h:]).astype(BF16), tabs[3])
    return e, o


def conj_dft_sandwich(tabs, e, o):
    h = e.shape[0] // 2
    e, o = e.astype(BF16), o.astype(BF16)
    even = mm(tabs[0], above(beside(e[:h, :h], o[:h, :h]), beside(e[:h, h:], o[:h, h:])))
    odd = mm(tabs[1], above(beside(e[h:, :h], o[h:, :h]), beside(e[h:, h:], o[h:, h:])))
    re = above(even[:h] + odd[:h], even[:h] - odd[:h]).astype(BF16)
    im = above(even[h:] + odd[h:], even[h:] - odd[h:]).astype(BF16)
    e = mm(beside(re[:, :h], im[:, :h]), tabs[2])
    o = mm(beside(re[:, h:], im[:, h:]), tabs[3])
    return (
        beside(e[:, :h] + o[:, :h], e[:, :h] - o[:, :h]),
        beside(e[:, h:] + o[:, h:], e[:, h:] - o[:, h:]),
    )


def place_of(off_ref, slot, h):
    row = off_ref[slot, 0] + h
    col = off_ref[slot, 1] + h
    top = pl.multiple_of((row >> 3) * 8, 8)
    block = pl.multiple_of((col >> 7) * 128, 128)
    return top, block, row & 7, col & 127


def build_canvas(own, up, down, left, right, corner_l, corner_r, canvas):
    n = own.shape[-1]
    h = n // 2
    canvas[:, :, h : h + n, h : h + n] = own[...]
    canvas[:, :, 0:h, h : h + n] = up[...]
    canvas[:, :, h + n :, h : h + n] = down[...]
    canvas[:, :, h : h + n, 0:h] = left[...]
    canvas[:, :, h : h + n, h + n :] = right[...]
    canvas[:, :, 0:h, 0:h] = corner_l[0]
    canvas[:, :, h + n :, 0:h] = corner_l[1]
    canvas[:, :, 0:h, h + n :] = corner_r[0]
    canvas[:, :, h + n :, h + n :] = corner_r[1]


def extract(off_ref, slot, canvas, patch):
    n = patch.shape[-1]
    h = n // 2
    top, block, row_rest, col_rest = place_of(off_ref, slot, h)
    row_shift = jnp.where(row_rest == 0, 0, n + 8 - row_rest)
    col_shift = jnp.where(col_rest == 0, 0, n + h - col_rest)
    for part in range(2):
        for layer in range(2):
            window = canvas[part, layer, pl.ds(top, n + 8), pl.ds(block, n + h)]
            window = pltpu.roll(window, col_shift, 1)[:, :n]
            patch[part, layer] = pltpu.roll(window, row_shift, 0)[:n]


def place(off_ref, grads, out_l, out_c, out_r, canvas):
    n = grads[0].shape[-1]
    h = n // 2
    canvas[...] = jnp.zeros_like(canvas)
    for slot, grad in enumerate(grads):
        top, block, row_rest, col_rest = place_of(off_ref, slot, h)
        for part in range(2):
            tall = above(grad[part], jnp.zeros((8, n), F32))
            tall = pltpu.roll(tall, row_rest, 0)
            wide = beside(tall, jnp.zeros((n + 8, h), F32))
            canvas[part, pl.ds(top, n + 8), pl.ds(block, n + h)] += pltpu.roll(wide, col_rest, 1)
    out_l[...] = canvas[:, :, 0:h]
    out_c[...] = canvas[:, :, h : h + n]
    out_r[...] = canvas[:, :, h + n :]


def each_mode(modes, step):
    def pair(i, carry):
        for j in range(2):
            step(i * 2 + j)
        return carry

    lax.fori_loop(0, modes // 2, pair, 0)


def forward(probe, patch, prop_l, prop_r, tabs, wave, far, inten):
    n = inten.shape[0]
    h = n // 2
    inten[...] = jnp.zeros_like(inten)

    def step(m):
        p_re, p_im = probe[0, m], probe[1, m]
        o_re, o_im = patch[0, 0], patch[1, 0]
        w_re, w_im = sandwich(
            prop_l[...], p_re * o_re - p_im * o_im, p_re * o_im + p_im * o_re, prop_r[...]
        )
        wave[m, 0] = w_re
        wave[m, 1] = w_im
        o_re, o_im = patch[0, 1], patch[1, 1]
        e, o = dft_sandwich(tabs, w_re * o_re - w_im * o_im, w_re * o_im + w_im * o_re)
        far[m, 0] = e
        far[m, 1] = o
        e, o = e * e, o * o
        inten[...] += beside(e[:, :h] + e[:, h:], o[:, :h] + o[:, h:])

    each_mode(probe.shape[1], step)


def forward_first_kernel(off, own, up, down, left, right, corner_l, corner_r, probe, prop_l,
                         prop_r, tabs, canvas, patch, wave, far, inten):
    build_canvas(own, up, down, left, right, corner_l, corner_r, canvas)
    extract(off, 0, canvas, patch)
    forward(probe, patch, prop_l, prop_r, tabs, wave, far, inten)


def forward_next_kernel(slot, off, canvas, probe, prop_l, prop_r, tabs, patch, wave, far, inten):
    extract(off, slot, canvas, patch)
    forward(probe, patch, prop_l, prop_r, tabs, wave, far, inten)


def back_last(slot, counts, mine, other, measured, far, wave, patch, tabs, grad, bar, resid):
    n = mine.shape[0]
    h = n // 2
    live = jnp.where(slot < counts[0], 2.0, 0.0).astype(F32)
    r = (mine[...] + other[...] - measured[slot]) * live
    resid[0] = beside(r[:, :h], r[:, :h])
    resid[1] = beside(r[:, h:], r[:, h:])
    grad[...] = jnp.zeros_like(grad)

    def step(m):
        b_re, b_im = conj_dft_sandwich(tabs, resid[0] * far[m, 0], resid[1] * far[m, 1])
        w_re, w_im = wave[m, 0], wave[m, 1]
        grad[0] += w_re * b_re + w_im * b_im
        grad[1] += w_re * b_im - w_im * b_re
        o_re, o_im = patch[0, 1], patch[1, 1]
        bar[m, 0] = (o_re * b_re + o_im * b_im).astype(BF16)
        bar[m, 1] = (o_re * b_im - o_im * b_re).astype(BF16)

    each_mode(far.shape[0], step)


def back_last_place_kernel(slot, counts, off, before, mine, other, measured, far, wave, patch,
                           tabs, bar, out_l, out_c, out_r, resid, grad, canvas):
    back_last(slot, counts, mine, other, measured, far, wave, patch, tabs, grad, bar, resid)
    place(off, (before, grad), out_l, out_c, out_r, canvas)


def back_first(bar, probe, patch, prop_l, prop_r, grad, emit):
    grad[...] = jnp.zeros_like(grad)

    def step(m):
        b_re, b_im = sandwich(prop_l[...], bar[m, 0], bar[m, 1], prop_r[...])
        p_re, p_im = probe[0, m], probe[1, m]
        grad[0] += p_re * b_re + p_im * b_im
        grad[1] += p_re * b_im - p_im * b_re
        o_re, o_im = patch[0, 0], patch[1, 0]
        emit(m, o_re * b_re + o_im * b_im, o_re * b_im - o_im * b_re)

    each_mode(probe.shape[1], step)


def back_first_kernel(bar, probe, patch, prop_l, prop_r, grad, part):
    def emit(m, re, im):
        part[0, m] = re
        part[1, m] = im

    back_first(bar, probe, patch, prop_l, prop_r, grad, emit)


def back_first_add_kernel(bar, probe, patch, prop_l, prop_r, part, grad, total):
    def emit(m, re, im):
        total[0, 0, m] = part[0, m] + re
        total[0, 1, m] = part[1, m] + im

    back_first(bar, probe, patch, prop_l, prop_r, grad, emit)


def place_kernel(off, grad0, grad1, out_l, out_c, out_r, canvas):
    place(off, (grad0, grad1), out_l, out_c, out_r, canvas)


def prepare_kernel(prop, probe, measured, order, order_t, dft_in, conj_in, prop_l, prop_r,
                   back_l, back_r, probe_out, meas_out, dft_out, conj_out):
    re, im = prop[0].astype(F32), prop[1].astype(F32)
    re_t, im_t = re.T, im.T
    prop_l[...] = left_form(re, im, jnp).astype(BF16)
    prop_r[...] = right_form(re_t, im_t, jnp).astype(BF16)
    back_l[...] = left_form(re_t, -im_t, jnp).astype(BF16)
    back_r[...] = right_form(re, -im, jnp).astype(BF16)
    probe_out[...] = probe[...]
    dft_out[...] = dft_in[...]
    conj_out[...] = conj_in[...]
    exact = functools.partial(
        jnp.dot, precision=lax.Precision.HIGHEST, preferred_element_type=F32
    )
    for slot in range(measured.shape[0]):
        meas_out[slot] = exact(exact(order[...], measured[slot]), order_t[...])


def rows_by(value, step):
    count = lax.axis_size("tile")
    pairs = [(i, i + GY * step) for i in range(count) if 0 <= i + GY * step < count]
    return lax.ppermute(value, "tile", pairs)


def cols_by(value, step):
    count = lax.axis_size("tile")
    pairs = [(i, i + step) for i in range(count) if 0 <= i % GY + step < GY]
    return lax.ppermute(value, "tile", pairs)


def swap_mode(value):
    return lax.ppermute(value, "mode", [(0, 1), (1, 0)])


def call(kernel, name, outs, args, scratch=(), smem=1, after=()):
    vmem = pl.BlockSpec(memory_space=pltpu.VMEM)
    scalars = pl.BlockSpec(memory_space=pltpu.SMEM)
    n_args, n_after = len(args), len(after)

    def run(*refs):
        kernel(*refs[:n_args], *refs[n_args + n_after :])

    return pl.pallas_call(
        run,
        out_shape=tuple(jax.ShapeDtypeStruct(shape, dtype) for shape, dtype in outs),
        in_specs=[scalars] * smem
        + [vmem] * (n_args - smem)
        + [pl.BlockSpec(memory_space=pl.ANY)] * n_after,
        out_specs=tuple(vmem for _ in outs),
        scratch_shapes=[pltpu.VMEM(shape, F32) for shape in scratch],
        compiler_params=pltpu.CompilerParams(vmem_limit_bytes=VMEM_LIMIT),
        name=name,
    )(*args, *after)


def body(object_tiles, probe_modes, propagator, offsets, counts, measured):
    n = probe_modes.shape[-1]
    h = n // 2
    modes = probe_modes.shape[1]
    slots = measured.shape[1]
    own = object_tiles[0]
    off = offsets[0]

    down_strip = rows_by(own[:, :, :h, :], -1)
    up_strip = rows_by(own[:, :, h:, :], 1)
    left_strip = cols_by(own[:, :, :, h:], 1)
    right_strip = cols_by(own[:, :, :, :h], -1)
    corner_l = cols_by(jnp.stack([up_strip[..., h:], down_strip[..., h:]]), 1)
    corner_r = cols_by(jnp.stack([up_strip[..., :h], down_strip[..., :h]]), -1)

    dft, conj_dft = dft_tables(n)
    order = np.eye(n, dtype=np.float32)[np.r_[0:n:2, 1:n:2]]
    plane, pair, mat = ((n, n), F32), ((2, n, n), F32), ((2 * n, 2 * n), BF16)
    patch_out, field = ((2, 2, n, n), F32), ((modes, 2, n, n), F32)
    probes, tables = ((2, modes, n, n), F32), (dft.shape, BF16)
    prop_l, prop_r, back_prop_l, back_prop_r, probe, measured, dft, conj_dft = call(
        prepare_kernel,
        "prepare",
        (mat, mat, mat, mat, probes, ((slots, n, n), F32), tables, tables),
        (propagator, probe_modes, measured[0], jnp.asarray(order), jnp.asarray(order.T.copy()),
         jnp.asarray(dft), jnp.asarray(conj_dft)),
        smem=0,
    )

    canvas, patch0, wave0, far0, inten0 = call(
        forward_first_kernel,
        "forward_0",
        (((2, 2, 2 * n, 2 * n), F32), patch_out, field, field, plane),
        (off, own, up_strip, down_strip, left_strip, right_strip, corner_l, corner_r,
         probe, prop_l, prop_r, dft),
    )
    other0 = swap_mode(inten0)
    patch1, wave1, far1, inten1 = call(
        functools.partial(forward_next_kernel, 1),
        "forward_1",
        (patch_out, field, field, plane),
        (off, canvas, probe, prop_l, prop_r, dft),
    )
    other1 = swap_mode(inten1)

    bar_out = ((modes, 2, n, n), BF16)
    strips = (((2, 2 * n, h), F32), ((2, 2 * n, n), F32), ((2, 2 * n, h), F32))
    wide = (2, 2 * n, 2 * n)
    grad_last0, bar0 = call(
        functools.partial(back_last, 0),
        "back_last_0",
        (pair, bar_out),
        (counts, inten0, other0, measured, far0, wave0, patch0, conj_dft),
        scratch=((2, n, n),),
    )
    grad_first0, part = call(
        back_first_kernel,
        "back_first_0",
        (pair, probes),
        (bar0, probe, patch0, back_prop_l, back_prop_r),
        smem=0,
    )
    bar1, out_l, out_c, out_r = call(
        functools.partial(back_last_place_kernel, 1),
        "back_last_1",
        (bar_out,) + strips,
        (counts, off, grad_last0, inten1, other1, measured, far1, wave1, patch1, conj_dft),
        scratch=((2, n, n), (2, n, n), wide),
        smem=2,
        after=(grad_first0,),
    )

    def add_cols(out_l, out_c, out_r):
        from_left = cols_by(out_r, 1)
        from_right = cols_by(out_l, -1)
        return out_c + jnp.concatenate([from_left, from_right], axis=2)

    def add_rows(tall):
        from_up = rows_by(tall[:, n + h :, :], 1)
        from_down = rows_by(tall[:, :h, :], -1)
        return tall[:, h : h + n, :] + jnp.concatenate([from_up, from_down], axis=1)

    tall_last = add_cols(out_l, out_c, out_r)
    grad_first1, probe_grad = call(
        back_first_add_kernel,
        "back_first_1",
        (pair, ((1, 2, modes, n, n), F32)),
        (bar1, probe, patch1, back_prop_l, back_prop_r, part),
        smem=0,
    )
    mine_last = add_rows(tall_last)
    other_last = swap_mode(mine_last)
    out_l, out_c, out_r = call(
        place_kernel,
        "place_first",
        strips,
        (off, grad_first0, grad_first1),
        scratch=(wide,),
        after=(tall_last,),
    )
    mine_first = add_rows(add_cols(out_l, out_c, out_r))
    other_first = swap_mode(mine_first)
    object_grad = jnp.stack([mine_first + other_first, mine_last + other_last], axis=1)
    return (object_grad.reshape(object_tiles.shape), probe_grad)


def solution(mesh):
    placed = (
        P("tile", None, None, None, None),
        P(None, "mode", None, None),
        P(),
        P("tile", None, None),
        P("tile"),
        P("tile", None, None, None),
    )
    return jax.shard_map(
        body,
        mesh=mesh,
        in_specs=placed,
        out_specs=(P("tile", None, None, None, None), P("tile", None, "mode", None, None)),
        check_vma=False,
    )
```

```python
import functools
import math

import jax
import jax.numpy as jnp
import ml_dtypes
import numpy as np
from jax import lax
from jax.experimental import pallas as pl
from jax.experimental.pallas import tpu as pltpu
from jax.sharding import PartitionSpec as P

GY = 8
BAND = 16
F32 = jnp.float32
BF16 = jnp.bfloat16
VMEM_LIMIT = 24 * 1024 * 1024


def dft_pair(extent):
    counter = np.arange(extent)
    angle = -2.0 * math.pi / extent * (counter[:, None] * counter[None, :] % extent)
    scale = 1.0 / math.sqrt(extent)
    return (
        (np.cos(angle) * scale).astype(ml_dtypes.bfloat16),
        (np.sin(angle) * scale).astype(ml_dtypes.bfloat16),
    )


def left_form(re, im, xp):
    return xp.concatenate(
        [xp.concatenate([re, -im], axis=1), xp.concatenate([im, re], axis=1)], axis=0
    )


def right_form(re, im, xp):
    return xp.concatenate(
        [xp.concatenate([re, im], axis=1), xp.concatenate([-im, re], axis=1)], axis=0
    )


def dft_tables(extent):
    re, im = dft_pair(extent)
    h = extent // 2

    def tables(re, im, evens_first):
        by_row = [(re[b::2, :h], im[b::2, :h]) for b in range(2)]
        by_col = [(re[:h, b::2], im[:h, b::2]) for b in range(2)]
        lefts, rights = (by_row, by_col) if evens_first else (by_col, by_row)
        return np.stack(
            [left_form(*pair, np) for pair in lefts] + [right_form(*pair, np) for pair in rights]
        )

    return tables(re, im, True), tables(re, -im, False)


def mm(a, b):
    return jnp.dot(a, b, preferred_element_type=F32)


def beside(a, b):
    return jnp.concatenate([a, b], axis=1)


def above(a, b):
    return jnp.concatenate([a, b], axis=0)


def band_left(re, im):
    n = re.shape[0]
    h, a, b = n // 2, n // 2 - BAND, n // 2 + BAND
    diag = [left_form(re[r, r], im[r, r], jnp) for r in (slice(0, h), slice(h, n))]
    row = lax.broadcasted_iota(jnp.int32, (2 * BAND, 2 * BAND), 0) < BAND
    col = lax.broadcasted_iota(jnp.int32, (2 * BAND, 2 * BAND), 1) < BAND
    corners = [jnp.where(row == col, 0.0, part[a:b, a:b]) for part in (re, im)]
    return diag, left_form(*corners, jnp)


def sandwich(diag, corner, re, im, right):
    n = re.shape[0]
    h, a, b = n // 2, n // 2 - BAND, n // 2 + BAND
    re, im = re.astype(BF16), im.astype(BF16)
    top = mm(diag[0], above(re[:h], im[:h]))
    low = mm(diag[1], above(re[h:], im[h:]))
    mid = mm(corner[...], above(re[a:b], im[a:b]))
    re = [top[:a], top[a:h] + mid[:BAND], low[:BAND] + mid[BAND : 2 * BAND], low[BAND:h]]
    mid, top, low = mid[2 * BAND :], top[h:], low[h:]
    im = [top[:a], top[a:h] + mid[:BAND], low[:BAND] + mid[BAND:], low[BAND:]]
    re, im = jnp.concatenate(re, axis=0), jnp.concatenate(im, axis=0)
    both = mm(beside(re.astype(BF16), im.astype(BF16)), right[...])
    return both[:, :n], both[:, n:]


def dft_sandwich(tabs, re, im):
    h = re.shape[0] // 2
    even = mm(tabs[0], above(re[:h] + re[h:], im[:h] + im[h:]).astype(BF16))
    odd = mm(tabs[1], above(re[:h] - re[h:], im[:h] - im[h:]).astype(BF16))
    re, im = above(even[:h], odd[:h]), above(even[h:], odd[h:])
    e = mm(beside(re[:, :h] + re[:, h:], im[:, :h] + im[:, h:]).astype(BF16), tabs[2])
    o = mm(beside(re[:, :h] - re[:, h:], im[:, :h] - im[:, h:]).astype(BF16), tabs[3])
    return e, o


def conj_dft_sandwich(tabs, e, o):
    h = e.shape[0] // 2
    e, o = e.astype(BF16), o.astype(BF16)
    even = mm(tabs[0], above(beside(e[:h, :h], o[:h, :h]), beside(e[:h, h:], o[:h, h:])))
    odd = mm(tabs[1], above(beside(e[h:, :h], o[h:, :h]), beside(e[h:, h:], o[h:, h:])))
    re = above(even[:h] + odd[:h], even[:h] - odd[:h]).astype(BF16)
    im = above(even[h:] + odd[h:], even[h:] - odd[h:]).astype(BF16)
    e = mm(beside(re[:, :h], im[:, :h]), tabs[2])
    o = mm(beside(re[:, h:], im[:, h:]), tabs[3])
    return (
        beside(e[:, :h] + o[:, :h], e[:, :h] - o[:, :h]),
        beside(e[:, h:] + o[:, h:], e[:, h:] - o[:, h:]),
    )


def place_of(off_ref, slot, h):
    row = off_ref[slot, 0] + h
    col = off_ref[slot, 1] + h
    top = pl.multiple_of((row >> 3) * 8, 8)
    block = pl.multiple_of((col >> 7) * 128, 128)
    return top, block, row & 7, col & 127


def build_canvas(own, up, down, left, right, corner_l, corner_r, canvas):
    n = own.shape[-1]
    h = n // 2
    canvas[:, :, h : h + n, h : h + n] = own[...]
    canvas[:, :, 0:h, h : h + n] = up[...]
    canvas[:, :, h + n :, h : h + n] = down[...]
    canvas[:, :, h : h + n, 0:h] = left[...]
    canvas[:, :, h : h + n, h + n :] = right[...]
    canvas[:, :, 0:h, 0:h] = corner_l[0]
    canvas[:, :, h + n :, 0:h] = corner_l[1]
    canvas[:, :, 0:h, h + n :] = corner_r[0]
    canvas[:, :, h + n :, h + n :] = corner_r[1]


def extract(off_ref, slot, canvas, patch):
    n = patch.shape[-1]
    h = n // 2
    top, block, row_rest, col_rest = place_of(off_ref, slot, h)
    row_shift = jnp.where(row_rest == 0, 0, n + 8 - row_rest)
    col_shift = jnp.where(col_rest == 0, 0, n + h - col_rest)
    for part in range(2):
        for layer in range(2):
            window = canvas[part, layer, pl.ds(top, n + 8), pl.ds(block, n + h)]
            window = pltpu.roll(window, col_shift, 1)[:, :n]
            patch[part, layer] = pltpu.roll(window, row_shift, 0)[:n]


def lay(off_ref, grads, canvas):
    n = grads[0].shape[-1]
    h = n // 2
    canvas[...] = jnp.zeros_like(canvas)
    for slot, grad in enumerate(grads):
        top, block, row_rest, col_rest = place_of(off_ref, slot, h)
        for part in range(canvas.shape[0]):
            tall = above(grad[part], jnp.zeros((8, n), F32))
            tall = pltpu.roll(tall, row_rest, 0)
            wide = beside(tall, jnp.zeros((n + 8, h), F32))
            canvas[part, pl.ds(top, n + 8), pl.ds(block, n + h)] += pltpu.roll(wide, col_rest, 1)


def each_mode(modes, step):
    for m in range(modes):
        step(m)


def forward(probe, patch, diag, corner, right, tabs, wave, far, inten):
    n = inten.shape[0]
    h = n // 2
    inten[...] = jnp.zeros_like(inten)

    def step(m):
        p_re, p_im = probe[0, m], probe[1, m]
        o_re, o_im = patch[0, 0], patch[1, 0]
        w_re, w_im = sandwich(
            diag, corner, p_re * o_re - p_im * o_im, p_re * o_im + p_im * o_re, right
        )
        wave[m, 0] = w_re
        wave[m, 1] = w_im
        o_re, o_im = patch[0, 1], patch[1, 1]
        e, o = dft_sandwich(tabs, w_re * o_re - w_im * o_im, w_re * o_im + w_im * o_re)
        far[m, 0] = e
        far[m, 1] = o
        e, o = e * e, o * o
        inten[...] += beside(e[:, :h] + e[:, h:], o[:, :h] + o[:, h:])

    each_mode(probe.shape[1], step)


def forward_first_kernel(off, own, up, down, left, right, corner_l, corner_r, probe, diag,
                         corner, mat, tabs, canvas, patch, wave, far, inten):
    build_canvas(own, up, down, left, right, corner_l, corner_r, canvas)
    extract(off, 0, canvas, patch)
    forward(probe, patch, diag, corner, mat, tabs, wave, far, inten)


def forward_next_kernel(slot, off, canvas, probe, diag, corner, mat, tabs, patch, wave, far,
                        inten):
    extract(off, slot, canvas, patch)
    forward(probe, patch, diag, corner, mat, tabs, wave, far, inten)


def back_last(slot, counts, mine, other, measured, far, wave, patch, tabs, grad, bar, resid):
    n = mine.shape[0]
    h = n // 2
    live = jnp.where(slot < counts[0], 2.0, 0.0).astype(F32)
    r = (mine[...] + other[...] - measured[slot]) * live
    resid[0] = beside(r[:, :h], r[:, :h])
    resid[1] = beside(r[:, h:], r[:, h:])
    grad[...] = jnp.zeros_like(grad)

    def step(m):
        b_re, b_im = conj_dft_sandwich(tabs, resid[0] * far[m, 0], resid[1] * far[m, 1])
        w_re, w_im = wave[m, 0], wave[m, 1]
        grad[0] += w_re * b_re + w_im * b_im
        grad[1] += w_re * b_im - w_im * b_re
        o_re, o_im = patch[0, 1], patch[1, 1]
        bar[m, 0] = (o_re * b_re + o_im * b_im).astype(BF16)
        bar[m, 1] = (o_re * b_im - o_im * b_re).astype(BF16)

    each_mode(far.shape[0], step)


def back_last_place_kernel(slot, counts, off, before, mine, other, measured, far, wave, patch,
                           tabs, bar, out_l, out_c, out_r, resid, grad, canvas):
    back_last(slot, counts, mine, other, measured, far, wave, patch, tabs, grad, bar, resid)
    lay(off, (before, grad), canvas)
    n = grad.shape[-1]
    h = n // 2
    out_l[...] = canvas[:, :, 0:h]
    out_c[...] = canvas[:, :, h : h + n]
    out_r[...] = canvas[:, :, h + n :]


def back_first(bar, probe, patch, diag, corner, mat, grad, emit):
    grad[...] = jnp.zeros_like(grad)

    def step(m):
        b_re, b_im = sandwich(diag, corner, bar[m, 0], bar[m, 1], mat)
        p_re, p_im = probe[0, m], probe[1, m]
        grad[0] += p_re * b_re + p_im * b_im
        grad[1] += p_re * b_im - p_im * b_re
        o_re, o_im = patch[0, 0], patch[1, 0]
        emit(m, o_re * b_re + o_im * b_im, o_re * b_im - o_im * b_re)

    each_mode(probe.shape[1], step)


def back_first_kernel(bar, probe, patch, diag, corner, mat, grad, part):
    def emit(m, re, im):
        part[0, m] = re
        part[1, m] = im

    back_first(bar, probe, patch, diag, corner, mat, grad, emit)


def back_first_add_kernel(bar, probe, patch, diag, corner, mat, part, grad, total):
    def emit(m, re, im):
        total[0, 0, m] = part[0, m] + re
        total[0, 1, m] = part[1, m] + im

    back_first(bar, probe, patch, diag, corner, mat, grad, emit)


def place_sides_kernel(off, grad0, grad1, out_l, out_r, canvas):
    lay(off, (grad0, grad1), canvas)
    h = grad0.shape[-1] // 2
    out_l[...] = canvas[:, :, 0:h]
    out_r[...] = canvas[:, :, 3 * h :]


def place_center_kernel(off, grad0, grad1, out_c, canvas):
    lay(off, (grad0, grad1), canvas)
    h = grad0.shape[-1] // 2
    out_c[...] = canvas[:, :, h : 3 * h]


def fold_cols_kernel(center, from_left, from_right, top, mid, low):
    n = center.shape[-1]
    h = n // 2
    for out, rows in ((top, slice(0, h)), (mid, slice(h, h + n)), (low, slice(h + n, 2 * n))):
        out[:, :, :h] = center[:, rows, :h] + from_left[:, rows]
        out[:, :, h:] = center[:, rows, h:] + from_right[:, rows]


def fold_rows_kernel(mid, from_up, from_down, out):
    h = from_up.shape[1]
    out[:, :h] = mid[:, :h] + from_up[...]
    out[:, h:] = mid[:, h:] + from_down[...]


def finish_kernel(mine_first, other_first, mine_last, other_last, out):
    out[0, :, 0] = mine_first[...] + other_first[...]
    out[0, :, 1] = mine_last[...] + other_last[...]


def prepare_kernel(prop, probe, measured, order, order_t, dft_in, conj_in, diag, corner, right,
                   back_diag, back_corner, back_right, probe_out, meas_out, dft_out, conj_out):
    re, im = prop[0].astype(F32), prop[1].astype(F32)
    re_t, im_t = re.T, im.T
    for out, edge, pair in ((diag, corner, (re, im)), (back_diag, back_corner, (re_t, -im_t))):
        blocks, corners = band_left(*pair)
        out[0] = blocks[0].astype(BF16)
        out[1] = blocks[1].astype(BF16)
        edge[...] = corners.astype(BF16)
    right[...] = right_form(re_t, im_t, jnp).astype(BF16)
    back_right[...] = right_form(re, -im, jnp).astype(BF16)
    probe_out[...] = probe[...]
    dft_out[...] = dft_in[...]
    conj_out[...] = conj_in[...]
    exact = functools.partial(
        jnp.dot, precision=lax.Precision.HIGHEST, preferred_element_type=F32
    )
    for slot in range(measured.shape[0]):
        meas_out[slot] = exact(exact(order[...], measured[slot]), order_t[...])


def rows_by(value, step):
    count = lax.axis_size("tile")
    pairs = [(i, i + GY * step) for i in range(count) if 0 <= i + GY * step < count]
    return lax.ppermute(value, "tile", pairs)


def cols_by(value, step):
    count = lax.axis_size("tile")
    pairs = [(i, i + step) for i in range(count) if 0 <= i % GY + step < GY]
    return lax.ppermute(value, "tile", pairs)


def swap_mode(value):
    return lax.ppermute(value, "mode", [(0, 1), (1, 0)])


def call(kernel, name, outs, args, scratch=(), smem=1, after=()):
    vmem = pl.BlockSpec(memory_space=pltpu.VMEM)
    scalars = pl.BlockSpec(memory_space=pltpu.SMEM)
    n_args, n_after = len(args), len(after)

    def run(*refs):
        kernel(*refs[:n_args], *refs[n_args + n_after :])

    return pl.pallas_call(
        run,
        out_shape=tuple(jax.ShapeDtypeStruct(shape, dtype) for shape, dtype in outs),
        in_specs=[scalars] * smem
        + [vmem] * (n_args - smem)
        + [pl.BlockSpec(memory_space=pl.ANY)] * n_after,
        out_specs=tuple(vmem for _ in outs),
        scratch_shapes=[pltpu.VMEM(shape, F32) for shape in scratch],
        compiler_params=pltpu.CompilerParams(vmem_limit_bytes=VMEM_LIMIT),
        name=name,
    )(*args, *after)


def body(object_tiles, probe_modes, propagator, offsets, counts, measured):
    n = probe_modes.shape[-1]
    h = n // 2
    modes = probe_modes.shape[1]
    slots = measured.shape[1]
    own = object_tiles[0]
    off = offsets[0]

    down_strip = rows_by(own[:, :, :h, :], -1)
    up_strip = rows_by(own[:, :, h:, :], 1)
    left_strip = cols_by(own[:, :, :, h:], 1)
    right_strip = cols_by(own[:, :, :, :h], -1)
    corner_l = cols_by(jnp.stack([up_strip[..., h:], down_strip[..., h:]]), 1)
    corner_r = cols_by(jnp.stack([up_strip[..., :h], down_strip[..., :h]]), -1)

    dft, conj_dft = dft_tables(n)
    order = np.eye(n, dtype=np.float32)[np.r_[0:n:2, 1:n:2]]
    plane, pair, mat = ((n, n), F32), ((2, n, n), F32), ((2 * n, 2 * n), BF16)
    patch_out, field = ((2, 2, n, n), F32), ((modes, 2, n, n), F32)
    probes, tables = ((2, modes, n, n), F32), (dft.shape, BF16)
    band = (((2, n, n), BF16), ((4 * BAND, 4 * BAND), BF16), mat)
    *made, probe, measured, dft, conj_dft = call(
        prepare_kernel,
        "prepare",
        band + band + (probes, ((slots, n, n), F32), tables, tables),
        (propagator, probe_modes, measured[0], jnp.asarray(order), jnp.asarray(order.T.copy()),
         jnp.asarray(dft), jnp.asarray(conj_dft)),
        smem=0,
    )
    prop, back_prop = made[:3], made[3:]

    canvas, patch0, wave0, far0, inten0 = call(
        forward_first_kernel,
        "forward_0",
        (((2, 2, 2 * n, 2 * n), F32), patch_out, field, field, plane),
        (off, own, up_strip, down_strip, left_strip, right_strip, corner_l, corner_r,
         probe, *prop, dft),
    )
    other0 = swap_mode(inten0)
    patch1, wave1, far1, inten1 = call(
        functools.partial(forward_next_kernel, 1),
        "forward_1",
        (patch_out, field, field, plane),
        (off, canvas, probe, *prop, dft),
    )
    other1 = swap_mode(inten1)

    bar_out = ((modes, 2, n, n), BF16)
    strips = (((2, 2 * n, h), F32), ((2, 2 * n, n), F32), ((2, 2 * n, h), F32))
    wide = (2, 2 * n, 2 * n)
    grad_last0, bar0 = call(
        functools.partial(back_last, 0),
        "back_last_0",
        (pair, bar_out),
        (counts, inten0, other0, measured, far0, wave0, patch0, conj_dft),
        scratch=((2, n, n),),
    )
    grad_first0, part = call(
        back_first_kernel,
        "back_first_0",
        (pair, probes),
        (bar0, probe, patch0, *back_prop),
        smem=0,
    )
    bar1, out_l, out_c, out_r = call(
        functools.partial(back_last_place_kernel, 1),
        "back_last_1",
        (bar_out,) + strips,
        (counts, off, grad_last0, inten1, other1, measured, far1, wave1, patch1, conj_dft),
        scratch=((2, n, n), (2, n, n), wide),
        smem=2,
        after=(grad_first0,),
    )

    half = ((2, h, n), F32)

    def fold_cols(name, out_l, out_c, out_r, after):
        from_left = cols_by(out_r, 1)
        from_right = cols_by(out_l, -1)
        return call(fold_cols_kernel, name, (half, pair, half), (out_c, from_left, from_right),
                    smem=0, after=after)

    def fold_rows(name, top, mid, low, after):
        from_up = rows_by(low, 1)
        from_down = rows_by(top, -1)
        return call(fold_rows_kernel, name, (pair,), (mid, from_up, from_down), smem=0,
                    after=after)[0]

    grad_first1, probe_grad = call(
        back_first_add_kernel,
        "back_first_1",
        (pair, ((1, 2, modes, n, n), F32)),
        (bar1, probe, patch1, *back_prop, part),
        smem=0,
    )
    strips_last = fold_cols("cols_last", out_l, out_c, out_r, (grad_first1,))
    mine_last = fold_rows("rows_last", *strips_last, ())
    other_last = swap_mode(mine_last)
    out_l, out_r = call(
        place_sides_kernel,
        "place_sides",
        (strips[0], strips[2]),
        (off, grad_first0, grad_first1),
        scratch=(wide,),
        after=(strips_last[0],),
    )
    (out_c,) = call(
        place_center_kernel,
        "place_center",
        (strips[1],),
        (off, grad_first0, grad_first1),
        scratch=(wide,),
        after=(out_l,),
    )
    strips_first = fold_cols("cols_first", out_l, out_c, out_r, ())
    mine_first = fold_rows("rows_first", *strips_first, (other_last,))
    other_first = swap_mode(mine_first)
    (object_grad,) = call(
        finish_kernel,
        "finish",
        ((object_tiles.shape, F32),),
        (mine_first, other_first, mine_last, other_last),
        smem=0,
    )
    return (object_grad, probe_grad)


def solution(mesh):
    placed = (
        P("tile", None, None, None, None),
        P(None, "mode", None, None),
        P(),
        P("tile", None, None),
        P("tile"),
        P("tile", None, None, None),
    )
    return jax.shard_map(
        body,
        mesh=mesh,
        in_specs=placed,
        out_specs=(P("tile", None, None, None, None), P("tile", None, "mode", None, None)),
        check_vma=False,
    )
```

```python
import functools
import math

import jax
import jax.numpy as jnp
import ml_dtypes
import numpy as np
from jax import lax
from jax.experimental import pallas as pl
from jax.experimental.pallas import tpu as pltpu
from jax.sharding import PartitionSpec as P

GY = 8
BAND = 16
F32 = jnp.float32
BF16 = jnp.bfloat16
VMEM_LIMIT = 24 * 1024 * 1024


def dft_pair(extent):
    counter = np.arange(extent)
    angle = -2.0 * math.pi / extent * (counter[:, None] * counter[None, :] % extent)
    scale = 1.0 / math.sqrt(extent)
    return (
        (np.cos(angle) * scale).astype(ml_dtypes.bfloat16),
        (np.sin(angle) * scale).astype(ml_dtypes.bfloat16),
    )


def left_form(re, im, xp):
    return xp.concatenate(
        [xp.concatenate([re, -im], axis=1), xp.concatenate([im, re], axis=1)], axis=0
    )


def right_form(re, im, xp):
    return xp.concatenate(
        [xp.concatenate([re, im], axis=1), xp.concatenate([-im, re], axis=1)], axis=0
    )


def dft_tables(extent):
    re, im = dft_pair(extent)
    h = extent // 2

    def tables(re, im, evens_first):
        by_row = [(re[b::2, :h], im[b::2, :h]) for b in range(2)]
        by_col = [(re[:h, b::2], im[:h, b::2]) for b in range(2)]
        lefts, rights = (by_row, by_col) if evens_first else (by_col, by_row)
        return np.stack(
            [left_form(*pair, np) for pair in lefts] + [right_form(*pair, np) for pair in rights]
        )

    return tables(re, im, True), tables(re, -im, False)


def mm(a, b):
    return jnp.dot(a, b, preferred_element_type=F32)


def beside(a, b):
    return jnp.concatenate([a, b], axis=1)


def above(a, b):
    return jnp.concatenate([a, b], axis=0)


def band_left(re, im):
    n = re.shape[0]
    h, a, b = n // 2, n // 2 - BAND, n // 2 + BAND
    diag = [left_form(re[r, r], im[r, r], jnp) for r in (slice(0, h), slice(h, n))]
    row = lax.broadcasted_iota(jnp.int32, (2 * BAND, 2 * BAND), 0) < BAND
    col = lax.broadcasted_iota(jnp.int32, (2 * BAND, 2 * BAND), 1) < BAND
    corners = [jnp.where(row == col, 0.0, part[a:b, a:b]) for part in (re, im)]
    return diag, left_form(*corners, jnp)


def sandwich(diag, corner, re, im, right):
    n = re.shape[0]
    h, a, b = n // 2, n // 2 - BAND, n // 2 + BAND
    re, im = re.astype(BF16), im.astype(BF16)
    top = mm(diag[0], above(re[:h], im[:h]))
    low = mm(diag[1], above(re[h:], im[h:]))
    mid = mm(corner[...], above(re[a:b], im[a:b]))
    re = [top[:a], top[a:h] + mid[:BAND], low[:BAND] + mid[BAND : 2 * BAND], low[BAND:h]]
    mid, top, low = mid[2 * BAND :], top[h:], low[h:]
    im = [top[:a], top[a:h] + mid[:BAND], low[:BAND] + mid[BAND:], low[BAND:]]
    re, im = jnp.concatenate(re, axis=0), jnp.concatenate(im, axis=0)
    both = mm(beside(re.astype(BF16), im.astype(BF16)), right[...])
    return both[:, :n], both[:, n:]


def dft_sandwich(tabs, re, im):
    h = re.shape[0] // 2
    even = mm(tabs[0], above(re[:h] + re[h:], im[:h] + im[h:]).astype(BF16))
    odd = mm(tabs[1], above(re[:h] - re[h:], im[:h] - im[h:]).astype(BF16))
    re, im = above(even[:h], odd[:h]), above(even[h:], odd[h:])
    e = mm(beside(re[:, :h] + re[:, h:], im[:, :h] + im[:, h:]).astype(BF16), tabs[2])
    o = mm(beside(re[:, :h] - re[:, h:], im[:, :h] - im[:, h:]).astype(BF16), tabs[3])
    return e, o


def conj_dft_sandwich(tabs, e, o):
    h = e.shape[0] // 2
    e, o = e.astype(BF16), o.astype(BF16)
    even = mm(tabs[0], above(beside(e[:h, :h], o[:h, :h]), beside(e[:h, h:], o[:h, h:])))
    odd = mm(tabs[1], above(beside(e[h:, :h], o[h:, :h]), beside(e[h:, h:], o[h:, h:])))
    re = above(even[:h] + odd[:h], even[:h] - odd[:h]).astype(BF16)
    im = above(even[h:] + odd[h:], even[h:] - odd[h:]).astype(BF16)
    e = mm(beside(re[:, :h], im[:, :h]), tabs[2])
    o = mm(beside(re[:, h:], im[:, h:]), tabs[3])
    return (
        beside(e[:, :h] + o[:, :h], e[:, :h] - o[:, :h]),
        beside(e[:, h:] + o[:, h:], e[:, h:] - o[:, h:]),
    )


def place_of(off_ref, slot, h):
    row = off_ref[slot, 0] + h
    col = off_ref[slot, 1] + h
    top = pl.multiple_of((row >> 3) * 8, 8)
    block = pl.multiple_of((col >> 7) * 128, 128)
    return top, block, row & 7, col & 127


def ends(info, axis, before, after):
    odd = info[axis]
    first = jnp.where(odd == 1, before, after)
    second = jnp.where(odd == 1, after, before)
    return pl.multiple_of(first, 128), pl.multiple_of(second, 128), info[2 + axis] == 1


def kept(good, value):
    return jnp.where(good, value, 0.0)


def build_canvas(info, own, rows_a, rows_b, cols_a, cols_b, corners_a, corners_b, canvas):
    n = own.shape[-1]
    h = n // 2
    ra, rb, row_ok = ends(info, 0, 0, h + n)
    ca, cb, col_ok = ends(info, 1, 0, h + n)
    canvas[:, :, h : h + n, h : h + n] = own[...]
    canvas[:, :, pl.ds(ra, h), h : h + n] = rows_a[...]
    canvas[:, :, pl.ds(rb, h), h : h + n] = kept(row_ok, rows_b[...])
    canvas[:, :, h : h + n, pl.ds(ca, h)] = cols_a[...]
    canvas[:, :, h : h + n, pl.ds(cb, h)] = kept(col_ok, cols_b[...])
    canvas[:, :, pl.ds(ra, h), pl.ds(ca, h)] = corners_a[0]
    canvas[:, :, pl.ds(rb, h), pl.ds(ca, h)] = kept(row_ok, corners_a[1])
    canvas[:, :, pl.ds(ra, h), pl.ds(cb, h)] = kept(col_ok, corners_b[0])
    canvas[:, :, pl.ds(rb, h), pl.ds(cb, h)] = kept(row_ok & col_ok, corners_b[1])


def extract(off_ref, slot, canvas, patch):
    n = patch.shape[-1]
    h = n // 2
    top, block, row_rest, col_rest = place_of(off_ref, slot, h)
    row_shift = jnp.where(row_rest == 0, 0, n + 8 - row_rest)
    col_shift = jnp.where(col_rest == 0, 0, n + h - col_rest)
    for part in range(2):
        for layer in range(2):
            window = canvas[part, layer, pl.ds(top, n + 8), pl.ds(block, n + h)]
            window = pltpu.roll(window, col_shift, 1)[:, :n]
            patch[part, layer] = pltpu.roll(window, row_shift, 0)[:n]


def lay(off_ref, grads, canvas):
    n = grads[0].shape[-1]
    h = n // 2
    canvas[...] = jnp.zeros_like(canvas)
    for slot, grad in enumerate(grads):
        top, block, row_rest, col_rest = place_of(off_ref, slot, h)
        for part in range(canvas.shape[0]):
            tall = above(grad[part], jnp.zeros((8, n), F32))
            tall = pltpu.roll(tall, row_rest, 0)
            wide = beside(tall, jnp.zeros((n + 8, h), F32))
            canvas[part, pl.ds(top, n + 8), pl.ds(block, n + h)] += pltpu.roll(wide, col_rest, 1)


def each_mode(modes, step):
    for m in range(modes):
        step(m)


def forward(probe, patch, diag, corner, right, tabs, wave, far, inten):
    n = inten.shape[0]
    h = n // 2
    inten[...] = jnp.zeros_like(inten)

    def step(m):
        p_re, p_im = probe[0, m], probe[1, m]
        o_re, o_im = patch[0, 0], patch[1, 0]
        w_re, w_im = sandwich(
            diag, corner, p_re * o_re - p_im * o_im, p_re * o_im + p_im * o_re, right
        )
        wave[m, 0] = w_re
        wave[m, 1] = w_im
        o_re, o_im = patch[0, 1], patch[1, 1]
        e, o = dft_sandwich(tabs, w_re * o_re - w_im * o_im, w_re * o_im + w_im * o_re)
        far[m, 0] = e
        far[m, 1] = o
        e, o = e * e, o * o
        inten[...] += beside(e[:, :h] + e[:, h:], o[:, :h] + o[:, h:])

    each_mode(probe.shape[1], step)


def forward_first_kernel(off, info, own, rows_a, rows_b, cols_a, cols_b, corners_a, corners_b,
                         probe, diag, corner, mat, tabs, canvas, patch, wave, far, inten):
    build_canvas(info, own, rows_a, rows_b, cols_a, cols_b, corners_a, corners_b, canvas)
    extract(off, 0, canvas, patch)
    forward(probe, patch, diag, corner, mat, tabs, wave, far, inten)


def forward_next_kernel(slot, off, canvas, probe, diag, corner, mat, tabs, patch, wave, far,
                        inten):
    extract(off, slot, canvas, patch)
    forward(probe, patch, diag, corner, mat, tabs, wave, far, inten)


def back_last(slot, counts, mine, other, measured, far, wave, patch, tabs, grad, bar, resid):
    n = mine.shape[0]
    h = n // 2
    live = jnp.where(slot < counts[0], 2.0, 0.0).astype(F32)
    r = (mine[...] + other[...] - measured[slot]) * live
    resid[0] = beside(r[:, :h], r[:, :h])
    resid[1] = beside(r[:, h:], r[:, h:])
    grad[...] = jnp.zeros_like(grad)

    def step(m):
        b_re, b_im = conj_dft_sandwich(tabs, resid[0] * far[m, 0], resid[1] * far[m, 1])
        w_re, w_im = wave[m, 0], wave[m, 1]
        grad[0] += w_re * b_re + w_im * b_im
        grad[1] += w_re * b_im - w_im * b_re
        o_re, o_im = patch[0, 1], patch[1, 1]
        bar[m, 0] = (o_re * b_re + o_im * b_im).astype(BF16)
        bar[m, 1] = (o_re * b_im - o_im * b_re).astype(BF16)

    each_mode(far.shape[0], step)


def back_last_place_kernel(slot, counts, off, info, before, mine, other, measured, far, wave, patch,
                           tabs, bar, out_a, out_c, out_b, resid, grad, canvas):
    back_last(slot, counts, mine, other, measured, far, wave, patch, tabs, grad, bar, resid)
    lay(off, (before, grad), canvas)
    n = grad.shape[-1]
    h = n // 2
    sides(info, canvas, out_a, out_b)
    out_c[...] = canvas[:, :, h : h + n]


def back_first(bar, probe, patch, diag, corner, mat, grad, emit):
    grad[...] = jnp.zeros_like(grad)

    def step(m):
        b_re, b_im = sandwich(diag, corner, bar[m, 0], bar[m, 1], mat)
        p_re, p_im = probe[0, m], probe[1, m]
        grad[0] += p_re * b_re + p_im * b_im
        grad[1] += p_re * b_im - p_im * b_re
        o_re, o_im = patch[0, 0], patch[1, 0]
        emit(m, o_re * b_re + o_im * b_im, o_re * b_im - o_im * b_re)

    each_mode(probe.shape[1], step)


def back_first_kernel(bar, probe, patch, diag, corner, mat, grad, part):
    def emit(m, re, im):
        part[0, m] = re
        part[1, m] = im

    back_first(bar, probe, patch, diag, corner, mat, grad, emit)


def back_first_add_kernel(bar, probe, patch, diag, corner, mat, part, grad, total):
    def emit(m, re, im):
        total[0, 0, m] = part[0, m] + re
        total[0, 1, m] = part[1, m] + im

    back_first(bar, probe, patch, diag, corner, mat, grad, emit)


def sides(info, canvas, out_a, out_b):
    h = out_a.shape[-1]
    a, b, _ = ends(info, 1, 0, 3 * h)
    out_a[...] = canvas[:, :, pl.ds(a, h)]
    out_b[...] = canvas[:, :, pl.ds(b, h)]


def place_sides_kernel(off, info, grad0, grad1, out_a, out_b, canvas):
    lay(off, (grad0, grad1), canvas)
    sides(info, canvas, out_a, out_b)


def place_center_kernel(off, grad0, grad1, out_c, canvas):
    lay(off, (grad0, grad1), canvas)
    h = grad0.shape[-1] // 2
    out_c[...] = canvas[:, :, h : 3 * h]


def fold_cols_kernel(info, center, got_a, got_b, out_a, mid, out_b):
    n = center.shape[-1]
    h = n // 2
    ca, cb, col_ok = ends(info, 1, 0, h)
    ra, rb, _ = ends(info, 0, 0, h + n)
    for a, out in ((ra, out_a), (rb, out_b)):
        out[:, :, pl.ds(ca, h)] = center[:, pl.ds(a, h), pl.ds(ca, h)] + got_a[:, pl.ds(a, h)]
        out[:, :, pl.ds(cb, h)] = center[:, pl.ds(a, h), pl.ds(cb, h)] + kept(
            col_ok, got_b[:, pl.ds(a, h)]
        )
    mid[:, :, pl.ds(ca, h)] = center[:, h : h + n, pl.ds(ca, h)] + got_a[:, h : h + n]
    mid[:, :, pl.ds(cb, h)] = center[:, h : h + n, pl.ds(cb, h)] + kept(
        col_ok, got_b[:, h : h + n]
    )


def fold_rows_kernel(info, mid, got_a, got_b, out):
    h = got_a.shape[1]
    ra, rb, row_ok = ends(info, 0, 0, h)
    out[:, pl.ds(ra, h)] = mid[:, pl.ds(ra, h)] + got_a[...]
    out[:, pl.ds(rb, h)] = mid[:, pl.ds(rb, h)] + kept(row_ok, got_b[...])


def finish_kernel(mine_first, other_first, mine_last, other_last, out):
    out[0, :, 0] = mine_first[...] + other_first[...]
    out[0, :, 1] = mine_last[...] + other_last[...]


def prepare_kernel(prop, probe, measured, order, order_t, dft_in, conj_in, diag, corner, right,
                   back_diag, back_corner, back_right, probe_out, meas_out, dft_out, conj_out):
    re, im = prop[0].astype(F32), prop[1].astype(F32)
    re_t, im_t = re.T, im.T
    for out, edge, pair in ((diag, corner, (re, im)), (back_diag, back_corner, (re_t, -im_t))):
        blocks, corners = band_left(*pair)
        out[0] = blocks[0].astype(BF16)
        out[1] = blocks[1].astype(BF16)
        edge[...] = corners.astype(BF16)
    right[...] = right_form(re_t, im_t, jnp).astype(BF16)
    back_right[...] = right_form(re, -im, jnp).astype(BF16)
    probe_out[...] = probe[...]
    dft_out[...] = dft_in[...]
    conj_out[...] = conj_in[...]
    exact = functools.partial(
        jnp.dot, precision=lax.Precision.HIGHEST, preferred_element_type=F32
    )
    for slot in range(measured.shape[0]):
        meas_out[slot] = exact(exact(order[...], measured[slot]), order_t[...])


def swap(value, axis, second):
    count = lax.axis_size("tile")
    step, length = (GY, count // GY) if axis == 0 else (1, GY)
    pairs = []
    for i in range(count):
        at = i // step % length
        to = (at + (1 if (at % 2 == 1) == second else -1)) % length
        pairs.append((i, i + (to - at) * step))
    return lax.ppermute(value, "tile", pairs)


def swap_mode(value):
    return lax.ppermute(value, "mode", [(0, 1), (1, 0)])


def call(kernel, name, outs, args, scratch=(), smem=1, after=()):
    vmem = pl.BlockSpec(memory_space=pltpu.VMEM)
    scalars = pl.BlockSpec(memory_space=pltpu.SMEM)
    n_args, n_after = len(args), len(after)

    def run(*refs):
        kernel(*refs[:n_args], *refs[n_args + n_after :])

    return pl.pallas_call(
        run,
        out_shape=tuple(jax.ShapeDtypeStruct(shape, dtype) for shape, dtype in outs),
        in_specs=[scalars] * smem
        + [vmem] * (n_args - smem)
        + [pl.BlockSpec(memory_space=pl.ANY)] * n_after,
        out_specs=tuple(vmem for _ in outs),
        scratch_shapes=[pltpu.VMEM(shape, F32) for shape in scratch],
        compiler_params=pltpu.CompilerParams(vmem_limit_bytes=VMEM_LIMIT),
        name=name,
    )(*args, *after)


def body(object_tiles, probe_modes, propagator, offsets, counts, measured):
    n = probe_modes.shape[-1]
    h = n // 2
    modes = probe_modes.shape[1]
    slots = measured.shape[1]
    own = object_tiles[0]
    off = offsets[0]

    tile = lax.axis_index("tile")
    row, col = tile // GY, tile % GY
    n_rows = lax.axis_size("tile") // GY
    odd_row, odd_col = row % 2 == 1, col % 2 == 1
    info = jnp.stack(
        [odd_row, odd_col, (row > 0) & (row < n_rows - 1), (col > 0) & (col < GY - 1)]
    ).astype(jnp.int32)

    top, low = own[:, :, :h, :], own[:, :, h:, :]
    rows_a = swap(jnp.where(odd_row, top, low), 0, False)
    rows_b = swap(jnp.where(odd_row, low, top), 0, True)
    left, right = own[:, :, :, :h], own[:, :, :, h:]
    cols_a = swap(jnp.where(odd_col, left, right), 1, False)
    cols_b = swap(jnp.where(odd_col, right, left), 1, True)
    strips = jnp.stack([rows_a, rows_b])
    left, right = strips[..., :h], strips[..., h:]
    corners_a = swap(jnp.where(odd_col, left, right), 1, False)
    corners_b = swap(jnp.where(odd_col, right, left), 1, True)

    dft, conj_dft = dft_tables(n)
    order = np.eye(n, dtype=np.float32)[np.r_[0:n:2, 1:n:2]]
    plane, pair, mat = ((n, n), F32), ((2, n, n), F32), ((2 * n, 2 * n), BF16)
    patch_out, field = ((2, 2, n, n), F32), ((modes, 2, n, n), F32)
    probes, tables = ((2, modes, n, n), F32), (dft.shape, BF16)
    band = (((2, n, n), BF16), ((4 * BAND, 4 * BAND), BF16), mat)
    *made, probe, measured, dft, conj_dft = call(
        prepare_kernel,
        "prepare",
        band + band + (probes, ((slots, n, n), F32), tables, tables),
        (propagator, probe_modes, measured[0], jnp.asarray(order), jnp.asarray(order.T.copy()),
         jnp.asarray(dft), jnp.asarray(conj_dft)),
        smem=0,
    )
    prop, back_prop = made[:3], made[3:]

    canvas, patch0, wave0, far0, inten0 = call(
        forward_first_kernel,
        "forward_0",
        (((2, 2, 2 * n, 2 * n), F32), patch_out, field, field, plane),
        (off, info, own, rows_a, rows_b, cols_a, cols_b, corners_a, corners_b, probe, *prop, dft),
        smem=2,
    )
    other0 = swap_mode(inten0)
    patch1, wave1, far1, inten1 = call(
        functools.partial(forward_next_kernel, 1),
        "forward_1",
        (patch_out, field, field, plane),
        (off, canvas, probe, *prop, dft),
    )
    other1 = swap_mode(inten1)

    bar_out = ((modes, 2, n, n), BF16)
    strips = (((2, 2 * n, h), F32), ((2, 2 * n, n), F32), ((2, 2 * n, h), F32))
    wide = (2, 2 * n, 2 * n)
    grad_last0, bar0 = call(
        functools.partial(back_last, 0),
        "back_last_0",
        (pair, bar_out),
        (counts, inten0, other0, measured, far0, wave0, patch0, conj_dft),
        scratch=((2, n, n),),
    )
    grad_first0, part = call(
        back_first_kernel,
        "back_first_0",
        (pair, probes),
        (bar0, probe, patch0, *back_prop),
        smem=0,
    )
    bar1, out_a, out_c, out_b = call(
        functools.partial(back_last_place_kernel, 1),
        "back_last_1",
        (bar_out,) + strips,
        (counts, off, info, grad_last0, inten1, other1, measured, far1, wave1, patch1, conj_dft),
        scratch=((2, n, n), (2, n, n), wide),
        smem=3,
        after=(grad_first0,),
    )

    half = ((2, h, n), F32)

    def fold_cols(name, out_a, out_c, out_b, after):
        got_a, got_b = swap(out_a, 1, False), swap(out_b, 1, True)
        return call(fold_cols_kernel, name, (half, pair, half), (info, out_c, got_a, got_b),
                    after=after)

    def fold_rows(name, out_a, mid, out_b, after):
        got_a, got_b = swap(out_a, 0, False), swap(out_b, 0, True)
        return call(fold_rows_kernel, name, (pair,), (info, mid, got_a, got_b), after=after)[0]

    grad_first1, probe_grad = call(
        back_first_add_kernel,
        "back_first_1",
        (pair, ((1, 2, modes, n, n), F32)),
        (bar1, probe, patch1, *back_prop, part),
        smem=0,
    )
    strips_last = fold_cols("cols_last", out_a, out_c, out_b, (grad_first1,))
    mine_last = fold_rows("rows_last", *strips_last, ())
    other_last = swap_mode(mine_last)
    out_a, out_b = call(
        place_sides_kernel,
        "place_sides",
        (strips[0], strips[2]),
        (off, info, grad_first0, grad_first1),
        scratch=(wide,),
        smem=2,
        after=(strips_last[0],),
    )
    (out_c,) = call(
        place_center_kernel,
        "place_center",
        (strips[1],),
        (off, grad_first0, grad_first1),
        scratch=(wide,),
        after=(out_a,),
    )
    strips_first = fold_cols("cols_first", out_a, out_c, out_b, ())
    mine_first = fold_rows("rows_first", *strips_first, (other_last,))
    other_first = swap_mode(mine_first)
    (object_grad,) = call(
        finish_kernel,
        "finish",
        ((object_tiles.shape, F32),),
        (mine_first, other_first, mine_last, other_last),
        smem=0,
    )
    return (object_grad, probe_grad)


def solution(mesh):
    placed = (
        P("tile", None, None, None, None),
        P(None, "mode", None, None),
        P(),
        P("tile", None, None),
        P("tile"),
        P("tile", None, None, None),
    )
    return jax.shard_map(
        body,
        mesh=mesh,
        in_specs=placed,
        out_specs=(P("tile", None, None, None, None), P("tile", None, "mode", None, None)),
        check_vma=False,
    )
```

```python
import functools
import math

import jax
import jax.numpy as jnp
import ml_dtypes
import numpy as np
from jax import lax
from jax.experimental import pallas as pl
from jax.experimental.pallas import tpu as pltpu
from jax.sharding import PartitionSpec as P

GY = 8
BAND = 16
F32 = jnp.float32
BF16 = jnp.bfloat16
VMEM_LIMIT = 24 * 1024 * 1024


def dft_pair(extent):
    counter = np.arange(extent)
    angle = -2.0 * math.pi / extent * (counter[:, None] * counter[None, :] % extent)
    scale = 1.0 / math.sqrt(extent)
    return (
        (np.cos(angle) * scale).astype(ml_dtypes.bfloat16),
        (np.sin(angle) * scale).astype(ml_dtypes.bfloat16),
    )


def left_form(re, im, xp):
    return xp.concatenate(
        [xp.concatenate([re, -im], axis=1), xp.concatenate([im, re], axis=1)], axis=0
    )


def right_form(re, im, xp):
    return xp.concatenate(
        [xp.concatenate([re, im], axis=1), xp.concatenate([-im, re], axis=1)], axis=0
    )


def dft_tables(extent):
    re, im = dft_pair(extent)
    h = extent // 2

    def tables(re, im, evens_first):
        by_row = [(re[b::2, :h], im[b::2, :h]) for b in range(2)]
        by_col = [(re[:h, b::2], im[:h, b::2]) for b in range(2)]
        lefts, rights = (by_row, by_col) if evens_first else (by_col, by_row)
        return np.stack(
            [left_form(*pair, np) for pair in lefts] + [right_form(*pair, np) for pair in rights]
        )

    return tables(re, im, True), tables(re, -im, False)


def mm(a, b):
    return jnp.dot(a, b, preferred_element_type=F32)


def beside(a, b):
    return jnp.concatenate([a, b], axis=1)


def above(a, b):
    return jnp.concatenate([a, b], axis=0)


def band_left(re, im):
    n = re.shape[0]
    h, a, b = n // 2, n // 2 - BAND, n // 2 + BAND
    diag = [left_form(re[r, r], im[r, r], jnp) for r in (slice(0, h), slice(h, n))]
    row = lax.broadcasted_iota(jnp.int32, (2 * BAND, 2 * BAND), 0) < BAND
    col = lax.broadcasted_iota(jnp.int32, (2 * BAND, 2 * BAND), 1) < BAND
    corners = [jnp.where(row == col, 0.0, part[a:b, a:b]) for part in (re, im)]
    return diag, left_form(*corners, jnp)


def sandwich(diag, corner, re, im, right):
    n = re.shape[0]
    h, a, b = n // 2, n // 2 - BAND, n // 2 + BAND
    re, im = re.astype(BF16), im.astype(BF16)
    top = mm(diag[0], above(re[:h], im[:h]))
    low = mm(diag[1], above(re[h:], im[h:]))
    mid = mm(corner[...], above(re[a:b], im[a:b]))
    re = [top[:a], top[a:h] + mid[:BAND], low[:BAND] + mid[BAND : 2 * BAND], low[BAND:h]]
    mid, top, low = mid[2 * BAND :], top[h:], low[h:]
    im = [top[:a], top[a:h] + mid[:BAND], low[:BAND] + mid[BAND:], low[BAND:]]
    re, im = jnp.concatenate(re, axis=0), jnp.concatenate(im, axis=0)
    both = mm(beside(re.astype(BF16), im.astype(BF16)), right[...])
    return both[:, :n], both[:, n:]


def dft_sandwich(tabs, re, im):
    h = re.shape[0] // 2
    even = mm(tabs[0], above(re[:h] + re[h:], im[:h] + im[h:]).astype(BF16))
    odd = mm(tabs[1], above(re[:h] - re[h:], im[:h] - im[h:]).astype(BF16))
    re, im = above(even[:h], odd[:h]), above(even[h:], odd[h:])
    e = mm(beside(re[:, :h] + re[:, h:], im[:, :h] + im[:, h:]).astype(BF16), tabs[2])
    o = mm(beside(re[:, :h] - re[:, h:], im[:, :h] - im[:, h:]).astype(BF16), tabs[3])
    return e, o


def conj_dft_sandwich(tabs, e, o):
    h = e.shape[0] // 2
    e, o = e.astype(BF16), o.astype(BF16)
    even = mm(tabs[0], above(beside(e[:h, :h], o[:h, :h]), beside(e[:h, h:], o[:h, h:])))
    odd = mm(tabs[1], above(beside(e[h:, :h], o[h:, :h]), beside(e[h:, h:], o[h:, h:])))
    re = above(even[:h] + odd[:h], even[:h] - odd[:h]).astype(BF16)
    im = above(even[h:] + odd[h:], even[h:] - odd[h:]).astype(BF16)
    e = mm(beside(re[:, :h], im[:, :h]), tabs[2])
    o = mm(beside(re[:, h:], im[:, h:]), tabs[3])
    return (
        beside(e[:, :h] + o[:, :h], e[:, :h] - o[:, :h]),
        beside(e[:, h:] + o[:, h:], e[:, h:] - o[:, h:]),
    )


def place_of(off_ref, slot, h):
    row = off_ref[slot, 0] + h
    col = off_ref[slot, 1] + h
    top = pl.multiple_of((row >> 3) * 8, 8)
    block = pl.multiple_of((col >> 7) * 128, 128)
    return top, block, row & 7, col & 127


def ends(info, axis, before, after):
    odd = info[axis]
    first = jnp.where(odd == 1, before, after)
    second = jnp.where(odd == 1, after, before)
    return pl.multiple_of(first, 128), pl.multiple_of(second, 128), info[2 + axis] == 1


def kept(good, value):
    return jnp.where(good, value, 0.0)


def build_canvas(info, own, rows_a, rows_b, cols_a, cols_b, corners_a, corners_b, canvas):
    n = own.shape[-1]
    h = n // 2
    ra, rb, row_ok = ends(info, 0, 0, h + n)
    ca, cb, col_ok = ends(info, 1, 0, h + n)
    canvas[:, :, h : h + n, h : h + n] = own[...]
    canvas[:, :, pl.ds(ra, h), h : h + n] = rows_a[...]
    canvas[:, :, pl.ds(rb, h), h : h + n] = kept(row_ok, rows_b[...])
    canvas[:, :, h : h + n, pl.ds(ca, h)] = cols_a[...]
    canvas[:, :, h : h + n, pl.ds(cb, h)] = kept(col_ok, cols_b[...])
    canvas[:, :, pl.ds(ra, h), pl.ds(ca, h)] = corners_a[0]
    canvas[:, :, pl.ds(rb, h), pl.ds(ca, h)] = kept(row_ok, corners_a[1])
    canvas[:, :, pl.ds(ra, h), pl.ds(cb, h)] = kept(col_ok, corners_b[0])
    canvas[:, :, pl.ds(rb, h), pl.ds(cb, h)] = kept(row_ok & col_ok, corners_b[1])


def extract(off_ref, slot, canvas, patch):
    n = patch.shape[-1]
    h = n // 2
    top, block, row_rest, col_rest = place_of(off_ref, slot, h)
    row_shift = jnp.where(row_rest == 0, 0, n + 8 - row_rest)
    col_shift = jnp.where(col_rest == 0, 0, n + h - col_rest)
    for part in range(2):
        for layer in range(2):
            window = canvas[part, layer, pl.ds(top, n + 8), pl.ds(block, n + h)]
            window = pltpu.roll(window, col_shift, 1)[:, :n]
            patch[part, layer] = pltpu.roll(window, row_shift, 0)[:n]


def lay(off_ref, grads, canvas):
    n = grads[0].shape[-1]
    h = n // 2
    canvas[...] = jnp.zeros_like(canvas)
    for slot, grad in enumerate(grads):
        top, block, row_rest, col_rest = place_of(off_ref, slot, h)
        for part in range(canvas.shape[0]):
            tall = above(grad[part], jnp.zeros((8, n), F32))
            tall = pltpu.roll(tall, row_rest, 0)
            wide = beside(tall, jnp.zeros((n + 8, h), F32))
            canvas[part, pl.ds(top, n + 8), pl.ds(block, n + h)] += pltpu.roll(wide, col_rest, 1)


def each_mode(modes, step):
    for m in range(modes):
        step(m)


def forward(probe, patch, diag, corner, right, tabs, wave, far, inten):
    n = inten.shape[0]
    h = n // 2
    inten[...] = jnp.zeros_like(inten)

    def step(m):
        p_re, p_im = probe[0, m], probe[1, m]
        o_re, o_im = patch[0, 0], patch[1, 0]
        w_re, w_im = sandwich(
            diag, corner, p_re * o_re - p_im * o_im, p_re * o_im + p_im * o_re, right
        )
        wave[m, 0] = w_re
        wave[m, 1] = w_im
        o_re, o_im = patch[0, 1], patch[1, 1]
        e, o = dft_sandwich(tabs, w_re * o_re - w_im * o_im, w_re * o_im + w_im * o_re)
        far[m, 0] = e
        far[m, 1] = o
        e, o = e * e, o * o
        inten[...] += beside(e[:, :h] + e[:, h:], o[:, :h] + o[:, h:])

    each_mode(probe.shape[1], step)


def forward_first_kernel(off, info, own, rows_a, rows_b, cols_a, cols_b, corners_a, corners_b,
                         probe, diag, corner, mat, tabs, canvas, patch, wave, far, inten):
    build_canvas(info, own, rows_a, rows_b, cols_a, cols_b, corners_a, corners_b, canvas)
    extract(off, 0, canvas, patch)
    forward(probe, patch, diag, corner, mat, tabs, wave, far, inten)


def forward_next_kernel(slot, off, canvas, probe, diag, corner, mat, tabs, patch, wave, far,
                        inten):
    extract(off, slot, canvas, patch)
    forward(probe, patch, diag, corner, mat, tabs, wave, far, inten)


def back_last(slot, counts, mine, other, measured, far, wave, patch, tabs, grad, bar, resid):
    n = mine.shape[0]
    h = n // 2
    live = jnp.where(slot < counts[0], 2.0, 0.0).astype(F32)
    r = (mine[...] + other[...] - measured[slot]) * live
    resid[0] = beside(r[:, :h], r[:, :h])
    resid[1] = beside(r[:, h:], r[:, h:])
    grad[...] = jnp.zeros_like(grad)

    def step(m):
        b_re, b_im = conj_dft_sandwich(tabs, resid[0] * far[m, 0], resid[1] * far[m, 1])
        w_re, w_im = wave[m, 0], wave[m, 1]
        grad[0] += w_re * b_re + w_im * b_im
        grad[1] += w_re * b_im - w_im * b_re
        o_re, o_im = patch[0, 1], patch[1, 1]
        bar[m, 0] = (o_re * b_re + o_im * b_im).astype(BF16)
        bar[m, 1] = (o_re * b_im - o_im * b_re).astype(BF16)

    each_mode(far.shape[0], step)


def back_last_place_kernel(slot, counts, off, info, before, mine, other, measured, far, wave, patch,
                           tabs, bar, out_a, out_c, out_b, resid, grad, canvas):
    back_last(slot, counts, mine, other, measured, far, wave, patch, tabs, grad, bar, resid)
    lay(off, (before, grad), canvas)
    n = grad.shape[-1]
    h = n // 2
    sides(info, canvas, out_a, out_b)
    out_c[...] = canvas[:, :, h : h + n]


def back_first(info, bar, probe, patch, diag, corner, mat, keep, send, grad, emit):
    grad[...] = jnp.zeros_like(grad)

    def step(m):
        b_re, b_im = sandwich(diag, corner, bar[m, 0], bar[m, 1], mat)
        p_re, p_im = probe[0, m], probe[1, m]
        grad[0] += p_re * b_re + p_im * b_im
        grad[1] += p_re * b_im - p_im * b_re
        o_re, o_im = patch[0, 0], patch[1, 0]
        emit(m, o_re * b_re + o_im * b_im, o_re * b_im - o_im * b_re)

    each_mode(probe.shape[1], step)
    part = info[4]
    keep[0] = grad[part]
    send[0] = grad[1 - part]


def back_first_kernel(info, bar, probe, patch, diag, corner, mat, keep, send, part, grad):
    def emit(m, re, im):
        part[0, m] = re
        part[1, m] = im

    back_first(info, bar, probe, patch, diag, corner, mat, keep, send, grad, emit)


def back_first_add_kernel(info, bar, probe, patch, diag, corner, mat, part, keep, send, total,
                          grad):
    def emit(m, re, im):
        total[0, 0, m] = part[0, m] + re
        total[0, 1, m] = part[1, m] + im

    back_first(info, bar, probe, patch, diag, corner, mat, keep, send, grad, emit)


def sides(info, canvas, out_a, out_b):
    h = out_a.shape[-1]
    a, b, _ = ends(info, 1, 0, 3 * h)
    out_a[...] = canvas[:, :, pl.ds(a, h)]
    out_b[...] = canvas[:, :, pl.ds(b, h)]


def lay_sums(off, parts, canvas, sums):
    for slot in range(2):
        sums[slot] = parts[2 * slot][...] + parts[2 * slot + 1][...]
    lay(off, (sums.at[0], sums.at[1]), canvas)


def place_sides_kernel(off, info, keep0, got0, keep1, got1, out_a, out_b, canvas, sums):
    lay_sums(off, (keep0, got0, keep1, got1), canvas, sums)
    sides(info, canvas, out_a, out_b)


def place_center_kernel(off, keep0, got0, keep1, got1, out_c, canvas, sums):
    lay_sums(off, (keep0, got0, keep1, got1), canvas, sums)
    h = keep0.shape[-1] // 2
    out_c[...] = canvas[:, :, h : 3 * h]


def fold_cols_kernel(info, center, got_a, got_b, out_a, mid, out_b):
    n = center.shape[-1]
    h = n // 2
    ca, cb, col_ok = ends(info, 1, 0, h)
    ra, rb, _ = ends(info, 0, 0, h + n)
    for a, out in ((ra, out_a), (rb, out_b)):
        out[:, :, pl.ds(ca, h)] = center[:, pl.ds(a, h), pl.ds(ca, h)] + got_a[:, pl.ds(a, h)]
        out[:, :, pl.ds(cb, h)] = center[:, pl.ds(a, h), pl.ds(cb, h)] + kept(
            col_ok, got_b[:, pl.ds(a, h)]
        )
    mid[:, :, pl.ds(ca, h)] = center[:, h : h + n, pl.ds(ca, h)] + got_a[:, h : h + n]
    mid[:, :, pl.ds(cb, h)] = center[:, h : h + n, pl.ds(cb, h)] + kept(
        col_ok, got_b[:, h : h + n]
    )


def fold_rows_kernel(info, mid, got_a, got_b, *outs):
    h = got_a.shape[1]
    ra, rb, row_ok = ends(info, 0, 0, h)
    for plane, out in enumerate(outs):
        out[0, pl.ds(ra, h)] = mid[plane, pl.ds(ra, h)] + got_a[plane]
        out[0, pl.ds(rb, h)] = mid[plane, pl.ds(rb, h)] + kept(row_ok, got_b[plane])


def finish_kernel(info, mine_first, other_first, mine_re, other_re, mine_im, other_im, out):
    part = info[4]
    out[0, part, 0] = mine_first[0]
    out[0, 1 - part, 0] = other_first[0]
    out[0, 0, 1] = mine_re[0] + other_re[0]
    out[0, 1, 1] = mine_im[0] + other_im[0]


def pick_corners_kernel(info, rows_a, rows_b, out_a, out_b):
    h = out_a.shape[-1]
    a, b, _ = ends(info, 1, 0, h)
    for i, rows in enumerate((rows_a, rows_b)):
        out_a[i] = rows[:, :, :, pl.ds(a, h)]
        out_b[i] = rows[:, :, :, pl.ds(b, h)]


def prepare_kernel(prop_in, probe_in, meas_in, order_in, order_t_in, dft_in, conj_in, diag, corner,
                   right, back_diag, back_corner, back_right, probe_out, meas_out, dft_out,
                   conj_out, prop, meas, order, order_t, sems):
    moves = (
        (prop_in, prop), (meas_in, meas), (order_in, order), (order_t_in, order_t),
        (probe_in, probe_out), (dft_in, dft_out), (conj_in, conj_out),
    )
    copies = [pltpu.make_async_copy(a, b, sems.at[i]) for i, (a, b) in enumerate(moves)]
    for copy in copies:
        copy.start()
    copies[0].wait()
    re, im = prop[0].astype(F32), prop[1].astype(F32)
    re_t, im_t = re.T, im.T
    for out, edge, pair in ((diag, corner, (re, im)), (back_diag, back_corner, (re_t, -im_t))):
        blocks, corners = band_left(*pair)
        out[0] = blocks[0].astype(BF16)
        out[1] = blocks[1].astype(BF16)
        edge[...] = corners.astype(BF16)
    right[...] = right_form(re_t, im_t, jnp).astype(BF16)
    back_right[...] = right_form(re, -im, jnp).astype(BF16)
    for copy in copies[1:]:
        copy.wait()
    exact = functools.partial(
        jnp.dot, precision=lax.Precision.HIGHEST, preferred_element_type=F32
    )
    for slot in range(meas.shape[0]):
        meas_out[slot] = exact(exact(order[...], meas[slot]), order_t[...])


def swap(value, axis, second):
    count = lax.axis_size("tile")
    step, length = (GY, count // GY) if axis == 0 else (1, GY)
    pairs = []
    for i in range(count):
        at = i // step % length
        to = (at + (1 if (at % 2 == 1) == second else -1)) % length
        pairs.append((i, i + (to - at) * step))
    return lax.ppermute(value, "tile", pairs)


def swap_mode(value):
    return lax.ppermute(value, "mode", [(0, 1), (1, 0)])


def call(kernel, name, outs, args, scratch=(), smem=1, after=(), copies=0):
    vmem = pl.BlockSpec(memory_space=pltpu.VMEM)
    held = pl.BlockSpec(memory_space=pltpu.HBM) if copies else vmem
    scalars = pl.BlockSpec(memory_space=pltpu.SMEM)
    n_args, n_after = len(args), len(after)

    def run(*refs):
        kernel(*refs[:n_args], *refs[n_args + n_after :])

    return pl.pallas_call(
        run,
        out_shape=tuple(jax.ShapeDtypeStruct(shape, dtype) for shape, dtype in outs),
        in_specs=[scalars] * smem
        + [held] * (n_args - smem)
        + [pl.BlockSpec(memory_space=pl.ANY)] * n_after,
        out_specs=tuple(vmem for _ in outs),
        scratch_shapes=[pltpu.VMEM(shape, dtype) for shape, dtype in scratch]
        + [pltpu.SemaphoreType.DMA((copies,))] * (copies > 0),
        compiler_params=pltpu.CompilerParams(vmem_limit_bytes=VMEM_LIMIT),
        name=name,
    )(*args, *after)


def body(object_tiles, probe_modes, propagator, offsets, counts, measured):
    n = probe_modes.shape[-1]
    h = n // 2
    modes = probe_modes.shape[1]
    slots = measured.shape[1]
    own = object_tiles[0]
    off = offsets[0]

    tile = lax.axis_index("tile")
    row, col = tile // GY, tile % GY
    n_rows = lax.axis_size("tile") // GY
    odd_row, odd_col = row % 2 == 1, col % 2 == 1
    paired = [(row > 0) & (row < n_rows - 1), (col > 0) & (col < GY - 1)]
    info = jnp.stack([odd_row, odd_col, *paired, lax.axis_index("mode") == 1]).astype(jnp.int32)

    top, low = own[:, :, :h, :], own[:, :, h:, :]
    rows_a = swap(jnp.where(odd_row, top, low), 0, False)
    rows_b = swap(jnp.where(odd_row, low, top), 0, True)
    left, right = own[:, :, :, :h], own[:, :, :, h:]
    cols_a = swap(jnp.where(odd_col, left, right), 1, False)
    cols_b = swap(jnp.where(odd_col, right, left), 1, True)
    dft, conj_dft = dft_tables(n)
    order = np.eye(n, dtype=np.float32)[np.r_[0:n:2, 1:n:2]]
    plane, pair, mat = ((n, n), F32), ((2, n, n), F32), ((2 * n, 2 * n), BF16)
    patch_out, field = ((2, 2, n, n), F32), ((modes, 2, n, n), F32)
    probes, tables = ((2, modes, n, n), F32), (dft.shape, BF16)
    band = (((2, n, n), BF16), ((4 * BAND, 4 * BAND), BF16), mat)
    *made, probe, measured, dft, conj_dft = call(
        prepare_kernel,
        "prepare",
        band + band + (probes, ((slots, n, n), F32), tables, tables),
        (propagator, probe_modes, measured[0], jnp.asarray(order), jnp.asarray(order.T.copy()),
         jnp.asarray(dft), jnp.asarray(conj_dft)),
        scratch=(((2, n, n), BF16), ((slots, n, n), F32), plane, plane),
        smem=0,
        copies=7,
    )
    prop, back_prop = made[:3], made[3:]
    quarter = ((2, 2, 2, h, h), F32)
    corners_a, corners_b = call(
        pick_corners_kernel,
        "pick_corners",
        (quarter, quarter),
        (info, rows_a, rows_b),
        after=(probe,),
    )
    corners_a, corners_b = swap(corners_a, 1, False), swap(corners_b, 1, True)

    canvas, patch0, wave0, far0, inten0 = call(
        forward_first_kernel,
        "forward_0",
        (((2, 2, 2 * n, 2 * n), F32), patch_out, field, field, plane),
        (off, info, own, rows_a, rows_b, cols_a, cols_b, corners_a, corners_b, probe, *prop, dft),
        smem=2,
    )
    other0 = swap_mode(inten0)
    patch1, wave1, far1, inten1 = call(
        functools.partial(forward_next_kernel, 1),
        "forward_1",
        (patch_out, field, field, plane),
        (off, canvas, probe, *prop, dft),
    )
    other1 = swap_mode(inten1)

    bar_out = ((modes, 2, n, n), BF16)
    strips = (((2, 2 * n, h), F32), ((2, 2 * n, n), F32), ((2, 2 * n, h), F32))
    wide = ((2, 2 * n, 2 * n), F32)
    grad_last0, bar0 = call(
        functools.partial(back_last, 0),
        "back_last_0",
        (pair, bar_out),
        (counts, inten0, other0, measured, far0, wave0, patch0, conj_dft),
        scratch=(pair,),
    )
    one = ((1, n, n), F32)
    keep0, send0, part = call(
        back_first_kernel,
        "back_first_0",
        (one, one, probes),
        (info, bar0, probe, patch0, *back_prop),
        scratch=(pair,),
    )
    got0 = swap_mode(send0)
    bar1, out_a, out_c, out_b = call(
        functools.partial(back_last_place_kernel, 1),
        "back_last_1",
        (bar_out,) + strips,
        (counts, off, info, grad_last0, inten1, other1, measured, far1, wave1, patch1, conj_dft),
        scratch=(pair, pair, wide),
        smem=3,
        after=(keep0,),
    )

    def fold_cols(name, out_a, out_c, out_b, after):
        got_a, got_b = swap(out_a, 1, False), swap(out_b, 1, True)
        planes = out_c.shape[0]
        half, mid = ((planes, h, n), F32), ((planes, n, n), F32)
        return call(fold_cols_kernel, name, (half, mid, half), (info, out_c, got_a, got_b),
                    after=after)

    def fold_rows(name, out_a, mid, out_b, after):
        got_a, got_b = swap(out_a, 0, False), swap(out_b, 0, True)
        return call(fold_rows_kernel, name, (one,) * mid.shape[0], (info, mid, got_a, got_b),
                    after=after)

    keep1, send1, probe_grad = call(
        back_first_add_kernel,
        "back_first_1",
        (one, one, ((1, 2, modes, n, n), F32)),
        (info, bar1, probe, patch1, *back_prop, part),
        scratch=(pair,),
        after=(),
    )
    got1 = swap_mode(send1)
    strips_last = fold_cols("cols_last", out_a, out_c, out_b, (keep1,))
    mine_re, mine_im = fold_rows("rows_last", *strips_last, ())
    other_re, other_im = swap_mode(mine_re), swap_mode(mine_im)
    strips = [((1,) + shape[1:], dtype) for shape, dtype in strips]
    wide = ((1, 2 * n, 2 * n), F32)
    parts = (keep0, got0, keep1, got1)
    out_a, out_b = call(
        place_sides_kernel,
        "place_sides",
        (strips[0], strips[2]),
        (off, info, *parts),
        scratch=(wide, ((2, 1, n, n), F32)),
        smem=2,
        after=(strips_last[0],),
    )
    (out_c,) = call(
        place_center_kernel,
        "place_center",
        (strips[1],),
        (off, *parts),
        scratch=(wide, ((2, 1, n, n), F32)),
        after=(out_a,),
    )
    strips_first = fold_cols("cols_first", out_a, out_c, out_b, ())
    (mine_first,) = fold_rows("rows_first", *strips_first, (other_re,))
    other_first = swap_mode(mine_first)
    (object_grad,) = call(
        finish_kernel,
        "finish",
        ((object_tiles.shape, F32),),
        (info, mine_first, other_first, mine_re, other_re, mine_im, other_im),
    )
    return (object_grad, probe_grad)


def solution(mesh):
    placed = (
        P("tile", None, None, None, None),
        P(None, "mode", None, None),
        P(),
        P("tile", None, None),
        P("tile"),
        P("tile", None, None, None),
    )
    return jax.shard_map(
        body,
        mesh=mesh,
        in_specs=placed,
        out_specs=(P("tile", None, None, None, None), P("tile", None, "mode", None, None)),
        check_vma=False,
    )
```

```python
import functools
import math

import jax
import jax.numpy as jnp
import ml_dtypes
import numpy as np
from jax import lax
from jax.experimental import pallas as pl
from jax.experimental.pallas import tpu as pltpu
from jax.sharding import PartitionSpec as P

GY = 8
BAND = 16
F32 = jnp.float32
BF16 = jnp.bfloat16
VMEM_LIMIT = 24 * 1024 * 1024


def dft_pair(extent):
    counter = np.arange(extent)
    angle = -2.0 * math.pi / extent * (counter[:, None] * counter[None, :] % extent)
    scale = 1.0 / math.sqrt(extent)
    return (
        (np.cos(angle) * scale).astype(ml_dtypes.bfloat16),
        (np.sin(angle) * scale).astype(ml_dtypes.bfloat16),
    )


def left_form(re, im, xp):
    return xp.concatenate(
        [xp.concatenate([re, -im], axis=1), xp.concatenate([im, re], axis=1)], axis=0
    )


def right_form(re, im, xp):
    return xp.concatenate(
        [xp.concatenate([re, im], axis=1), xp.concatenate([-im, re], axis=1)], axis=0
    )


def dft_tables(extent):
    re, im = dft_pair(extent)
    lefts = [left_form(re[b::2, : extent // 2], im[b::2, : extent // 2], np) for b in range(2)]
    return np.stack(lefts + [left.T for left in lefts])


def mm(a, b):
    return jnp.dot(a, b, preferred_element_type=F32)


def beside(a, b):
    return jnp.concatenate([a, b], axis=1)


def above(a, b):
    return jnp.concatenate([a, b], axis=0)


def band_left(re, im):
    n = re.shape[0]
    h, a, b = n // 2, n // 2 - BAND, n // 2 + BAND
    diag = [left_form(re[r, r], im[r, r], jnp) for r in (slice(0, h), slice(h, n))]
    row = lax.broadcasted_iota(jnp.int32, (2 * BAND, 2 * BAND), 0) < BAND
    col = lax.broadcasted_iota(jnp.int32, (2 * BAND, 2 * BAND), 1) < BAND
    corners = [jnp.where(row == col, 0.0, part[a:b, a:b]) for part in (re, im)]
    return diag, left_form(*corners, jnp)


def sandwich(diag, corner, re, im, right):
    n = re.shape[0]
    h, a, b = n // 2, n // 2 - BAND, n // 2 + BAND
    re, im = re.astype(BF16), im.astype(BF16)
    top = mm(diag[0], above(re[:h], im[:h]))
    low = mm(diag[1], above(re[h:], im[h:]))
    mid = mm(corner[...], above(re[a:b], im[a:b]))
    re = [top[:a], top[a:h] + mid[:BAND], low[:BAND] + mid[BAND : 2 * BAND], low[BAND:h]]
    mid, top, low = mid[2 * BAND :], top[h:], low[h:]
    im = [top[:a], top[a:h] + mid[:BAND], low[:BAND] + mid[BAND:], low[BAND:]]
    re, im = jnp.concatenate(re, axis=0), jnp.concatenate(im, axis=0)
    both = mm(beside(re.astype(BF16), im.astype(BF16)), right[...])
    return both[:, :n], both[:, n:]


def dft_sandwich(tabs, re, im):
    h = re.shape[0] // 2
    even = mm(tabs[0], above(re[:h] + re[h:], im[:h] + im[h:]).astype(BF16))
    odd = mm(tabs[1], above(re[:h] - re[h:], im[:h] - im[h:]).astype(BF16))
    re, im = above(even[:h], odd[:h]), above(even[h:], odd[h:])
    e = mm(beside(re[:, :h] + re[:, h:], im[:, :h] + im[:, h:]).astype(BF16), tabs[2])
    o = mm(beside(re[:, :h] - re[:, h:], im[:, :h] - im[:, h:]).astype(BF16), tabs[3])
    return e, o


def conj_dft_sandwich(tabs, e, o):
    h = e.shape[0] // 2
    e, o = e.astype(BF16), o.astype(BF16)
    even = mm(tabs[2], above(beside(e[:h, :h], o[:h, :h]), beside(e[:h, h:], o[:h, h:])))
    odd = mm(tabs[3], above(beside(e[h:, :h], o[h:, :h]), beside(e[h:, h:], o[h:, h:])))
    re = above(even[:h] + odd[:h], even[:h] - odd[:h]).astype(BF16)
    im = above(even[h:] + odd[h:], even[h:] - odd[h:]).astype(BF16)
    e = mm(beside(re[:, :h], im[:, :h]), tabs[0])
    o = mm(beside(re[:, h:], im[:, h:]), tabs[1])
    return (
        beside(e[:, :h] + o[:, :h], e[:, :h] - o[:, :h]),
        beside(e[:, h:] + o[:, h:], e[:, h:] - o[:, h:]),
    )


def place_of(off_ref, slot, h):
    row = off_ref[slot, 0] + h
    col = off_ref[slot, 1] + h
    top = pl.multiple_of((row >> 3) * 8, 8)
    block = pl.multiple_of((col >> 7) * 128, 128)
    return top, block, row & 7, col & 127


def ends(info, axis, before, after):
    odd = info[axis]
    first = jnp.where(odd == 1, before, after)
    second = jnp.where(odd == 1, after, before)
    return pl.multiple_of(first, 128), pl.multiple_of(second, 128), info[2 + axis] == 1


def kept(good, value):
    return jnp.where(good, value, 0.0)


def build_canvas(layer, info, own, rows_a, rows_b, cols_a, cols_b, canvas):
    n = own.shape[-1]
    h = n // 2
    ra, rb, row_ok = ends(info, 0, 0, h + n)
    ca, cb, col_ok = ends(info, 1, 0, h + n)
    canvas[:, h : h + n, h : h + n] = own[:, layer]
    canvas[:, pl.ds(ra, h), h : h + n] = rows_a[...]
    canvas[:, pl.ds(rb, h), h : h + n] = kept(row_ok, rows_b[...])
    canvas[:, :, pl.ds(ca, h)] = cols_a[...]
    canvas[:, :, pl.ds(cb, h)] = kept(col_ok, cols_b[...])


def extract(off_ref, slot, canvas, patch):
    n = patch.shape[-1]
    h = n // 2
    top, block, row_rest, col_rest = place_of(off_ref, slot, h)
    row_shift = jnp.where(row_rest == 0, 0, n + 8 - row_rest)
    col_shift = jnp.where(col_rest == 0, 0, n + h - col_rest)
    for part in range(2):
        window = canvas[part, pl.ds(top, n + 8), pl.ds(block, n + h)]
        window = pltpu.roll(window, col_shift, 1)[:, :n]
        patch[part] = pltpu.roll(window, row_shift, 0)[:n]


def lay(off_ref, grads, canvas):
    n = grads[0].shape[-1]
    h = n // 2
    canvas[...] = jnp.zeros_like(canvas)
    for slot, grad in enumerate(grads):
        top, block, row_rest, col_rest = place_of(off_ref, slot, h)
        for part in range(canvas.shape[0]):
            tall = above(grad[part], jnp.zeros((8, n), F32))
            tall = pltpu.roll(tall, row_rest, 0)
            wide = beside(tall, jnp.zeros((n + 8, h), F32))
            canvas[part, pl.ds(top, n + 8), pl.ds(block, n + h)] += pltpu.roll(wide, col_rest, 1)


def each_mode(modes, step):
    for m in range(modes):
        step(m)


def times(a_re, a_im, b_re, b_im):
    return a_re * b_re - a_im * b_im, a_re * b_im + a_im * b_re


def waves(probe, patch, diag, corner, right, wave):
    def step(m):
        e_re, e_im = times(probe[0, m], probe[1, m], patch[0], patch[1])
        wave[m, 0], wave[m, 1] = sandwich(diag, corner, e_re, e_im, right)

    each_mode(probe.shape[1], step)


def fars(wave, patch, tabs, far, inten):
    h = inten.shape[0] // 2
    inten[...] = jnp.zeros_like(inten)

    def step(m):
        e, o = dft_sandwich(tabs, *times(wave[m, 0], wave[m, 1], patch[0], patch[1]))
        far[m, 0] = e
        far[m, 1] = o
        e, o = e * e, o * o
        inten[...] += beside(e[:, :h] + e[:, h:], o[:, :h] + o[:, h:])

    each_mode(wave.shape[0], step)


def waves_first_kernel(off, info, own, rows_a, rows_b, cols_a, cols_b, probe, diag, corner,
                       mat, canvas, patch, wave):
    build_canvas(0, info, own, rows_a, rows_b, cols_a, cols_b, canvas)
    extract(off, 0, canvas, patch)
    waves(probe, patch, diag, corner, mat, wave)


def waves_next_kernel(off, canvas, probe, diag, corner, mat, patch, wave):
    extract(off, 1, canvas, patch)
    waves(probe, patch, diag, corner, mat, wave)


def fars_first_kernel(off, info, own, rows_a, rows_b, cols_a, cols_b, wave, tabs, canvas, patch,
                      far, inten):
    build_canvas(1, info, own, rows_a, rows_b, cols_a, cols_b, canvas)
    extract(off, 0, canvas, patch)
    fars(wave, patch, tabs, far, inten)


def fars_next_kernel(off, canvas, wave, tabs, patch, far, inten):
    extract(off, 1, canvas, patch)
    fars(wave, patch, tabs, far, inten)


def back_last(slot, counts, mine, other, measured, far, wave, patch, tabs, grad, bar, resid):
    n = mine.shape[0]
    h = n // 2
    live = jnp.where(slot < counts[0], 2.0, 0.0).astype(F32)
    r = (mine[...] + other[...] - measured[slot]) * live
    resid[0] = beside(r[:, :h], r[:, :h])
    resid[1] = beside(r[:, h:], r[:, h:])
    grad[...] = jnp.zeros_like(grad)

    def step(m):
        b_re, b_im = conj_dft_sandwich(tabs, resid[0] * far[m, 0], resid[1] * far[m, 1])
        w_re, w_im = wave[m, 0], wave[m, 1]
        grad[0] += w_re * b_re + w_im * b_im
        grad[1] += w_re * b_im - w_im * b_re
        o_re, o_im = patch[0], patch[1]
        bar[m, 0] = (o_re * b_re + o_im * b_im).astype(BF16)
        bar[m, 1] = (o_re * b_im - o_im * b_re).astype(BF16)

    each_mode(far.shape[0], step)


def back_last_place_kernel(slot, counts, off, info, before, mine, other, measured, far, wave, patch,
                           tabs, bar, out_a, out_c, out_b, resid, grad, canvas):
    back_last(slot, counts, mine, other, measured, far, wave, patch, tabs, grad, bar, resid)
    lay(off, (before, grad), canvas)
    n = grad.shape[-1]
    h = n // 2
    sides(info, canvas, out_a, out_b)
    out_c[...] = canvas[:, :, h : h + n]


def back_first_kernel(info, bar, probe, patch, diag, corner, mat, keep, send, part, grad):
    grad[...] = jnp.zeros_like(grad)

    def step(m):
        b_re, b_im = sandwich(diag, corner, bar[m, 0], bar[m, 1], mat)
        p_re, p_im = probe[0, m], probe[1, m]
        grad[0] += p_re * b_re + p_im * b_im
        grad[1] += p_re * b_im - p_im * b_re
        o_re, o_im = patch[0], patch[1]
        part[0, m] = o_re * b_re + o_im * b_im
        part[1, m] = o_re * b_im - o_im * b_re

    each_mode(probe.shape[1], step)
    mode = info[4]
    keep[0] = grad[mode]
    send[0] = grad[1 - mode]


def probe_sum_kernel(part0, part1, total):
    total[0] = part0[...] + part1[...]


def sides(info, canvas, out_a, out_b):
    h = out_a.shape[-1]
    a, b, _ = ends(info, 1, 0, 3 * h)
    out_a[...] = canvas[:, :, pl.ds(a, h)]
    out_b[...] = canvas[:, :, pl.ds(b, h)]


def lay_sums(off, parts, canvas, sums):
    for slot in range(2):
        sums[slot] = parts[2 * slot][...] + parts[2 * slot + 1][...]
    lay(off, (sums.at[0], sums.at[1]), canvas)


def place_sides_kernel(off, info, keep0, got0, keep1, got1, out_a, out_b, canvas, sums):
    lay_sums(off, (keep0, got0, keep1, got1), canvas, sums)
    sides(info, canvas, out_a, out_b)


def place_center_kernel(off, keep0, got0, keep1, got1, out_c, canvas, sums):
    lay_sums(off, (keep0, got0, keep1, got1), canvas, sums)
    h = keep0.shape[-1] // 2
    out_c[...] = canvas[:, :, h : 3 * h]


def fold_cols_kernel(info, center, got_a, got_b, out_a, mid, out_b):
    n = center.shape[-1]
    h = n // 2
    ca, cb, col_ok = ends(info, 1, 0, h)
    ra, rb, _ = ends(info, 0, 0, h + n)
    for a, out in ((ra, out_a), (rb, out_b)):
        out[:, :, pl.ds(ca, h)] = center[:, pl.ds(a, h), pl.ds(ca, h)] + got_a[:, pl.ds(a, h)]
        out[:, :, pl.ds(cb, h)] = center[:, pl.ds(a, h), pl.ds(cb, h)] + kept(
            col_ok, got_b[:, pl.ds(a, h)]
        )
    mid[:, :, pl.ds(ca, h)] = center[:, h : h + n, pl.ds(ca, h)] + got_a[:, h : h + n]
    mid[:, :, pl.ds(cb, h)] = center[:, h : h + n, pl.ds(cb, h)] + kept(
        col_ok, got_b[:, h : h + n]
    )


def fold_rows_kernel(info, mid, got_a, got_b, *outs):
    h = got_a.shape[1]
    ra, rb, row_ok = ends(info, 0, 0, h)
    for plane, out in enumerate(outs):
        out[0, pl.ds(ra, h)] = mid[plane, pl.ds(ra, h)] + got_a[plane]
        out[0, pl.ds(rb, h)] = mid[plane, pl.ds(rb, h)] + kept(row_ok, got_b[plane])


def finish_kernel(info, mine_first, other_first, mine_re, other_re, mine_im, other_im, out):
    part = info[4]
    out[0, part, 0] = mine_first[0]
    out[0, 1 - part, 0] = other_first[0]
    out[0, 0, 1] = mine_re[0] + other_re[0]
    out[0, 1, 1] = mine_im[0] + other_im[0]


def pick_rows_kernel(info, own, *refs):
    *outs, sems = refs
    h = outs[0].shape[1]
    a, b, _ = ends(info, 0, 0, h)
    copies = []
    for layer in range(2):
        for i, start in enumerate((a, b)):
            k = 2 * layer + i
            copies.append(pltpu.make_async_copy(
                own.at[:, layer, pl.ds(start, h), :], outs[k], sems.at[k]))
    for copy in copies:
        copy.start()
    for copy in copies:
        copy.wait()


def pick_cols_kernel(layer, info, own, rows_a, rows_b, out_a, out_b):
    n = own.shape[-1]
    h = n // 2
    ra, rb, row_ok = ends(info, 0, 0, h + n)
    a, b, _ = ends(info, 1, 0, h)
    for start, out in ((a, out_a), (b, out_b)):
        side = pl.ds(start, h)
        out[:, h : h + n] = own[:, layer, :, side]
        out[:, pl.ds(ra, h)] = rows_a[:, :, side]
        out[:, pl.ds(rb, h)] = kept(row_ok, rows_b[:, :, side])


def prepare_kernel(prop_in, probe_in, diag, corner, right, back_diag, back_corner, back_right,
                   probe_out, prop, sems):
    copies = [
        pltpu.make_async_copy(prop_in, prop, sems.at[0]),
        pltpu.make_async_copy(probe_in, probe_out, sems.at[1]),
    ]
    for copy in copies:
        copy.start()
    copies[0].wait()
    re, im = prop[0].astype(F32), prop[1].astype(F32)
    re_t, im_t = re.T, im.T
    for out, edge, pair in ((diag, corner, (re, im)), (back_diag, back_corner, (re_t, -im_t))):
        blocks, corners = band_left(*pair)
        out[0] = blocks[0].astype(BF16)
        out[1] = blocks[1].astype(BF16)
        edge[...] = corners.astype(BF16)
    right[...] = right_form(re_t, im_t, jnp).astype(BF16)
    back_right[...] = right_form(re, -im, jnp).astype(BF16)
    copies[1].wait()


def reorder_kernel(measured, tabs, out, tabs_out):
    n = out.shape[-1]
    h = n // 2
    tabs_out[...] = tabs[...]
    exact = functools.partial(
        jnp.dot, precision=lax.Precision.HIGHEST, preferred_element_type=F32
    )

    def order(to, of):
        a = lax.broadcasted_iota(jnp.int32, (n, n), to)
        b = lax.broadcasted_iota(jnp.int32, (n, n), of)
        return jnp.where(jnp.where(a < h, 2 * a, 2 * a - n + 1) == b, 1.0, 0.0).astype(F32)

    for slot in range(out.shape[0]):
        out[slot] = exact(exact(order(0, 1), measured[slot]), order(1, 0))


def swap(value, axis, second):
    count = lax.axis_size("tile")
    step, length = (GY, count // GY) if axis == 0 else (1, GY)
    pairs = []
    for i in range(count):
        at = i // step % length
        to = (at + (1 if (at % 2 == 1) == second else -1)) % length
        pairs.append((i, i + (to - at) * step))
    return lax.ppermute(value, "tile", pairs)


def swap_mode(value):
    return lax.ppermute(value, "mode", [(0, 1), (1, 0)])


def call(kernel, name, outs, args, scratch=(), smem=1, after=(), copies=0):
    vmem = pl.BlockSpec(memory_space=pltpu.VMEM)
    held = pl.BlockSpec(memory_space=pltpu.HBM) if copies else vmem
    scalars = pl.BlockSpec(memory_space=pltpu.SMEM)
    n_args, n_after = len(args), len(after)

    def run(*refs):
        kernel(*refs[:n_args], *refs[n_args + n_after :])

    return pl.pallas_call(
        run,
        out_shape=tuple(jax.ShapeDtypeStruct(shape, dtype) for shape, dtype in outs),
        in_specs=[scalars] * smem
        + [held] * (n_args - smem)
        + [pl.BlockSpec(memory_space=pl.ANY)] * n_after,
        out_specs=tuple(vmem for _ in outs),
        scratch_shapes=[pltpu.VMEM(shape, dtype) for shape, dtype in scratch]
        + [pltpu.SemaphoreType.DMA((copies,))] * (copies > 0),
        compiler_params=pltpu.CompilerParams(vmem_limit_bytes=VMEM_LIMIT),
        name=name,
    )(*args, *after)


def body(object_tiles, probe_modes, propagator, offsets, counts, measured):
    n = probe_modes.shape[-1]
    h = n // 2
    modes = probe_modes.shape[1]
    slots = measured.shape[1]
    own = object_tiles[0]
    off = offsets[0]

    tile = lax.axis_index("tile")
    row, col = tile // GY, tile % GY
    n_rows = lax.axis_size("tile") // GY
    odd_row, odd_col = row % 2 == 1, col % 2 == 1
    paired = [(row > 0) & (row < n_rows - 1), (col > 0) & (col < GY - 1)]
    info = jnp.stack([odd_row, odd_col, *paired, lax.axis_index("mode") == 1]).astype(jnp.int32)

    one, pair, mat = ((1, n, n), F32), ((2, n, n), F32), ((2 * n, 2 * n), BF16)
    plane, field, probes = ((n, n), F32), ((modes, 2, n, n), F32), ((2, modes, n, n), F32)
    band = (((2, n, n), BF16), ((4 * BAND, 4 * BAND), BF16), mat)
    strip, tall = ((2, h, n), F32), ((2, 2 * n, h), F32)

    picked = call(pick_rows_kernel, "pick_rows", (strip,) * 4, (info, own), copies=4)
    rows = [[swap(picked[2 * i + k], 0, k == 1) for k in range(2)] for i in range(2)]
    *made, probe = call(
        prepare_kernel,
        "prepare",
        band + band + (probes,),
        (propagator, probe_modes),
        scratch=(((2, n, n), BF16),),
        smem=0,
        copies=2,
    )
    prop, back_prop = made[:3], made[3:]
    tabs = jnp.asarray(dft_tables(n))
    measured, tabs = call(
        reorder_kernel,
        "reorder",
        (((slots, n, n), F32), (tabs.shape, BF16)),
        (measured[0], tabs),
        smem=0,
    )

    def beside_tiles(layer, after):
        picked = call(functools.partial(pick_cols_kernel, layer), f"pick_cols_{layer}", (tall,) * 2,
                      (info, own, *rows[layer]), after=after)
        return (own, *rows[layer], *(swap(picked[k], 1, k == 1) for k in range(2)))

    first = beside_tiles(0, (probe,))
    last = beside_tiles(1, (measured,))
    canvas, patch_first0, wave0 = call(
        waves_first_kernel,
        "waves_0",
        (((2, 2 * n, 2 * n), F32), pair, field),
        (off, info, *first, probe, *prop),
        smem=2,
        after=(),
    )
    patch_first1, wave1 = call(
        waves_next_kernel, "waves_1", (pair, field), (off, canvas, probe, *prop), after=()
    )
    canvas, patch_last0, far0, inten0 = call(
        fars_first_kernel,
        "fars_0",
        (((2, 2 * n, 2 * n), F32), pair, field, plane),
        (off, info, *last, wave0, tabs),
        smem=2,
        after=(patch_first1,),
    )
    other0 = swap_mode(inten0)
    patch_last1, far1, inten1 = call(
        fars_next_kernel, "fars_1", (pair, field, plane), (off, canvas, wave1, tabs)
    )
    other1 = swap_mode(inten1)

    bar_out = ((modes, 2, n, n), BF16)
    strips = (((2, 2 * n, h), F32), ((2, 2 * n, n), F32), ((2, 2 * n, h), F32))
    wide = ((2, 2 * n, 2 * n), F32)
    grad_last0, bar0 = call(
        functools.partial(back_last, 0),
        "back_last_0",
        (pair, bar_out),
        (counts, inten0, other0, measured, far0, wave0, patch_last0, tabs),
        scratch=(pair,),
    )
    keep0, send0, part0 = call(
        back_first_kernel,
        "back_first_0",
        (one, one, probes),
        (info, bar0, probe, patch_first0, *back_prop),
        scratch=(pair,),
    )
    got0 = swap_mode(send0)
    bar1, out_a, out_c, out_b = call(
        functools.partial(back_last_place_kernel, 1),
        "back_last_1",
        (bar_out,) + strips,
        (counts, off, info, grad_last0, inten1, other1, measured, far1, wave1, patch_last1, tabs),
        scratch=(pair, pair, wide),
        smem=3,
        after=(keep0,),
    )

    def fold_cols(name, out_a, out_c, out_b, after):
        got_a, got_b = swap(out_a, 1, False), swap(out_b, 1, True)
        planes = out_c.shape[0]
        half, mid = ((planes, h, n), F32), ((planes, n, n), F32)
        return call(fold_cols_kernel, name, (half, mid, half), (info, out_c, got_a, got_b),
                    after=after)

    def fold_rows(name, out_a, mid, out_b, after):
        got_a, got_b = swap(out_a, 0, False), swap(out_b, 0, True)
        return call(fold_rows_kernel, name, (one,) * mid.shape[0], (info, mid, got_a, got_b),
                    after=after)

    keep1, send1, part1 = call(
        back_first_kernel,
        "back_first_1",
        (one, one, probes),
        (info, bar1, probe, patch_first1, *back_prop),
        scratch=(pair,),
    )
    got1 = swap_mode(send1)
    strips_last = fold_cols("cols_last", out_a, out_c, out_b, (keep1,))
    mine_re, mine_im = fold_rows("rows_last", *strips_last, ())
    other_re, other_im = swap_mode(mine_re), swap_mode(mine_im)
    strips = [((1,) + shape[1:], dtype) for shape, dtype in strips]
    wide = ((1, 2 * n, 2 * n), F32)
    parts = (keep0, got0, keep1, got1)
    out_a, out_b = call(
        place_sides_kernel,
        "place_sides",
        (strips[0], strips[2]),
        (off, info, *parts),
        scratch=(wide, ((2, 1, n, n), F32)),
        smem=2,
        after=(strips_last[0],),
    )
    (out_c,) = call(
        place_center_kernel,
        "place_center",
        (strips[1],),
        (off, *parts),
        scratch=(wide, ((2, 1, n, n), F32)),
        after=(out_a,),
    )
    strips_first = fold_cols("cols_first", out_a, out_c, out_b, ())
    (mine_first,) = fold_rows("rows_first", *strips_first, (other_re,))
    other_first = swap_mode(mine_first)
    (probe_grad,) = call(
        probe_sum_kernel,
        "probe_sum",
        (((1, 2, modes, n, n), F32),),
        (part0, part1),
        smem=0,
        after=(),
    )
    (object_grad,) = call(
        finish_kernel,
        "finish",
        ((object_tiles.shape, F32),),
        (info, mine_first, other_first, mine_re, other_re, mine_im, other_im),
    )
    return (object_grad, probe_grad)


def solution(mesh):
    placed = (
        P("tile", None, None, None, None),
        P(None, "mode", None, None),
        P(),
        P("tile", None, None),
        P("tile"),
        P("tile", None, None, None),
    )
    return jax.shard_map(
        body,
        mesh=mesh,
        in_specs=placed,
        out_specs=(P("tile", None, None, None, None), P("tile", None, "mode", None, None)),
        check_vma=False,
    )
```

```python
import functools
import math

import jax
import jax.numpy as jnp
import ml_dtypes
import numpy as np
from jax import lax
from jax.experimental import pallas as pl
from jax.experimental.pallas import tpu as pltpu
from jax.sharding import PartitionSpec as P

GY = 8
BAND = 16
F32 = jnp.float32
BF16 = jnp.bfloat16
VMEM_LIMIT = 24 * 1024 * 1024


def dft_pair(extent):
    counter = np.arange(extent)
    angle = -2.0 * math.pi / extent * (counter[:, None] * counter[None, :] % extent)
    scale = 1.0 / math.sqrt(extent)
    return (
        (np.cos(angle) * scale).astype(ml_dtypes.bfloat16),
        (np.sin(angle) * scale).astype(ml_dtypes.bfloat16),
    )


def left_form(re, im, xp):
    return xp.concatenate(
        [xp.concatenate([re, -im], axis=1), xp.concatenate([im, re], axis=1)], axis=0
    )


def right_form(re, im, xp):
    return xp.concatenate(
        [xp.concatenate([re, im], axis=1), xp.concatenate([-im, re], axis=1)], axis=0
    )


def dft_tables(extent):
    re, im = dft_pair(extent)
    lefts = [left_form(re[b::2, : extent // 2], im[b::2, : extent // 2], np) for b in range(2)]
    return np.stack(lefts + [left.T for left in lefts])


def mm(a, b):
    return jnp.dot(a, b, preferred_element_type=F32)


def beside(a, b):
    return jnp.concatenate([a, b], axis=1)


def above(a, b):
    return jnp.concatenate([a, b], axis=0)


def band_left(re, im):
    n = re.shape[0]
    h, a, b = n // 2, n // 2 - BAND, n // 2 + BAND
    diag = [left_form(re[r, r], im[r, r], jnp) for r in (slice(0, h), slice(h, n))]
    row = lax.broadcasted_iota(jnp.int32, (2 * BAND, 2 * BAND), 0) < BAND
    col = lax.broadcasted_iota(jnp.int32, (2 * BAND, 2 * BAND), 1) < BAND
    corners = [jnp.where(row == col, 0.0, part[a:b, a:b]) for part in (re, im)]
    return diag, left_form(*corners, jnp)


def prop_left(diag, corner, re, im):
    n = re.shape[0]
    h, a, b = n // 2, n // 2 - BAND, n // 2 + BAND
    re, im = re.astype(BF16), im.astype(BF16)
    top = mm(diag[0], above(re[:h], im[:h]))
    low = mm(diag[1], above(re[h:], im[h:]))
    mid = mm(corner[...], above(re[a:b], im[a:b]))
    re = [top[:a], top[a:h] + mid[:BAND], low[:BAND] + mid[BAND : 2 * BAND], low[BAND:h]]
    mid, top, low = mid[2 * BAND :], top[h:], low[h:]
    im = [top[:a], top[a:h] + mid[:BAND], low[:BAND] + mid[BAND:], low[BAND:]]
    re, im = jnp.concatenate(re, axis=0), jnp.concatenate(im, axis=0)
    return beside(re.astype(BF16), im.astype(BF16))


def dft_left(tabs, re, im):
    h = re.shape[0] // 2
    even = mm(tabs[0], above(re[:h] + re[h:], im[:h] + im[h:]).astype(BF16))
    odd = mm(tabs[1], above(re[:h] - re[h:], im[:h] - im[h:]).astype(BF16))
    re, im = above(even[:h], odd[:h]), above(even[h:], odd[h:])
    e = beside(re[:, :h] + re[:, h:], im[:, :h] + im[:, h:])
    o = beside(re[:, :h] - re[:, h:], im[:, :h] - im[:, h:])
    return beside(e.astype(BF16), o.astype(BF16))


def conj_dft_left(tabs, e, o):
    h = e.shape[0] // 2
    e, o = e.astype(BF16), o.astype(BF16)
    even = mm(tabs[2], above(beside(e[:h, :h], o[:h, :h]), beside(e[:h, h:], o[:h, h:])))
    odd = mm(tabs[3], above(beside(e[h:, :h], o[h:, :h]), beside(e[h:, h:], o[h:, h:])))
    re = above(even[:h] + odd[:h], even[:h] - odd[:h]).astype(BF16)
    im = above(even[h:] + odd[h:], even[h:] - odd[h:]).astype(BF16)
    return beside(beside(re[:, :h], im[:, :h]), beside(re[:, h:], im[:, h:]))


def place_of(off_ref, slot, h):
    row = off_ref[slot, 0] + h
    col = off_ref[slot, 1] + h
    top = pl.multiple_of((row >> 3) * 8, 8)
    block = pl.multiple_of((col >> 7) * 128, 128)
    return top, block, row & 7, col & 127


def ends(info, axis, before, after):
    odd = info[axis]
    first = jnp.where(odd == 1, before, after)
    second = jnp.where(odd == 1, after, before)
    return pl.multiple_of(first, 128), pl.multiple_of(second, 128), info[2 + axis] == 1


def kept(good, value):
    return jnp.where(good, value, 0.0)


def build_canvas(layer, info, own, rows_a, rows_b, cols_a, cols_b, canvas):
    n = own.shape[-1]
    h = n // 2
    ra, rb, row_ok = ends(info, 0, 0, h + n)
    ca, cb, col_ok = ends(info, 1, 0, h + n)
    canvas[:, h : h + n, h : h + n] = own[:, layer]
    canvas[:, pl.ds(ra, h), h : h + n] = rows_a[...]
    canvas[:, pl.ds(rb, h), h : h + n] = kept(row_ok, rows_b[...])
    canvas[:, :, pl.ds(ca, h)] = cols_a[...]
    canvas[:, :, pl.ds(cb, h)] = kept(col_ok, cols_b[...])


def extract(off_ref, slot, canvas, patch):
    n = patch.shape[-1]
    h = n // 2
    top, block, row_rest, col_rest = place_of(off_ref, slot, h)
    row_shift = jnp.where(row_rest == 0, 0, n + 8 - row_rest)
    col_shift = jnp.where(col_rest == 0, 0, n + h - col_rest)
    for part in range(2):
        window = canvas[part, pl.ds(top, n + 8), pl.ds(block, n + h)]
        window = pltpu.roll(window, col_shift, 1)[:, :n]
        patch[part] = pltpu.roll(window, row_shift, 0)[:n]


def lay(off_ref, grads, canvas):
    n = grads[0].shape[-1]
    h = n // 2
    canvas[...] = jnp.zeros_like(canvas)
    for slot, grad in enumerate(grads):
        top, block, row_rest, col_rest = place_of(off_ref, slot, h)
        for part in range(canvas.shape[0]):
            tall = above(grad[part], jnp.zeros((8, n), F32))
            tall = pltpu.roll(tall, row_rest, 0)
            wide = beside(tall, jnp.zeros((n + 8, h), F32))
            canvas[part, pl.ds(top, n + 8), pl.ds(block, n + h)] += pltpu.roll(wide, col_rest, 1)


def times(a_re, a_im, b_re, b_im):
    return a_re * b_re - a_im * b_im, a_re * b_im + a_im * b_re


def by_mode(held, modes, left):
    n = held.shape[0] // modes
    rows = [slice(m * n, (m + 1) * n) for m in range(modes)]
    for m in range(modes):
        held[rows[m]] = left(m)
    return rows


def waves(probe, patch, diag, corner, right, wave, held):
    n = patch.shape[-1]

    def left(m):
        return prop_left(diag, corner, *times(probe[0, m], probe[1, m], patch[0], patch[1]))

    rows = by_mode(held, probe.shape[1], left)
    both = mm(held[...], right[...])
    for m, at in enumerate(rows):
        wave[m, 0] = both[at, :n]
        wave[m, 1] = both[at, n:]


def fars(wave, patch, tabs, far, inten, held):
    n = patch.shape[-1]
    h = n // 2

    def left(m):
        return dft_left(tabs, *times(wave[m, 0], wave[m, 1], patch[0], patch[1]))

    rows = by_mode(held, wave.shape[0], left)
    evens, odds = mm(held[:, :n], tabs[2]), mm(held[:, n:], tabs[3])
    total_e = total_o = 0.0
    for m, at in enumerate(rows):
        e, o = evens[at], odds[at]
        far[m, 0] = e
        far[m, 1] = o
        total_e += e * e
        total_o += o * o
    inten[...] = beside(total_e[:, :h] + total_e[:, h:], total_o[:, :h] + total_o[:, h:])


def waves_first_kernel(off, info, own, rows_a, rows_b, cols_a, cols_b, probe, diag, corner,
                       mat, canvas, patch, wave, held):
    build_canvas(0, info, own, rows_a, rows_b, cols_a, cols_b, canvas)
    extract(off, 0, canvas, patch)
    waves(probe, patch, diag, corner, mat, wave, held)


def waves_next_kernel(off, canvas, probe, diag, corner, mat, patch, wave, held):
    extract(off, 1, canvas, patch)
    waves(probe, patch, diag, corner, mat, wave, held)


def fars_first_kernel(off, info, own, rows_a, rows_b, cols_a, cols_b, wave, tabs, canvas, patch,
                      far, inten, held):
    build_canvas(1, info, own, rows_a, rows_b, cols_a, cols_b, canvas)
    extract(off, 0, canvas, patch)
    fars(wave, patch, tabs, far, inten, held)


def fars_next_kernel(off, canvas, wave, tabs, patch, far, inten, held):
    extract(off, 1, canvas, patch)
    fars(wave, patch, tabs, far, inten, held)


def back_last(slot, counts, mine, other, measured, far, wave, patch, tabs, grad, bar, resid, held):
    n = mine.shape[0]
    h = n // 2
    live = jnp.where(slot < counts[0], 2.0, 0.0).astype(F32)
    r = (mine[...] + other[...] - measured[slot]) * live
    resid[0] = beside(r[:, :h], r[:, :h])
    resid[1] = beside(r[:, h:], r[:, h:])
    rows = by_mode(
        held,
        far.shape[0],
        lambda m: conj_dft_left(tabs, resid[0] * far[m, 0], resid[1] * far[m, 1]),
    )
    evens, odds = mm(held[:, :n], tabs[0]), mm(held[:, n:], tabs[1])
    g_re = g_im = 0.0
    o_re, o_im = patch[0], patch[1]
    for m, at in enumerate(rows):
        e, o = evens[at], odds[at]
        b_re = beside(e[:, :h] + o[:, :h], e[:, :h] - o[:, :h])
        b_im = beside(e[:, h:] + o[:, h:], e[:, h:] - o[:, h:])
        w_re, w_im = wave[m, 0], wave[m, 1]
        g_re += w_re * b_re + w_im * b_im
        g_im += w_re * b_im - w_im * b_re
        bar[m, 0] = (o_re * b_re + o_im * b_im).astype(BF16)
        bar[m, 1] = (o_re * b_im - o_im * b_re).astype(BF16)
    grad[0] = g_re
    grad[1] = g_im


def back_last_place_kernel(slot, counts, off, info, before, mine, other, measured, far, wave, patch,
                           tabs, bar, out_a, out_c, out_b, resid, held, grad, canvas):
    back_last(
        slot, counts, mine, other, measured, far, wave, patch, tabs, grad, bar, resid, held
    )
    lay(off, (before, grad), canvas)
    n = grad.shape[-1]
    h = n // 2
    sides(info, canvas, out_a, out_b)
    out_c[...] = canvas[:, :, h : h + n]


def back_first_kernel(info, bar, probe, patch, diag, corner, mat, keep, send, part, grad, held):
    n = patch.shape[-1]
    rows = by_mode(
        held, probe.shape[1], lambda m: prop_left(diag, corner, bar[m, 0], bar[m, 1])
    )
    both = mm(held[...], mat[...])
    g_re = g_im = 0.0
    o_re, o_im = patch[0], patch[1]
    for m, at in enumerate(rows):
        b_re, b_im = both[at, :n], both[at, n:]
        p_re, p_im = probe[0, m], probe[1, m]
        g_re += p_re * b_re + p_im * b_im
        g_im += p_re * b_im - p_im * b_re
        part[0, m] = o_re * b_re + o_im * b_im
        part[1, m] = o_re * b_im - o_im * b_re
    grad[0] = g_re
    grad[1] = g_im
    mode = info[4]
    keep[0] = grad[mode]
    send[0] = grad[1 - mode]


def probe_sum_kernel(part0, part1, total):
    total[0] = part0[...] + part1[...]


def sides(info, canvas, out_a, out_b):
    h = out_a.shape[-1]
    a, b, _ = ends(info, 1, 0, 3 * h)
    out_a[...] = canvas[:, :, pl.ds(a, h)]
    out_b[...] = canvas[:, :, pl.ds(b, h)]


def lay_sums(off, parts, canvas, sums):
    for slot in range(2):
        sums[slot] = parts[2 * slot][...] + parts[2 * slot + 1][...]
    lay(off, (sums.at[0], sums.at[1]), canvas)


def place_sides_kernel(off, info, keep0, got0, keep1, got1, out_a, out_b, canvas, sums):
    lay_sums(off, (keep0, got0, keep1, got1), canvas, sums)
    sides(info, canvas, out_a, out_b)


def place_center_kernel(off, keep0, got0, keep1, got1, out_c, canvas, sums):
    lay_sums(off, (keep0, got0, keep1, got1), canvas, sums)
    h = keep0.shape[-1] // 2
    out_c[...] = canvas[:, :, h : 3 * h]


def fold_cols_kernel(info, center, got_a, got_b, out_a, mid, out_b):
    n = center.shape[-1]
    h = n // 2
    ca, cb, col_ok = ends(info, 1, 0, h)
    ra, rb, _ = ends(info, 0, 0, h + n)
    for a, out in ((ra, out_a), (rb, out_b)):
        out[:, :, pl.ds(ca, h)] = center[:, pl.ds(a, h), pl.ds(ca, h)] + got_a[:, pl.ds(a, h)]
        out[:, :, pl.ds(cb, h)] = center[:, pl.ds(a, h), pl.ds(cb, h)] + kept(
            col_ok, got_b[:, pl.ds(a, h)]
        )
    mid[:, :, pl.ds(ca, h)] = center[:, h : h + n, pl.ds(ca, h)] + got_a[:, h : h + n]
    mid[:, :, pl.ds(cb, h)] = center[:, h : h + n, pl.ds(cb, h)] + kept(
        col_ok, got_b[:, h : h + n]
    )


def fold_rows_kernel(info, mid, got_a, got_b, *outs):
    h = got_a.shape[1]
    ra, rb, row_ok = ends(info, 0, 0, h)
    for plane, out in enumerate(outs):
        out[0, pl.ds(ra, h)] = mid[plane, pl.ds(ra, h)] + got_a[plane]
        out[0, pl.ds(rb, h)] = mid[plane, pl.ds(rb, h)] + kept(row_ok, got_b[plane])


def finish_kernel(info, mine_first, other_first, mine_re, other_re, mine_im, other_im, out):
    part = info[4]
    out[0, part, 0] = mine_first[0]
    out[0, 1 - part, 0] = other_first[0]
    out[0, 0, 1] = mine_re[0] + other_re[0]
    out[0, 1, 1] = mine_im[0] + other_im[0]


def pick_rows_kernel(info, own, *refs):
    *outs, sems = refs
    h = outs[0].shape[1]
    a, b, _ = ends(info, 0, 0, h)
    copies = []
    for layer in range(2):
        for i, start in enumerate((a, b)):
            k = 2 * layer + i
            copies.append(pltpu.make_async_copy(
                own.at[:, layer, pl.ds(start, h), :], outs[k], sems.at[k]))
    for copy in copies:
        copy.start()
    for copy in copies:
        copy.wait()


def pick_cols_kernel(layer, info, own, rows_a, rows_b, out_a, out_b):
    n = own.shape[-1]
    h = n // 2
    ra, rb, row_ok = ends(info, 0, 0, h + n)
    a, b, _ = ends(info, 1, 0, h)
    for start, out in ((a, out_a), (b, out_b)):
        side = pl.ds(start, h)
        out[:, h : h + n] = own[:, layer, :, side]
        out[:, pl.ds(ra, h)] = rows_a[:, :, side]
        out[:, pl.ds(rb, h)] = kept(row_ok, rows_b[:, :, side])


def prepare_kernel(prop_in, probe_in, diag, corner, right, back_diag, back_corner, back_right,
                   probe_out, prop, sems):
    copies = [
        pltpu.make_async_copy(prop_in, prop, sems.at[0]),
        pltpu.make_async_copy(probe_in, probe_out, sems.at[1]),
    ]
    for copy in copies:
        copy.start()
    copies[0].wait()
    re, im = prop[0].astype(F32), prop[1].astype(F32)
    re_t, im_t = re.T, im.T
    for out, edge, pair in ((diag, corner, (re, im)), (back_diag, back_corner, (re_t, -im_t))):
        blocks, corners = band_left(*pair)
        out[0] = blocks[0].astype(BF16)
        out[1] = blocks[1].astype(BF16)
        edge[...] = corners.astype(BF16)
    right[...] = right_form(re_t, im_t, jnp).astype(BF16)
    back_right[...] = right_form(re, -im, jnp).astype(BF16)
    copies[1].wait()


def reorder_kernel(measured, tabs, out, tabs_out):
    n = out.shape[-1]
    h = n // 2
    tabs_out[...] = tabs[...]
    exact = functools.partial(
        jnp.dot, precision=lax.Precision.HIGHEST, preferred_element_type=F32
    )

    def order(to, of):
        a = lax.broadcasted_iota(jnp.int32, (n, n), to)
        b = lax.broadcasted_iota(jnp.int32, (n, n), of)
        return jnp.where(jnp.where(a < h, 2 * a, 2 * a - n + 1) == b, 1.0, 0.0).astype(F32)

    for slot in range(out.shape[0]):
        out[slot] = exact(exact(order(0, 1), measured[slot]), order(1, 0))


def swap(value, axis, second):
    count = lax.axis_size("tile")
    step, length = (GY, count // GY) if axis == 0 else (1, GY)
    pairs = []
    for i in range(count):
        at = i // step % length
        to = (at + (1 if (at % 2 == 1) == second else -1)) % length
        pairs.append((i, i + (to - at) * step))
    return lax.ppermute(value, "tile", pairs)


def swap_mode(value):
    return lax.ppermute(value, "mode", [(0, 1), (1, 0)])


def call(kernel, name, outs, args, scratch=(), smem=1, after=(), copies=0):
    vmem = pl.BlockSpec(memory_space=pltpu.VMEM)
    held = pl.BlockSpec(memory_space=pltpu.HBM) if copies else vmem
    scalars = pl.BlockSpec(memory_space=pltpu.SMEM)
    n_args, n_after = len(args), len(after)

    def run(*refs):
        kernel(*refs[:n_args], *refs[n_args + n_after :])

    return pl.pallas_call(
        run,
        out_shape=tuple(jax.ShapeDtypeStruct(shape, dtype) for shape, dtype in outs),
        in_specs=[scalars] * smem
        + [held] * (n_args - smem)
        + [pl.BlockSpec(memory_space=pl.ANY)] * n_after,
        out_specs=tuple(vmem for _ in outs),
        scratch_shapes=[pltpu.VMEM(shape, dtype) for shape, dtype in scratch]
        + [pltpu.SemaphoreType.DMA((copies,))] * (copies > 0),
        compiler_params=pltpu.CompilerParams(vmem_limit_bytes=VMEM_LIMIT),
        name=name,
    )(*args, *after)


def body(object_tiles, probe_modes, propagator, offsets, counts, measured):
    n = probe_modes.shape[-1]
    h = n // 2
    modes = probe_modes.shape[1]
    slots = measured.shape[1]
    own = object_tiles[0]
    off = offsets[0]

    tile = lax.axis_index("tile")
    row, col = tile // GY, tile % GY
    n_rows = lax.axis_size("tile") // GY
    odd_row, odd_col = row % 2 == 1, col % 2 == 1
    paired = [(row > 0) & (row < n_rows - 1), (col > 0) & (col < GY - 1)]
    info = jnp.stack([odd_row, odd_col, *paired, lax.axis_index("mode") == 1]).astype(jnp.int32)

    one, pair, mat = ((1, n, n), F32), ((2, n, n), F32), ((2 * n, 2 * n), BF16)
    plane, field, probes = ((n, n), F32), ((modes, 2, n, n), F32), ((2, modes, n, n), F32)
    band = (((2, n, n), BF16), ((4 * BAND, 4 * BAND), BF16), mat)
    held = ((modes * n, 2 * n), BF16)
    strip, tall = ((2, h, n), F32), ((2, 2 * n, h), F32)

    picked = call(pick_rows_kernel, "pick_rows", (strip,) * 4, (info, own), copies=4)
    rows = [[swap(picked[2 * i + k], 0, k == 1) for k in range(2)] for i in range(2)]
    *made, probe = call(
        prepare_kernel,
        "prepare",
        band + band + (probes,),
        (propagator, probe_modes),
        scratch=(((2, n, n), BF16),),
        smem=0,
        copies=2,
    )
    prop, back_prop = made[:3], made[3:]
    tabs = jnp.asarray(dft_tables(n))
    measured, tabs = call(
        reorder_kernel,
        "reorder",
        (((slots, n, n), F32), (tabs.shape, BF16)),
        (measured[0], tabs),
        smem=0,
    )

    def beside_tiles(layer, after):
        picked = call(functools.partial(pick_cols_kernel, layer), f"pick_cols_{layer}", (tall,) * 2,
                      (info, own, *rows[layer]), after=after)
        return (own, *rows[layer], *(swap(picked[k], 1, k == 1) for k in range(2)))

    first = beside_tiles(0, (probe,))
    last = beside_tiles(1, (measured,))
    canvas, patch_first0, wave0 = call(
        waves_first_kernel,
        "waves_0",
        (((2, 2 * n, 2 * n), F32), pair, field),
        (off, info, *first, probe, *prop),
        scratch=(held,),
        smem=2,
        after=(),
    )
    patch_first1, wave1 = call(
        waves_next_kernel, "waves_1", (pair, field), (off, canvas, probe, *prop), scratch=(held,),
        after=()
    )
    canvas, patch_last0, far0, inten0 = call(
        fars_first_kernel,
        "fars_0",
        (((2, 2 * n, 2 * n), F32), pair, field, plane),
        (off, info, *last, wave0, tabs),
        scratch=(held,),
        smem=2,
        after=(patch_first1,),
    )
    other0 = swap_mode(inten0)
    patch_last1, far1, inten1 = call(
        fars_next_kernel, "fars_1", (pair, field, plane), (off, canvas, wave1, tabs), scratch=(held,)
    )
    other1 = swap_mode(inten1)

    bar_out = ((modes, 2, n, n), BF16)
    strips = (((2, 2 * n, h), F32), ((2, 2 * n, n), F32), ((2, 2 * n, h), F32))
    wide = ((2, 2 * n, 2 * n), F32)
    grad_last0, bar0 = call(
        functools.partial(back_last, 0),
        "back_last_0",
        (pair, bar_out),
        (counts, inten0, other0, measured, far0, wave0, patch_last0, tabs),
        scratch=(pair, held),
    )
    keep0, send0, part0 = call(
        back_first_kernel,
        "back_first_0",
        (one, one, probes),
        (info, bar0, probe, patch_first0, *back_prop),
        scratch=(pair, held),
    )
    got0 = swap_mode(send0)
    bar1, out_a, out_c, out_b = call(
        functools.partial(back_last_place_kernel, 1),
        "back_last_1",
        (bar_out,) + strips,
        (counts, off, info, grad_last0, inten1, other1, measured, far1, wave1, patch_last1, tabs),
        scratch=(pair, held, pair, wide),
        smem=3,
        after=(keep0,),
    )

    def fold_cols(name, out_a, out_c, out_b, after):
        got_a, got_b = swap(out_a, 1, False), swap(out_b, 1, True)
        planes = out_c.shape[0]
        half, mid = ((planes, h, n), F32), ((planes, n, n), F32)
        return call(fold_cols_kernel, name, (half, mid, half), (info, out_c, got_a, got_b),
                    after=after)

    def fold_rows(name, out_a, mid, out_b, after):
        got_a, got_b = swap(out_a, 0, False), swap(out_b, 0, True)
        return call(fold_rows_kernel, name, (one,) * mid.shape[0], (info, mid, got_a, got_b),
                    after=after)

    keep1, send1, part1 = call(
        back_first_kernel,
        "back_first_1",
        (one, one, probes),
        (info, bar1, probe, patch_first1, *back_prop),
        scratch=(pair, held),
    )
    got1 = swap_mode(send1)
    strips_last = fold_cols("cols_last", out_a, out_c, out_b, (keep1,))
    mine_re, mine_im = fold_rows("rows_last", *strips_last, ())
    other_re, other_im = swap_mode(mine_re), swap_mode(mine_im)
    strips = [((1,) + shape[1:], dtype) for shape, dtype in strips]
    wide = ((1, 2 * n, 2 * n), F32)
    parts = (keep0, got0, keep1, got1)
    out_a, out_b = call(
        place_sides_kernel,
        "place_sides",
        (strips[0], strips[2]),
        (off, info, *parts),
        scratch=(wide, ((2, 1, n, n), F32)),
        smem=2,
        after=(strips_last[0],),
    )
    (out_c,) = call(
        place_center_kernel,
        "place_center",
        (strips[1],),
        (off, *parts),
        scratch=(wide, ((2, 1, n, n), F32)),
        after=(out_a,),
    )
    strips_first = fold_cols("cols_first", out_a, out_c, out_b, ())
    (mine_first,) = fold_rows("rows_first", *strips_first, (other_re,))
    other_first = swap_mode(mine_first)
    (probe_grad,) = call(
        probe_sum_kernel,
        "probe_sum",
        (((1, 2, modes, n, n), F32),),
        (part0, part1),
        smem=0,
        after=(),
    )
    (object_grad,) = call(
        finish_kernel,
        "finish",
        ((object_tiles.shape, F32),),
        (info, mine_first, other_first, mine_re, other_re, mine_im, other_im),
    )
    return (object_grad, probe_grad)


def solution(mesh):
    placed = (
        P("tile", None, None, None, None),
        P(None, "mode", None, None),
        P(),
        P("tile", None, None),
        P("tile"),
        P("tile", None, None, None),
    )
    return jax.shard_map(
        body,
        mesh=mesh,
        in_specs=placed,
        out_specs=(P("tile", None, None, None, None), P("tile", None, "mode", None, None)),
        check_vma=False,
    )
```

```python
import functools
import math

import jax
import jax.numpy as jnp
import ml_dtypes
import numpy as np
from jax import lax
from jax.experimental import pallas as pl
from jax.experimental.pallas import tpu as pltpu
from jax.sharding import PartitionSpec as P

GY = 8
BAND = 16
F32 = jnp.float32
BF16 = jnp.bfloat16
VMEM_LIMIT = 24 * 1024 * 1024


def dft_pair(extent):
    counter = np.arange(extent)
    angle = -2.0 * math.pi / extent * (counter[:, None] * counter[None, :] % extent)
    scale = 1.0 / math.sqrt(extent)
    return (
        (np.cos(angle) * scale).astype(ml_dtypes.bfloat16),
        (np.sin(angle) * scale).astype(ml_dtypes.bfloat16),
    )


def left_form(re, im, xp):
    return xp.concatenate(
        [xp.concatenate([re, -im], axis=1), xp.concatenate([im, re], axis=1)], axis=0
    )


def right_form(re, im, xp):
    return xp.concatenate(
        [xp.concatenate([re, im], axis=1), xp.concatenate([-im, re], axis=1)], axis=0
    )


def dft_tables(extent):
    re, im = dft_pair(extent)
    lefts = [left_form(re[b::2, : extent // 2], im[b::2, : extent // 2], np) for b in range(2)]
    return np.stack(lefts + [left.T for left in lefts])


def mm(a, b):
    return jnp.dot(a, b, preferred_element_type=F32)


def beside(a, b):
    return jnp.concatenate([a, b], axis=1)


def above(a, b):
    return jnp.concatenate([a, b], axis=0)


def band_left(re, im):
    n = re.shape[0]
    h, a, b = n // 2, n // 2 - BAND, n // 2 + BAND
    diag = [left_form(re[r, r], im[r, r], jnp) for r in (slice(0, h), slice(h, n))]
    row = lax.broadcasted_iota(jnp.int32, (2 * BAND, 2 * BAND), 0) < BAND
    col = lax.broadcasted_iota(jnp.int32, (2 * BAND, 2 * BAND), 1) < BAND
    corners = [jnp.where(row == col, 0.0, part[a:b, a:b]) for part in (re, im)]
    return diag, left_form(*corners, jnp)


def prop_left(diag, corner, re, im):
    n = re.shape[0]
    h, a, b = n // 2, n // 2 - BAND, n // 2 + BAND
    re, im = re.astype(BF16), im.astype(BF16)
    top = mm(diag[0], above(re[:h], im[:h]))
    low = mm(diag[1], above(re[h:], im[h:]))
    mid = mm(corner[...], above(re[a:b], im[a:b]))
    re = [top[:a], top[a:h] + mid[:BAND], low[:BAND] + mid[BAND : 2 * BAND], low[BAND:h]]
    mid, top, low = mid[2 * BAND :], top[h:], low[h:]
    im = [top[:a], top[a:h] + mid[:BAND], low[:BAND] + mid[BAND:], low[BAND:]]
    re, im = jnp.concatenate(re, axis=0), jnp.concatenate(im, axis=0)
    return beside(re.astype(BF16), im.astype(BF16))


def dft_left(tabs, re, im):
    h = re.shape[0] // 2
    even = mm(tabs[0], above(re[:h] + re[h:], im[:h] + im[h:]).astype(BF16))
    odd = mm(tabs[1], above(re[:h] - re[h:], im[:h] - im[h:]).astype(BF16))
    re, im = above(even[:h], odd[:h]), above(even[h:], odd[h:])
    e = beside(re[:, :h] + re[:, h:], im[:, :h] + im[:, h:])
    o = beside(re[:, :h] - re[:, h:], im[:, :h] - im[:, h:])
    return beside(e.astype(BF16), o.astype(BF16))


def conj_dft_left(tabs, e, o):
    h = e.shape[0] // 2
    e, o = e.astype(BF16), o.astype(BF16)
    even = mm(tabs[2], above(beside(e[:h, :h], o[:h, :h]), beside(e[:h, h:], o[:h, h:])))
    odd = mm(tabs[3], above(beside(e[h:, :h], o[h:, :h]), beside(e[h:, h:], o[h:, h:])))
    re = above(even[:h] + odd[:h], even[:h] - odd[:h]).astype(BF16)
    im = above(even[h:] + odd[h:], even[h:] - odd[h:]).astype(BF16)
    return beside(beside(re[:, :h], im[:, :h]), beside(re[:, h:], im[:, h:]))


def place_of(off_ref, slot, h):
    row = off_ref[slot, 0] + h
    col = off_ref[slot, 1] + h
    top = pl.multiple_of((row >> 3) * 8, 8)
    block = pl.multiple_of((col >> 7) * 128, 128)
    return top, block, row & 7, col & 127


def ends(info, axis, before, after):
    odd = info[axis]
    first = jnp.where(odd == 1, before, after)
    second = jnp.where(odd == 1, after, before)
    return pl.multiple_of(first, 128), pl.multiple_of(second, 128), info[2 + axis] == 1


def kept(good, value):
    return jnp.where(good, value, 0.0)


def build_canvas(layer, info, own, rows_a, rows_b, cols_b, cols_a, corners_b, canvas):
    n = own.shape[-1]
    h = n // 2
    ra, rb, row_ok = ends(info, 0, 0, h + n)
    ca, cb, col_ok = ends(info, 1, 0, h + n)
    canvas[:, h : h + n, h : h + n] = own[:, layer]
    canvas[:, pl.ds(ra, h), h : h + n] = rows_a[...]
    canvas[:, pl.ds(rb, h), h : h + n] = kept(row_ok, rows_b[...])
    canvas[:, :, pl.ds(ca, h)] = cols_a[...]
    canvas[:, h : h + n, pl.ds(cb, h)] = kept(col_ok, cols_b[:, layer])
    canvas[:, pl.ds(ra, h), pl.ds(cb, h)] = kept(col_ok, corners_b[0])
    canvas[:, pl.ds(rb, h), pl.ds(cb, h)] = kept(row_ok & col_ok, corners_b[1])


def extract(off_ref, slot, canvas, patch):
    n = patch.shape[-1]
    h = n // 2
    top, block, row_rest, col_rest = place_of(off_ref, slot, h)
    row_shift = jnp.where(row_rest == 0, 0, n + 8 - row_rest)
    col_shift = jnp.where(col_rest == 0, 0, n + h - col_rest)
    for part in range(2):
        window = canvas[part, pl.ds(top, n + 8), pl.ds(block, n + h)]
        window = pltpu.roll(window, col_shift, 1)[:, :n]
        patch[part] = pltpu.roll(window, row_shift, 0)[:n]


def lay(off_ref, grads, canvas):
    n = grads[0].shape[-1]
    h = n // 2
    canvas[...] = jnp.zeros_like(canvas)
    for slot, grad in enumerate(grads):
        top, block, row_rest, col_rest = place_of(off_ref, slot, h)
        for part in range(canvas.shape[0]):
            tall = above(grad[part], jnp.zeros((8, n), F32))
            tall = pltpu.roll(tall, row_rest, 0)
            wide = beside(tall, jnp.zeros((n + 8, h), F32))
            canvas[part, pl.ds(top, n + 8), pl.ds(block, n + h)] += pltpu.roll(wide, col_rest, 1)


def times(a_re, a_im, b_re, b_im):
    return a_re * b_re - a_im * b_im, a_re * b_im + a_im * b_re


def by_mode(held, modes, left):
    n = held.shape[0] // modes
    rows = [slice(m * n, (m + 1) * n) for m in range(modes)]
    for m in range(modes):
        held[rows[m]] = left(m)
    return rows


def waves(probe, patch, diag, corner, right, wave, held):
    n = patch.shape[-1]

    def left(m):
        return prop_left(diag, corner, *times(probe[0, m], probe[1, m], patch[0], patch[1]))

    rows = by_mode(held, probe.shape[1], left)
    both = mm(held[...], right[...])
    for m, at in enumerate(rows):
        wave[m, 0] = both[at, :n]
        wave[m, 1] = both[at, n:]


def fars(wave, patch, tabs, far, inten, held):
    n = patch.shape[-1]
    h = n // 2

    def left(m):
        return dft_left(tabs, *times(wave[m, 0], wave[m, 1], patch[0], patch[1]))

    rows = by_mode(held, wave.shape[0], left)
    evens, odds = mm(held[:, :n], tabs[2]), mm(held[:, n:], tabs[3])
    total_e = total_o = 0.0
    for m, at in enumerate(rows):
        e, o = evens[at], odds[at]
        far[m, 0] = e
        far[m, 1] = o
        total_e += e * e
        total_o += o * o
    inten[...] = beside(total_e[:, :h] + total_e[:, h:], total_o[:, :h] + total_o[:, h:])


def waves_first_kernel(off, info, own, rows_a, rows_b, cols_b, cols_a, corners_b, probe,
                       diag, corner, mat, canvas, patch, wave, held):
    build_canvas(0, info, own, rows_a, rows_b, cols_b, cols_a, corners_b, canvas)
    extract(off, 0, canvas, patch)
    waves(probe, patch, diag, corner, mat, wave, held)


def waves_next_kernel(off, canvas, probe, diag, corner, mat, patch, wave, held):
    extract(off, 1, canvas, patch)
    waves(probe, patch, diag, corner, mat, wave, held)


def fars_first_kernel(off, info, own, rows_a, rows_b, cols_b, cols_a, corners_b, wave, tabs,
                      canvas, patch, far, inten, held):
    build_canvas(1, info, own, rows_a, rows_b, cols_b, cols_a, corners_b, canvas)
    extract(off, 0, canvas, patch)
    fars(wave, patch, tabs, far, inten, held)


def fars_next_kernel(off, canvas, wave, tabs, patch, far, inten, held):
    extract(off, 1, canvas, patch)
    fars(wave, patch, tabs, far, inten, held)


def back_last(slot, counts, mine, other, measured, far, wave, patch, tabs, grad, bar, resid, held):
    n = mine.shape[0]
    h = n // 2
    live = jnp.where(slot < counts[0], 2.0, 0.0).astype(F32)
    r = (mine[...] + other[...] - measured[slot]) * live
    resid[0] = beside(r[:, :h], r[:, :h])
    resid[1] = beside(r[:, h:], r[:, h:])
    rows = by_mode(
        held,
        far.shape[0],
        lambda m: conj_dft_left(tabs, resid[0] * far[m, 0], resid[1] * far[m, 1]),
    )
    evens, odds = mm(held[:, :n], tabs[0]), mm(held[:, n:], tabs[1])
    g_re = g_im = 0.0
    o_re, o_im = patch[0], patch[1]
    for m, at in enumerate(rows):
        e, o = evens[at], odds[at]
        b_re = beside(e[:, :h] + o[:, :h], e[:, :h] - o[:, :h])
        b_im = beside(e[:, h:] + o[:, h:], e[:, h:] - o[:, h:])
        w_re, w_im = wave[m, 0], wave[m, 1]
        g_re += w_re * b_re + w_im * b_im
        g_im += w_re * b_im - w_im * b_re
        bar[m, 0] = (o_re * b_re + o_im * b_im).astype(BF16)
        bar[m, 1] = (o_re * b_im - o_im * b_re).astype(BF16)
    grad[0] = g_re
    grad[1] = g_im


def back_last_place_kernel(slot, counts, off, info, before, mine, other, measured, far, wave, patch,
                           tabs, bar, out_a, out_c, out_b, resid, held, grad, canvas):
    back_last(
        slot, counts, mine, other, measured, far, wave, patch, tabs, grad, bar, resid, held
    )
    lay(off, (before, grad), canvas)
    n = grad.shape[-1]
    h = n // 2
    sides(info, canvas, out_a, out_b)
    out_c[...] = canvas[:, :, h : h + n]


def back_first_kernel(info, bar, probe, patch, diag, corner, mat, keep, send, part, grad, held):
    n = patch.shape[-1]
    rows = by_mode(
        held, probe.shape[1], lambda m: prop_left(diag, corner, bar[m, 0], bar[m, 1])
    )
    both = mm(held[...], mat[...])
    g_re = g_im = 0.0
    o_re, o_im = patch[0], patch[1]
    for m, at in enumerate(rows):
        b_re, b_im = both[at, :n], both[at, n:]
        p_re, p_im = probe[0, m], probe[1, m]
        g_re += p_re * b_re + p_im * b_im
        g_im += p_re * b_im - p_im * b_re
        part[0, m] = o_re * b_re + o_im * b_im
        part[1, m] = o_re * b_im - o_im * b_re
    grad[0] = g_re
    grad[1] = g_im
    mode = info[4]
    keep[0] = grad[mode]
    send[0] = grad[1 - mode]


def probe_sum_kernel(part0, part1, total):
    total[0] = part0[...] + part1[...]


def sides(info, canvas, out_a, out_b):
    h = out_a.shape[-1]
    a, b, _ = ends(info, 1, 0, 3 * h)
    out_a[...] = canvas[:, :, pl.ds(a, h)]
    out_b[...] = canvas[:, :, pl.ds(b, h)]


def lay_sums(off, parts, canvas, sums):
    for slot in range(2):
        sums[slot] = parts[2 * slot][...] + parts[2 * slot + 1][...]
    lay(off, (sums.at[0], sums.at[1]), canvas)


def place_sides_kernel(off, info, keep0, got0, keep1, got1, out_a, out_b, canvas, sums):
    lay_sums(off, (keep0, got0, keep1, got1), canvas, sums)
    sides(info, canvas, out_a, out_b)


def place_center_kernel(off, keep0, got0, keep1, got1, out_c, canvas, sums):
    lay_sums(off, (keep0, got0, keep1, got1), canvas, sums)
    h = keep0.shape[-1] // 2
    out_c[...] = canvas[:, :, h : 3 * h]


def fold_cols_kernel(info, center, got_a, got_b, out_a, mid, out_b):
    n = center.shape[-1]
    h = n // 2
    ca, cb, col_ok = ends(info, 1, 0, h)
    ra, rb, _ = ends(info, 0, 0, h + n)
    for a, out in ((ra, out_a), (rb, out_b)):
        out[:, :, pl.ds(ca, h)] = center[:, pl.ds(a, h), pl.ds(ca, h)] + got_a[:, pl.ds(a, h)]
        out[:, :, pl.ds(cb, h)] = center[:, pl.ds(a, h), pl.ds(cb, h)] + kept(
            col_ok, got_b[:, pl.ds(a, h)]
        )
    mid[:, :, pl.ds(ca, h)] = center[:, h : h + n, pl.ds(ca, h)] + got_a[:, h : h + n]
    mid[:, :, pl.ds(cb, h)] = center[:, h : h + n, pl.ds(cb, h)] + kept(
        col_ok, got_b[:, h : h + n]
    )


def fold_rows_kernel(info, mid, got_a, got_b, *outs):
    h = got_a.shape[1]
    ra, rb, row_ok = ends(info, 0, 0, h)
    for plane, out in enumerate(outs):
        out[0, pl.ds(ra, h)] = mid[plane, pl.ds(ra, h)] + got_a[plane]
        out[0, pl.ds(rb, h)] = mid[plane, pl.ds(rb, h)] + kept(row_ok, got_b[plane])


def finish_last_kernel(info, mine_first, mine_re, other_re, mine_im, other_im, out, sums, sems):
    sums[0] = mine_re[0] + other_re[0]
    sums[1] = mine_im[0] + other_im[0]
    moves = ((sums.at[0], out.at[0, 0, 1]), (sums.at[1], out.at[0, 1, 1]),
             (mine_first.at[0], out.at[0, info[4], 0]))
    copies = [pltpu.make_async_copy(a, b, sems.at[i]) for i, (a, b) in enumerate(moves)]
    for copy in copies:
        copy.start()
    for copy in copies:
        copy.wait()


def finish_kernel(info, other_first, partial, out, sems):
    copy = pltpu.make_async_copy(other_first.at[0], out.at[0, 1 - info[4], 0], sems.at[0])
    copy.start()
    copy.wait()


def pick_rows_kernel(info, own, *refs):
    *outs, sems = refs
    h = outs[0].shape[1]
    a, b, _ = ends(info, 0, 0, h)
    copies = []
    for layer in range(2):
        for i, start in enumerate((a, b)):
            k = 2 * layer + i
            copies.append(pltpu.make_async_copy(
                own.at[:, layer, pl.ds(start, h), :], outs[k], sems.at[k]))
    for copy in copies:
        copy.start()
    for copy in copies:
        copy.wait()


def pick_cols_kernel(info, own, out_b):
    h = out_b.shape[-1]
    _, b, _ = ends(info, 1, 0, h)
    out_b[...] = own[:, :, :, pl.ds(b, h)]


def pick_rest_kernel(layer, info, own, rows_a, rows_b, out_a, corners_b):
    n = own.shape[-1]
    h = n // 2
    ra, rb, row_ok = ends(info, 0, 0, h + n)
    a, b, _ = ends(info, 1, 0, h)
    a, b = pl.ds(a, h), pl.ds(b, h)
    out_a[:, h : h + n] = own[:, layer, :, a]
    out_a[:, pl.ds(ra, h)] = rows_a[:, :, a]
    out_a[:, pl.ds(rb, h)] = kept(row_ok, rows_b[:, :, a])
    corners_b[0] = rows_a[:, :, b]
    corners_b[1] = rows_b[:, :, b]


def prepare_kernel(prop_in, probe_in, diag, corner, right, back_diag, back_corner, back_right,
                   probe_out, prop, sems):
    copies = [
        pltpu.make_async_copy(prop_in, prop, sems.at[0]),
        pltpu.make_async_copy(probe_in, probe_out, sems.at[1]),
    ]
    for copy in copies:
        copy.start()
    copies[0].wait()
    re, im = prop[0].astype(F32), prop[1].astype(F32)
    re_t, im_t = re.T, im.T
    for out, edge, pair in ((diag, corner, (re, im)), (back_diag, back_corner, (re_t, -im_t))):
        blocks, corners = band_left(*pair)
        out[0] = blocks[0].astype(BF16)
        out[1] = blocks[1].astype(BF16)
        edge[...] = corners.astype(BF16)
    right[...] = right_form(re_t, im_t, jnp).astype(BF16)
    back_right[...] = right_form(re, -im, jnp).astype(BF16)
    copies[1].wait()


def reorder_kernel(measured, tabs, out, tabs_out):
    n = out.shape[-1]
    h = n // 2
    tabs_out[...] = tabs[...]
    exact = functools.partial(
        jnp.dot, precision=lax.Precision.HIGHEST, preferred_element_type=F32
    )

    def order(to, of):
        a = lax.broadcasted_iota(jnp.int32, (n, n), to)
        b = lax.broadcasted_iota(jnp.int32, (n, n), of)
        return jnp.where(jnp.where(a < h, 2 * a, 2 * a - n + 1) == b, 1.0, 0.0).astype(F32)

    for slot in range(out.shape[0]):
        out[slot] = exact(exact(order(0, 1), measured[slot]), order(1, 0))


def swap(value, axis, second):
    count = lax.axis_size("tile")
    step, length = (GY, count // GY) if axis == 0 else (1, GY)
    pairs = []
    for i in range(count):
        at = i // step % length
        to = (at + (1 if (at % 2 == 1) == second else -1)) % length
        pairs.append((i, i + (to - at) * step))
    return lax.ppermute(value, "tile", pairs)


def swap_mode(value):
    return lax.ppermute(value, "mode", [(0, 1), (1, 0)])


def call(kernel, name, outs, args, scratch=(), smem=1, after=(), copies=0, out=None, alias=None):
    vmem = pl.BlockSpec(memory_space=pltpu.VMEM)
    held = pl.BlockSpec(memory_space=pltpu.HBM) if copies and out is None else vmem
    out = vmem if out is None else pl.BlockSpec(memory_space=out)
    scalars = pl.BlockSpec(memory_space=pltpu.SMEM)
    n_args, n_after = len(args), len(after)

    def run(*refs):
        kept_args = n_args if alias is None else n_args + n_after
        kernel(*refs[:kept_args], *refs[n_args + n_after :])

    return pl.pallas_call(
        run,
        out_shape=tuple(jax.ShapeDtypeStruct(shape, dtype) for shape, dtype in outs),
        in_specs=[scalars] * smem
        + [held] * (n_args - smem)
        + [pl.BlockSpec(memory_space=pl.ANY)] * n_after,
        out_specs=tuple(out for _ in outs),
        input_output_aliases={} if alias is None else {alias: 0},
        scratch_shapes=[pltpu.VMEM(shape, dtype) for shape, dtype in scratch]
        + [pltpu.SemaphoreType.DMA((copies,))] * (copies > 0),
        compiler_params=pltpu.CompilerParams(vmem_limit_bytes=VMEM_LIMIT),
        name=name,
    )(*args, *after)


def body(object_tiles, probe_modes, propagator, offsets, counts, measured):
    n = probe_modes.shape[-1]
    h = n // 2
    modes = probe_modes.shape[1]
    slots = measured.shape[1]
    own = object_tiles[0]
    off = offsets[0]

    tile = lax.axis_index("tile")
    row, col = tile // GY, tile % GY
    n_rows = lax.axis_size("tile") // GY
    odd_row, odd_col = row % 2 == 1, col % 2 == 1
    paired = [(row > 0) & (row < n_rows - 1), (col > 0) & (col < GY - 1)]
    info = jnp.stack([odd_row, odd_col, *paired, lax.axis_index("mode") == 1]).astype(jnp.int32)

    one, pair, mat = ((1, n, n), F32), ((2, n, n), F32), ((2 * n, 2 * n), BF16)
    plane, field, probes = ((n, n), F32), ((modes, 2, n, n), F32), ((2, modes, n, n), F32)
    band = (((2, n, n), BF16), ((4 * BAND, 4 * BAND), BF16), mat)
    held = ((modes * n, 2 * n), BF16)
    strip, tall = ((2, h, n), F32), ((2, 2 * n, h), F32)
    side_strip, quarter = ((2, 2, n, h), F32), ((2, 2, h, h), F32)

    picked = call(pick_rows_kernel, "pick_rows", (strip,) * 4, (info, own), copies=4)
    rows = [[swap(picked[2 * i + k], 0, k == 1) for k in range(2)] for i in range(2)]
    *made, probe = call(
        prepare_kernel,
        "prepare",
        band + band + (probes,),
        (propagator, probe_modes),
        scratch=(((2, n, n), BF16),),
        smem=0,
        copies=2,
    )
    prop, back_prop = made[:3], made[3:]
    tabs = jnp.asarray(dft_tables(n))
    measured, tabs = call(
        reorder_kernel,
        "reorder",
        (((slots, n, n), F32), (tabs.shape, BF16)),
        (measured[0], tabs),
        smem=0,
    )

    (picked,) = call(pick_cols_kernel, "pick_cols", (side_strip,), (info, own), after=())
    cols_b = swap(picked, 1, True)

    def beside_tiles(layer, after):
        picked = call(functools.partial(pick_rest_kernel, layer), f"pick_rest_{layer}",
                      (tall, quarter), (info, own, *rows[layer]), after=after)
        rest = [swap(picked[k], 1, k == 1) for k in range(2)]
        return (own, *rows[layer], cols_b, *rest)

    first = beside_tiles(0, (probe,))
    last = beside_tiles(1, (measured, first[3],first[5]))
    canvas, patch_first0, wave0 = call(
        waves_first_kernel,
        "waves_0",
        (((2, 2 * n, 2 * n), F32), pair, field),
        (off, info, *first, probe, *prop),
        scratch=(held,),
        smem=2,
        after=(),
    )
    patch_first1, wave1 = call(
        waves_next_kernel, "waves_1", (pair, field), (off, canvas, probe, *prop), scratch=(held,),
        after=()
    )
    canvas, patch_last0, far0, inten0 = call(
        fars_first_kernel,
        "fars_0",
        (((2, 2 * n, 2 * n), F32), pair, field, plane),
        (off, info, *last, wave0, tabs),
        scratch=(held,),
        smem=2,
        after=(patch_first1,),
    )
    other0 = swap_mode(inten0)
    patch_last1, far1, inten1 = call(
        fars_next_kernel, "fars_1", (pair, field, plane), (off, canvas, wave1, tabs), scratch=(held,)
    )
    other1 = swap_mode(inten1)

    bar_out = ((modes, 2, n, n), BF16)
    strips = (((2, 2 * n, h), F32), ((2, 2 * n, n), F32), ((2, 2 * n, h), F32))
    wide = ((2, 2 * n, 2 * n), F32)
    grad_last0, bar0 = call(
        functools.partial(back_last, 0),
        "back_last_0",
        (pair, bar_out),
        (counts, inten0, other0, measured, far0, wave0, patch_last0, tabs),
        scratch=(pair, held),
    )
    keep0, send0, part0 = call(
        back_first_kernel,
        "back_first_0",
        (one, one, probes),
        (info, bar0, probe, patch_first0, *back_prop),
        scratch=(pair, held),
    )
    got0 = swap_mode(send0)
    bar1, out_a, out_c, out_b = call(
        functools.partial(back_last_place_kernel, 1),
        "back_last_1",
        (bar_out,) + strips,
        (counts, off, info, grad_last0, inten1, other1, measured, far1, wave1, patch_last1, tabs),
        scratch=(pair, held, pair, wide),
        smem=3,
        after=(keep0,),
    )

    def fold_cols(name, out_a, out_c, out_b, after):
        got_a, got_b = swap(out_a, 1, False), swap(out_b, 1, True)
        planes = out_c.shape[0]
        half, mid = ((planes, h, n), F32), ((planes, n, n), F32)
        return call(fold_cols_kernel, name, (half, mid, half), (info, out_c, got_a, got_b),
                    after=after)

    def fold_rows(name, out_a, mid, out_b, after):
        got_a, got_b = swap(out_a, 0, False), swap(out_b, 0, True)
        return call(fold_rows_kernel, name, (one,) * mid.shape[0], (info, mid, got_a, got_b),
                    after=after)

    keep1, send1, part1 = call(
        back_first_kernel,
        "back_first_1",
        (one, one, probes),
        (info, bar1, probe, patch_first1, *back_prop),
        scratch=(pair, held),
    )
    got1 = swap_mode(send1)
    strips_last = fold_cols("cols_last", out_a, out_c, out_b, (keep1,))
    mine_re, mine_im = fold_rows("rows_last", *strips_last, ())
    other_re, other_im = swap_mode(mine_re), swap_mode(mine_im)
    strips = [((1,) + shape[1:], dtype) for shape, dtype in strips]
    wide = ((1, 2 * n, 2 * n), F32)
    parts = (keep0, got0, keep1, got1)
    out_a, out_b = call(
        place_sides_kernel,
        "place_sides",
        (strips[0], strips[2]),
        (off, info, *parts),
        scratch=(wide, ((2, 1, n, n), F32)),
        smem=2,
        after=(strips_last[0],),
    )
    (out_c,) = call(
        place_center_kernel,
        "place_center",
        (strips[1],),
        (off, *parts),
        scratch=(wide, ((2, 1, n, n), F32)),
        after=(out_a,),
    )
    strips_first = fold_cols("cols_first", out_a, out_c, out_b, ())
    (mine_first,) = fold_rows("rows_first", *strips_first, (other_re,))
    other_first = swap_mode(mine_first)
    (probe_grad,) = call(
        probe_sum_kernel,
        "probe_sum",
        (((1, 2, modes, n, n), F32),),
        (part0, part1),
        smem=0,
        after=(),
    )
    shape = ((object_tiles.shape, F32),)
    (partial,) = call(
        finish_last_kernel,
        "finish_last",
        shape,
        (info, mine_first, mine_re, other_re, mine_im, other_im),
        scratch=(pair,),
        copies=3,
        out=pl.ANY,
    )
    (object_grad,) = call(
        finish_kernel,
        "finish",
        shape,
        (info, other_first),
        after=(partial,),
        copies=1,
        out=pl.ANY,
        alias=2,
    )
    return (object_grad, probe_grad)


def solution(mesh):
    placed = (
        P("tile", None, None, None, None),
        P(None, "mode", None, None),
        P(),
        P("tile", None, None),
        P("tile"),
        P("tile", None, None, None),
    )
    return jax.shard_map(
        body,
        mesh=mesh,
        in_specs=placed,
        out_specs=(P("tile", None, None, None, None), P("tile", None, "mode", None, None)),
        check_vma=False,
    )
```

```python
import functools
import math

import jax
import jax.numpy as jnp
import ml_dtypes
import numpy as np
from jax import lax
from jax.experimental import pallas as pl
from jax.experimental.pallas import tpu as pltpu
from jax.sharding import PartitionSpec as P

GY = 8
BAND = 16
F32 = jnp.float32
BF16 = jnp.bfloat16
VMEM_LIMIT = 24 * 1024 * 1024


def dft_pair(extent):
    counter = np.arange(extent)
    angle = -2.0 * math.pi / extent * (counter[:, None] * counter[None, :] % extent)
    scale = 1.0 / math.sqrt(extent)
    return (
        (np.cos(angle) * scale).astype(ml_dtypes.bfloat16),
        (np.sin(angle) * scale).astype(ml_dtypes.bfloat16),
    )


def left_form(re, im, xp):
    return xp.concatenate(
        [xp.concatenate([re, -im], axis=1), xp.concatenate([im, re], axis=1)], axis=0
    )


def right_form(re, im, xp):
    return xp.concatenate(
        [xp.concatenate([re, im], axis=1), xp.concatenate([-im, re], axis=1)], axis=0
    )


def dft_tables(extent):
    re, im = dft_pair(extent)
    lefts = [left_form(re[b::2, : extent // 2], im[b::2, : extent // 2], np) for b in range(2)]
    return np.stack(lefts + [left.T for left in lefts])


def mm(a, b):
    return jnp.dot(a, b, preferred_element_type=F32)


def beside(a, b):
    return jnp.concatenate([a, b], axis=1)


def above(a, b):
    return jnp.concatenate([a, b], axis=0)


def band_left(re, im):
    n = re.shape[0]
    h, a, b = n // 2, n // 2 - BAND, n // 2 + BAND
    diag = [left_form(re[r, r], im[r, r], jnp) for r in (slice(0, h), slice(h, n))]
    row = lax.broadcasted_iota(jnp.int32, (2 * BAND, 2 * BAND), 0) < BAND
    col = lax.broadcasted_iota(jnp.int32, (2 * BAND, 2 * BAND), 1) < BAND
    corners = [jnp.where(row == col, 0.0, part[a:b, a:b]) for part in (re, im)]
    return diag, left_form(*corners, jnp)


def prop_left(diag, corner, re, im):
    n = re.shape[0]
    h, a, b = n // 2, n // 2 - BAND, n // 2 + BAND
    re, im = re.astype(BF16), im.astype(BF16)
    top = mm(diag[0], above(re[:h], im[:h]))
    low = mm(diag[1], above(re[h:], im[h:]))
    mid = mm(corner[...], above(re[a:b], im[a:b]))
    re = [top[:a], top[a:h] + mid[:BAND], low[:BAND] + mid[BAND : 2 * BAND], low[BAND:h]]
    mid, top, low = mid[2 * BAND :], top[h:], low[h:]
    im = [top[:a], top[a:h] + mid[:BAND], low[:BAND] + mid[BAND:], low[BAND:]]
    re, im = jnp.concatenate(re, axis=0), jnp.concatenate(im, axis=0)
    return beside(re.astype(BF16), im.astype(BF16))


def dft_left(tabs, re, im):
    h = re.shape[0] // 2
    even = mm(tabs[0], above(re[:h] + re[h:], im[:h] + im[h:]).astype(BF16))
    odd = mm(tabs[1], above(re[:h] - re[h:], im[:h] - im[h:]).astype(BF16))
    re, im = above(even[:h], odd[:h]), above(even[h:], odd[h:])
    e = beside(re[:, :h] + re[:, h:], im[:, :h] + im[:, h:])
    o = beside(re[:, :h] - re[:, h:], im[:, :h] - im[:, h:])
    return beside(e.astype(BF16), o.astype(BF16))


def conj_dft_left(tabs, e, o):
    h = e.shape[0] // 2
    e, o = e.astype(BF16), o.astype(BF16)
    even = mm(tabs[2], above(beside(e[:h, :h], o[:h, :h]), beside(e[:h, h:], o[:h, h:])))
    odd = mm(tabs[3], above(beside(e[h:, :h], o[h:, :h]), beside(e[h:, h:], o[h:, h:])))
    re = above(even[:h] + odd[:h], even[:h] - odd[:h]).astype(BF16)
    im = above(even[h:] + odd[h:], even[h:] - odd[h:]).astype(BF16)
    return beside(beside(re[:, :h], im[:, :h]), beside(re[:, h:], im[:, h:]))


def place_of(off_ref, slot, h):
    row = off_ref[slot, 0] + h
    col = off_ref[slot, 1] + h
    top = pl.multiple_of((row >> 3) * 8, 8)
    block = pl.multiple_of((col >> 7) * 128, 128)
    return top, block, row & 7, col & 127


def ends(info, axis, before, after):
    odd = info[axis]
    first = jnp.where(odd == 1, before, after)
    second = jnp.where(odd == 1, after, before)
    return pl.multiple_of(first, 128), pl.multiple_of(second, 128), info[2 + axis] == 1


def kept(good, value):
    return jnp.where(good, value, 0.0)


def build_canvas(layer, info, own, rows_a, rows_b, cols_b, cols_a, corners_b, canvas):
    n = own.shape[-1]
    h = n // 2
    ra, rb, row_ok = ends(info, 0, 0, h + n)
    ca, cb, col_ok = ends(info, 1, 0, h + n)
    canvas[:, h : h + n, h : h + n] = own[:, layer]
    canvas[:, pl.ds(ra, h), h : h + n] = rows_a[...]
    canvas[:, pl.ds(rb, h), h : h + n] = kept(row_ok, rows_b[...])
    canvas[:, :, pl.ds(ca, h)] = cols_a[...]
    canvas[:, h : h + n, pl.ds(cb, h)] = kept(col_ok, cols_b[:, layer])
    canvas[:, pl.ds(ra, h), pl.ds(cb, h)] = kept(col_ok, corners_b[0])
    canvas[:, pl.ds(rb, h), pl.ds(cb, h)] = kept(row_ok & col_ok, corners_b[1])


def extract(off_ref, slot, canvas, patch):
    n = patch.shape[-1]
    h = n // 2
    top, block, row_rest, col_rest = place_of(off_ref, slot, h)
    row_shift = jnp.where(row_rest == 0, 0, n + 8 - row_rest)
    col_shift = jnp.where(col_rest == 0, 0, n + h - col_rest)
    for part in range(2):
        window = canvas[part, pl.ds(top, n + 8), pl.ds(block, n + h)]
        window = pltpu.roll(window, col_shift, 1)[:, :n]
        patch[part] = pltpu.roll(window, row_shift, 0)[:n]


def lay(off_ref, grads, canvas):
    n = grads[0].shape[-1]
    h = n // 2
    canvas[...] = jnp.zeros_like(canvas)
    for slot, grad in enumerate(grads):
        top, block, row_rest, col_rest = place_of(off_ref, slot, h)
        for part in range(canvas.shape[0]):
            tall = above(grad[part], jnp.zeros((8, n), F32))
            tall = pltpu.roll(tall, row_rest, 0)
            wide = beside(tall, jnp.zeros((n + 8, h), F32))
            canvas[part, pl.ds(top, n + 8), pl.ds(block, n + h)] += pltpu.roll(wide, col_rest, 1)


def times(a_re, a_im, b_re, b_im):
    return a_re * b_re - a_im * b_im, a_re * b_im + a_im * b_re


def by_mode(held, modes, left):
    n = held.shape[0] // modes
    rows = [slice(m * n, (m + 1) * n) for m in range(modes)]
    for m in range(modes):
        held[rows[m]] = left(m)
    return rows


def waves(probe, patch, diag, corner, right, wave, held):
    n = patch.shape[-1]

    def left(m):
        return prop_left(diag, corner, *times(probe[0, m], probe[1, m], patch[0], patch[1]))

    rows = by_mode(held, probe.shape[1], left)
    both = mm(held[...], right[...])
    for m, at in enumerate(rows):
        wave[m, 0] = both[at, :n]
        wave[m, 1] = both[at, n:]


def fars(wave, patch, tabs, far, inten, held):
    n = patch.shape[-1]
    h = n // 2

    def left(m):
        return dft_left(tabs, *times(wave[m, 0], wave[m, 1], patch[0], patch[1]))

    rows = by_mode(held, wave.shape[0], left)
    evens, odds = mm(held[:, :n], tabs[2]), mm(held[:, n:], tabs[3])
    total_e = total_o = 0.0
    for m, at in enumerate(rows):
        e, o = evens[at], odds[at]
        far[m, 0] = e
        far[m, 1] = o
        total_e += e * e
        total_o += o * o
    inten[...] = beside(total_e[:, :h] + total_e[:, h:], total_o[:, :h] + total_o[:, h:])


def waves_first_kernel(off, info, own, rows_a, rows_b, cols_b, cols_a, corners_b, probe,
                       diag, corner, mat, canvas, patch, wave, held):
    build_canvas(0, info, own, rows_a, rows_b, cols_b, cols_a, corners_b, canvas)
    extract(off, 0, canvas, patch)
    waves(probe, patch, diag, corner, mat, wave, held)


def waves_next_kernel(off, canvas, probe, diag, corner, mat, patch, wave, held):
    extract(off, 1, canvas, patch)
    waves(probe, patch, diag, corner, mat, wave, held)


def fars_first_kernel(off, info, own, rows_a, rows_b, cols_b, cols_a, corners_b, wave, tabs,
                      canvas, patch, far, inten, held):
    build_canvas(1, info, own, rows_a, rows_b, cols_b, cols_a, corners_b, canvas)
    extract(off, 0, canvas, patch)
    fars(wave, patch, tabs, far, inten, held)


def fars_next_kernel(off, canvas, wave, tabs, patch, far, inten, held):
    extract(off, 1, canvas, patch)
    fars(wave, patch, tabs, far, inten, held)


def back_last(slot, counts, mine, other, measured, far, wave, patch, tabs, grad, bar, resid, held):
    n = mine.shape[0]
    h = n // 2
    live = jnp.where(slot < counts[0], 2.0, 0.0).astype(F32)
    r = (mine[...] + other[...] - measured[slot]) * live
    resid[0] = beside(r[:, :h], r[:, :h])
    resid[1] = beside(r[:, h:], r[:, h:])
    rows = by_mode(
        held,
        far.shape[0],
        lambda m: conj_dft_left(tabs, resid[0] * far[m, 0], resid[1] * far[m, 1]),
    )
    evens, odds = mm(held[:, :n], tabs[0]), mm(held[:, n:], tabs[1])
    g_re = g_im = 0.0
    o_re, o_im = patch[0], patch[1]
    for m, at in enumerate(rows):
        e, o = evens[at], odds[at]
        b_re = beside(e[:, :h] + o[:, :h], e[:, :h] - o[:, :h])
        b_im = beside(e[:, h:] + o[:, h:], e[:, h:] - o[:, h:])
        w_re, w_im = wave[m, 0], wave[m, 1]
        g_re += w_re * b_re + w_im * b_im
        g_im += w_re * b_im - w_im * b_re
        bar[m, 0] = (o_re * b_re + o_im * b_im).astype(BF16)
        bar[m, 1] = (o_re * b_im - o_im * b_re).astype(BF16)
    grad[0] = g_re
    grad[1] = g_im


def back_last_place_kernel(slot, counts, off, info, before, mine, other, measured, far, wave, patch,
                           tabs, bar, out_a, out_c, out_b, resid, held, grad, canvas):
    back_last(
        slot, counts, mine, other, measured, far, wave, patch, tabs, grad, bar, resid, held
    )
    lay(off, (before, grad), canvas)
    n = grad.shape[-1]
    h = n // 2
    sides(info, canvas, out_a, out_b)
    out_c[...] = canvas[:, :, h : h + n]


def back_first_kernel(info, bar, probe, patch, diag, corner, mat, keep, send, part, grad, held):
    n = patch.shape[-1]
    rows = by_mode(
        held, probe.shape[1], lambda m: prop_left(diag, corner, bar[m, 0], bar[m, 1])
    )
    both = mm(held[...], mat[...])
    g_re = g_im = 0.0
    o_re, o_im = patch[0], patch[1]
    for m, at in enumerate(rows):
        b_re, b_im = both[at, :n], both[at, n:]
        p_re, p_im = probe[0, m], probe[1, m]
        g_re += p_re * b_re + p_im * b_im
        g_im += p_re * b_im - p_im * b_re
        part[0, m] = o_re * b_re + o_im * b_im
        part[1, m] = o_re * b_im - o_im * b_re
    grad[0] = g_re
    grad[1] = g_im
    mode = info[4]
    keep[0] = grad[mode]
    send[0] = grad[1 - mode]


def probe_sum_kernel(part0, part1, total):
    total[0] = part0[...] + part1[...]


def sides(info, canvas, out_a, out_b):
    h = out_a.shape[-1]
    a, b, _ = ends(info, 1, 0, 3 * h)
    out_a[...] = canvas[:, :, pl.ds(a, h)]
    out_b[...] = canvas[:, :, pl.ds(b, h)]


def lay_sums(off, parts, canvas, sums):
    for slot in range(2):
        sums[slot] = parts[2 * slot][...] + parts[2 * slot + 1][...]
    lay(off, (sums.at[0], sums.at[1]), canvas)


def place_sides_kernel(off, info, keep0, got0, keep1, got1, out_a, out_b, canvas, sums):
    lay_sums(off, (keep0, got0, keep1, got1), canvas, sums)
    sides(info, canvas, out_a, out_b)


def place_center_kernel(off, keep0, got0, keep1, got1, out_c, canvas, sums):
    lay_sums(off, (keep0, got0, keep1, got1), canvas, sums)
    h = keep0.shape[-1] // 2
    out_c[...] = canvas[:, :, h : 3 * h]


def fold_cols_kernel(info, center, got_a, got_b, out_a, mid, out_b):
    n = center.shape[-1]
    h = n // 2
    ca, cb, col_ok = ends(info, 1, 0, h)
    ra, rb, _ = ends(info, 0, 0, h + n)
    for a, out in ((ra, out_a), (rb, out_b)):
        out[:, :, pl.ds(ca, h)] = center[:, pl.ds(a, h), pl.ds(ca, h)] + got_a[:, pl.ds(a, h)]
        out[:, :, pl.ds(cb, h)] = center[:, pl.ds(a, h), pl.ds(cb, h)] + kept(
            col_ok, got_b[:, pl.ds(a, h)]
        )
    mid[:, :, pl.ds(ca, h)] = center[:, h : h + n, pl.ds(ca, h)] + got_a[:, h : h + n]
    mid[:, :, pl.ds(cb, h)] = center[:, h : h + n, pl.ds(cb, h)] + kept(
        col_ok, got_b[:, h : h + n]
    )


def fold_rows_kernel(info, mid, got_a, got_b, *outs):
    h = got_a.shape[1]
    ra, rb, row_ok = ends(info, 0, 0, h)
    for plane, out in enumerate(outs):
        out[0, pl.ds(ra, h)] = mid[plane, pl.ds(ra, h)] + got_a[plane]
        out[0, pl.ds(rb, h)] = mid[plane, pl.ds(rb, h)] + kept(row_ok, got_b[plane])


def finish_last_kernel(info, mine_first, mine_re, other_re, mine_im, other_im, out, sums, sems):
    sums[0] = mine_re[0] + other_re[0]
    sums[1] = mine_im[0] + other_im[0]
    moves = ((sums.at[0], out.at[0, 0, 1]), (sums.at[1], out.at[0, 1, 1]),
             (mine_first.at[0], out.at[0, info[4], 0]))
    copies = [pltpu.make_async_copy(a, b, sems.at[i]) for i, (a, b) in enumerate(moves)]
    for copy in copies:
        copy.start()
    for copy in copies:
        copy.wait()


def finish_kernel(info, other_first, partial, out, sems):
    copy = pltpu.make_async_copy(other_first.at[0], out.at[0, 1 - info[4], 0], sems.at[0])
    copy.start()
    copy.wait()


def pick_rows_kernel(info, own, out_a, out_b, sems):
    h = out_a.shape[1]
    a, b, _ = ends(info, 0, 0, h)
    copies = [
        pltpu.make_async_copy(own.at[:, 1, pl.ds(start, h), :], out, sems.at[k])
        for k, (start, out) in enumerate(((a, out_a), (b, out_b)))
    ]
    for copy in copies:
        copy.start()
    for copy in copies:
        copy.wait()


def pick_cols_kernel(info, own, out_b):
    h = out_b.shape[-1]
    _, b, _ = ends(info, 1, 0, h)
    out_b[...] = own[:, :, :, pl.ds(b, h)]


def pick_rest_kernel(layer, info, own, rows_a, rows_b, out_a, corners_b):
    n = own.shape[-1]
    h = n // 2
    ra, rb, row_ok = ends(info, 0, 0, h + n)
    a, b, _ = ends(info, 1, 0, h)
    a, b = pl.ds(a, h), pl.ds(b, h)
    out_a[:, h : h + n] = own[:, layer, :, a]
    out_a[:, pl.ds(ra, h)] = rows_a[:, :, a]
    out_a[:, pl.ds(rb, h)] = kept(row_ok, rows_b[:, :, a])
    corners_b[0] = rows_a[:, :, b]
    corners_b[1] = rows_b[:, :, b]


def prepare_kernel(prop_in, probe_in, diag, corner, right, back_diag, back_corner, back_right,
                   probe_out, prop, sems):
    copies = [
        pltpu.make_async_copy(prop_in, prop, sems.at[0]),
        pltpu.make_async_copy(probe_in, probe_out, sems.at[1]),
    ]
    for copy in copies:
        copy.start()
    copies[0].wait()
    re, im = prop[0].astype(F32), prop[1].astype(F32)
    re_t, im_t = re.T, im.T
    for out, edge, pair in ((diag, corner, (re, im)), (back_diag, back_corner, (re_t, -im_t))):
        blocks, corners = band_left(*pair)
        out[0] = blocks[0].astype(BF16)
        out[1] = blocks[1].astype(BF16)
        edge[...] = corners.astype(BF16)
    right[...] = right_form(re_t, im_t, jnp).astype(BF16)
    back_right[...] = right_form(re, -im, jnp).astype(BF16)
    copies[1].wait()


def reorder_kernel(measured, tabs, out, tabs_out):
    n = out.shape[-1]
    h = n // 2
    tabs_out[...] = tabs[...]
    exact = functools.partial(
        jnp.dot, precision=lax.Precision.HIGHEST, preferred_element_type=F32
    )

    def order(to, of):
        a = lax.broadcasted_iota(jnp.int32, (n, n), to)
        b = lax.broadcasted_iota(jnp.int32, (n, n), of)
        return jnp.where(jnp.where(a < h, 2 * a, 2 * a - n + 1) == b, 1.0, 0.0).astype(F32)

    for slot in range(out.shape[0]):
        out[slot] = exact(exact(order(0, 1), measured[slot]), order(1, 0))


def swap(value, axis, second):
    count = lax.axis_size("tile")
    step, length = (GY, count // GY) if axis == 0 else (1, GY)
    pairs = []
    for i in range(count):
        at = i // step % length
        to = (at + (1 if (at % 2 == 1) == second else -1)) % length
        pairs.append((i, i + (to - at) * step))
    return lax.ppermute(value, "tile", pairs)


def swap_mode(value):
    return lax.ppermute(value, "mode", [(0, 1), (1, 0)])


def call(kernel, name, outs, args, scratch=(), smem=1, after=(), copies=0, out=None, alias=None):
    vmem = pl.BlockSpec(memory_space=pltpu.VMEM)
    held = pl.BlockSpec(memory_space=pltpu.HBM) if copies and out is None else vmem
    out = vmem if out is None else pl.BlockSpec(memory_space=out)
    scalars = pl.BlockSpec(memory_space=pltpu.SMEM)
    n_args, n_after = len(args), len(after)

    def run(*refs):
        kept_args = n_args if alias is None else n_args + n_after
        kernel(*refs[:kept_args], *refs[n_args + n_after :])

    return pl.pallas_call(
        run,
        out_shape=tuple(jax.ShapeDtypeStruct(shape, dtype) for shape, dtype in outs),
        in_specs=[scalars] * smem
        + [held] * (n_args - smem)
        + [pl.BlockSpec(memory_space=pl.ANY)] * n_after,
        out_specs=tuple(out for _ in outs),
        input_output_aliases={} if alias is None else {alias: 0},
        scratch_shapes=[pltpu.VMEM(shape, dtype) for shape, dtype in scratch]
        + [pltpu.SemaphoreType.DMA((copies,))] * (copies > 0),
        compiler_params=pltpu.CompilerParams(vmem_limit_bytes=VMEM_LIMIT),
        name=name,
    )(*args, *after)


def body(object_tiles, probe_modes, propagator, offsets, counts, measured):
    n = probe_modes.shape[-1]
    h = n // 2
    modes = probe_modes.shape[1]
    slots = measured.shape[1]
    own = object_tiles[0]
    off = offsets[0]

    tile = lax.axis_index("tile")
    row, col = tile // GY, tile % GY
    n_rows = lax.axis_size("tile") // GY
    odd_row, odd_col = row % 2 == 1, col % 2 == 1
    paired = [(row > 0) & (row < n_rows - 1), (col > 0) & (col < GY - 1)]
    info = jnp.stack([odd_row, odd_col, *paired, lax.axis_index("mode") == 1]).astype(jnp.int32)

    one, pair, mat = ((1, n, n), F32), ((2, n, n), F32), ((2 * n, 2 * n), BF16)
    plane, field, probes = ((n, n), F32), ((modes, 2, n, n), F32), ((2, modes, n, n), F32)
    band = (((2, n, n), BF16), ((4 * BAND, 4 * BAND), BF16), mat)
    held = ((modes * n, 2 * n), BF16)
    strip, tall = ((2, h, n), F32), ((2, 2 * n, h), F32)
    side_strip, quarter = ((2, 2, n, h), F32), ((2, 2, h, h), F32)

    top, low = own[:, 0, :h, :], own[:, 0, h:, :]
    picked = [jnp.where(odd_row, top, low), jnp.where(odd_row, low, top)]
    picked += call(pick_rows_kernel, "pick_rows", (strip,) * 2, (info, own), copies=2)
    rows = [[swap(picked[2 * i + k], 0, k == 1) for k in range(2)] for i in range(2)]
    *made, probe = call(
        prepare_kernel,
        "prepare",
        band + band + (probes,),
        (propagator, probe_modes),
        scratch=(((2, n, n), BF16),),
        smem=0,
        copies=2,
    )
    prop, back_prop = made[:3], made[3:]
    tabs = jnp.asarray(dft_tables(n))
    measured, tabs = call(
        reorder_kernel,
        "reorder",
        (((slots, n, n), F32), (tabs.shape, BF16)),
        (measured[0], tabs),
        smem=0,
    )

    (picked,) = call(pick_cols_kernel, "pick_cols", (side_strip,), (info, own), after=())
    cols_b = swap(picked, 1, True)

    def beside_tiles(layer, after):
        picked = call(functools.partial(pick_rest_kernel, layer), f"pick_rest_{layer}",
                      (tall, quarter), (info, own, *rows[layer]), after=after)
        rest = [swap(picked[k], 1, k == 1) for k in range(2)]
        return (own, *rows[layer], cols_b, *rest)

    first = beside_tiles(0, (probe,))
    last = beside_tiles(1, (measured, first[3],first[5]))
    canvas, patch_first0, wave0 = call(
        waves_first_kernel,
        "waves_0",
        (((2, 2 * n, 2 * n), F32), pair, field),
        (off, info, *first, probe, *prop),
        scratch=(held,),
        smem=2,
        after=(),
    )
    patch_first1, wave1 = call(
        waves_next_kernel, "waves_1", (pair, field), (off, canvas, probe, *prop), scratch=(held,),
        after=()
    )
    canvas, patch_last0, far0, inten0 = call(
        fars_first_kernel,
        "fars_0",
        (((2, 2 * n, 2 * n), F32), pair, field, plane),
        (off, info, *last, wave0, tabs),
        scratch=(held,),
        smem=2,
        after=(patch_first1,),
    )
    other0 = swap_mode(inten0)
    patch_last1, far1, inten1 = call(
        fars_next_kernel, "fars_1", (pair, field, plane), (off, canvas, wave1, tabs), scratch=(held,)
    )
    other1 = swap_mode(inten1)

    bar_out = ((modes, 2, n, n), BF16)
    strips = (((2, 2 * n, h), F32), ((2, 2 * n, n), F32), ((2, 2 * n, h), F32))
    wide = ((2, 2 * n, 2 * n), F32)
    grad_last0, bar0 = call(
        functools.partial(back_last, 0),
        "back_last_0",
        (pair, bar_out),
        (counts, inten0, other0, measured, far0, wave0, patch_last0, tabs),
        scratch=(pair, held),
    )
    keep0, send0, part0 = call(
        back_first_kernel,
        "back_first_0",
        (one, one, probes),
        (info, bar0, probe, patch_first0, *back_prop),
        scratch=(pair, held),
    )
    got0 = swap_mode(send0)
    bar1, out_a, out_c, out_b = call(
        functools.partial(back_last_place_kernel, 1),
        "back_last_1",
        (bar_out,) + strips,
        (counts, off, info, grad_last0, inten1, other1, measured, far1, wave1, patch_last1, tabs),
        scratch=(pair, held, pair, wide),
        smem=3,
        after=(keep0,),
    )

    def fold_cols(name, out_a, out_c, out_b, after):
        got_a, got_b = swap(out_a, 1, False), swap(out_b, 1, True)
        planes = out_c.shape[0]
        half, mid = ((planes, h, n), F32), ((planes, n, n), F32)
        return call(fold_cols_kernel, name, (half, mid, half), (info, out_c, got_a, got_b),
                    after=after)

    def fold_rows(name, out_a, mid, out_b, after):
        got_a, got_b = swap(out_a, 0, False), swap(out_b, 0, True)
        return call(fold_rows_kernel, name, (one,) * mid.shape[0], (info, mid, got_a, got_b),
                    after=after)

    keep1, send1, part1 = call(
        back_first_kernel,
        "back_first_1",
        (one, one, probes),
        (info, bar1, probe, patch_first1, *back_prop),
        scratch=(pair, held),
    )
    got1 = swap_mode(send1)
    strips_last = fold_cols("cols_last", out_a, out_c, out_b, (keep1,))
    mine_re, mine_im = fold_rows("rows_last", *strips_last, ())
    other_re, other_im = swap_mode(mine_re), swap_mode(mine_im)
    strips = [((1,) + shape[1:], dtype) for shape, dtype in strips]
    wide = ((1, 2 * n, 2 * n), F32)
    parts = (keep0, got0, keep1, got1)
    out_a, out_b = call(
        place_sides_kernel,
        "place_sides",
        (strips[0], strips[2]),
        (off, info, *parts),
        scratch=(wide, ((2, 1, n, n), F32)),
        smem=2,
        after=(strips_last[0],),
    )
    (out_c,) = call(
        place_center_kernel,
        "place_center",
        (strips[1],),
        (off, *parts),
        scratch=(wide, ((2, 1, n, n), F32)),
        after=(out_a,),
    )
    strips_first = fold_cols("cols_first", out_a, out_c, out_b, ())
    (mine_first,) = fold_rows("rows_first", *strips_first, (other_re, other_im))
    other_first = swap_mode(mine_first)
    (probe_grad,) = call(
        probe_sum_kernel,
        "probe_sum",
        (((1, 2, modes, n, n), F32),),
        (part0, part1),
        smem=0,
        after=(),
    )
    shape = ((object_tiles.shape, F32),)
    (partial,) = call(
        finish_last_kernel,
        "finish_last",
        shape,
        (info, mine_first, mine_re, other_re, mine_im, other_im),
        scratch=(pair,),
        copies=3,
        out=pl.ANY,
    )
    (object_grad,) = call(
        finish_kernel,
        "finish",
        shape,
        (info, other_first),
        after=(partial,),
        copies=1,
        out=pl.ANY,
        alias=2,
    )
    return (object_grad, probe_grad)


def solution(mesh):
    placed = (
        P("tile", None, None, None, None),
        P(None, "mode", None, None),
        P(),
        P("tile", None, None),
        P("tile"),
        P("tile", None, None, None),
    )
    return jax.shard_map(
        body,
        mesh=mesh,
        in_specs=placed,
        out_specs=(P("tile", None, None, None, None), P("tile", None, "mode", None, None)),
        check_vma=False,
    )
```

```python
import functools
import math

import jax
import jax.numpy as jnp
import ml_dtypes
import numpy as np
from jax import lax
from jax.experimental import pallas as pl
from jax.experimental.pallas import tpu as pltpu
from jax.sharding import PartitionSpec as P

GY = 8
BAND = 16
F32 = jnp.float32
BF16 = jnp.bfloat16
VMEM_LIMIT = 24 * 1024 * 1024


def dft_pair(extent):
    counter = np.arange(extent)
    angle = -2.0 * math.pi / extent * (counter[:, None] * counter[None, :] % extent)
    scale = 1.0 / math.sqrt(extent)
    return (
        (np.cos(angle) * scale).astype(ml_dtypes.bfloat16),
        (np.sin(angle) * scale).astype(ml_dtypes.bfloat16),
    )


def left_form(re, im, xp):
    return xp.concatenate(
        [xp.concatenate([re, -im], axis=1), xp.concatenate([im, re], axis=1)], axis=0
    )


def right_form(re, im, xp):
    return xp.concatenate(
        [xp.concatenate([re, im], axis=1), xp.concatenate([-im, re], axis=1)], axis=0
    )


def dft_tables(extent):
    re, im = dft_pair(extent)
    lefts = [left_form(re[b::2, : extent // 2], im[b::2, : extent // 2], np) for b in range(2)]
    return np.stack(lefts + [left.T for left in lefts])


def mm(a, b):
    return jnp.dot(a, b, preferred_element_type=F32)


def beside(a, b):
    return jnp.concatenate([a, b], axis=1)


def above(a, b):
    return jnp.concatenate([a, b], axis=0)


def band_left(re, im):
    n = re.shape[0]
    h, a, b = n // 2, n // 2 - BAND, n // 2 + BAND
    diag = [left_form(re[r, r], im[r, r], jnp) for r in (slice(0, h), slice(h, n))]
    row = lax.broadcasted_iota(jnp.int32, (2 * BAND, 2 * BAND), 0) < BAND
    col = lax.broadcasted_iota(jnp.int32, (2 * BAND, 2 * BAND), 1) < BAND
    corners = [jnp.where(row == col, 0.0, part[a:b, a:b]) for part in (re, im)]
    return diag, left_form(*corners, jnp)


def prop_left(diag, corner, re, im):
    n = re.shape[0]
    h, a, b = n // 2, n // 2 - BAND, n // 2 + BAND
    re, im = re.astype(BF16), im.astype(BF16)
    top = mm(diag[0], above(re[:h], im[:h]))
    low = mm(diag[1], above(re[h:], im[h:]))
    mid = mm(corner[...], above(re[a:b], im[a:b]))
    re = [top[:a], top[a:h] + mid[:BAND], low[:BAND] + mid[BAND : 2 * BAND], low[BAND:h]]
    mid, top, low = mid[2 * BAND :], top[h:], low[h:]
    im = [top[:a], top[a:h] + mid[:BAND], low[:BAND] + mid[BAND:], low[BAND:]]
    re, im = jnp.concatenate(re, axis=0), jnp.concatenate(im, axis=0)
    return beside(re.astype(BF16), im.astype(BF16))


def dft_left(tabs, re, im):
    h = re.shape[0] // 2
    even = mm(tabs[0], above(re[:h] + re[h:], im[:h] + im[h:]).astype(BF16))
    odd = mm(tabs[1], above(re[:h] - re[h:], im[:h] - im[h:]).astype(BF16))
    re, im = above(even[:h], odd[:h]), above(even[h:], odd[h:])
    e = beside(re[:, :h] + re[:, h:], im[:, :h] + im[:, h:])
    o = beside(re[:, :h] - re[:, h:], im[:, :h] - im[:, h:])
    return beside(e.astype(BF16), o.astype(BF16))


def conj_dft_left(tabs, e, o):
    h = e.shape[0] // 2
    e, o = e.astype(BF16), o.astype(BF16)
    even = mm(tabs[2], above(beside(e[:h, :h], o[:h, :h]), beside(e[:h, h:], o[:h, h:])))
    odd = mm(tabs[3], above(beside(e[h:, :h], o[h:, :h]), beside(e[h:, h:], o[h:, h:])))
    re = above(even[:h] + odd[:h], even[:h] - odd[:h]).astype(BF16)
    im = above(even[h:] + odd[h:], even[h:] - odd[h:]).astype(BF16)
    return beside(beside(re[:, :h], im[:, :h]), beside(re[:, h:], im[:, h:]))


def place_of(off_ref, slot, h):
    row = off_ref[slot, 0] + h
    col = off_ref[slot, 1] + h
    top = pl.multiple_of((row >> 3) * 8, 8)
    block = pl.multiple_of((col >> 7) * 128, 128)
    return top, block, row & 7, col & 127


def ends(info, axis, before, after):
    odd = info[axis]
    first = jnp.where(odd == 1, before, after)
    second = jnp.where(odd == 1, after, before)
    return pl.multiple_of(first, 128), pl.multiple_of(second, 128), info[2 + axis] == 1


def kept(good, value):
    return jnp.where(good, value, 0.0)


def build_canvas(layer, info, own, rows_a, rows_b, cols_b, cols_a, corners_b, canvas):
    n = own.shape[-1]
    h = n // 2
    ra, rb, row_ok = ends(info, 0, 0, h + n)
    ca, cb, col_ok = ends(info, 1, 0, h + n)
    canvas[:, h : h + n, h : h + n] = own[:, layer]
    canvas[:, pl.ds(ra, h), h : h + n] = rows_a[...]
    canvas[:, pl.ds(rb, h), h : h + n] = kept(row_ok, rows_b[...])
    canvas[:, :, pl.ds(ca, h)] = cols_a[...]
    canvas[:, h : h + n, pl.ds(cb, h)] = kept(col_ok, cols_b[:, layer])
    canvas[:, pl.ds(ra, h), pl.ds(cb, h)] = kept(col_ok, corners_b[0])
    canvas[:, pl.ds(rb, h), pl.ds(cb, h)] = kept(row_ok & col_ok, corners_b[1])


def extract(off_ref, slot, canvas, patch):
    n = patch.shape[-1]
    h = n // 2
    top, block, row_rest, col_rest = place_of(off_ref, slot, h)
    row_shift = jnp.where(row_rest == 0, 0, n + 8 - row_rest)
    col_shift = jnp.where(col_rest == 0, 0, n + h - col_rest)
    for part in range(2):
        window = canvas[part, pl.ds(top, n + 8), pl.ds(block, n + h)]
        window = pltpu.roll(window, col_shift, 1)[:, :n]
        patch[part] = pltpu.roll(window, row_shift, 0)[:n]


def lay(off_ref, grads, canvas):
    n = grads[0].shape[-1]
    h = n // 2
    canvas[...] = jnp.zeros_like(canvas)
    for slot, grad in enumerate(grads):
        top, block, row_rest, col_rest = place_of(off_ref, slot, h)
        for part in range(canvas.shape[0]):
            tall = above(grad[part], jnp.zeros((8, n), F32))
            tall = pltpu.roll(tall, row_rest, 0)
            wide = beside(tall, jnp.zeros((n + 8, h), F32))
            canvas[part, pl.ds(top, n + 8), pl.ds(block, n + h)] += pltpu.roll(wide, col_rest, 1)


def times(a_re, a_im, b_re, b_im):
    return a_re * b_re - a_im * b_im, a_re * b_im + a_im * b_re


def by_mode(held, modes, left):
    n = held.shape[0] // modes
    rows = [slice(m * n, (m + 1) * n) for m in range(modes)]
    for m in range(modes):
        held[rows[m]] = left(m)
    return rows


def waves(probe, patch, diag, corner, right, wave, held):
    n = patch.shape[-1]

    def left(m):
        return prop_left(diag, corner, *times(probe[0, m], probe[1, m], patch[0], patch[1]))

    rows = by_mode(held, probe.shape[1], left)
    both = mm(held[...], right[...])
    for m, at in enumerate(rows):
        wave[m, 0] = both[at, :n]
        wave[m, 1] = both[at, n:]


def fars(wave, patch, tabs, far, inten, held):
    n = patch.shape[-1]
    h = n // 2

    def left(m):
        return dft_left(tabs, *times(wave[m, 0], wave[m, 1], patch[0], patch[1]))

    rows = by_mode(held, wave.shape[0], left)
    evens, odds = mm(held[:, :n], tabs[2]), mm(held[:, n:], tabs[3])
    total_e = total_o = 0.0
    for m, at in enumerate(rows):
        e, o = evens[at], odds[at]
        far[m, 0] = e
        far[m, 1] = o
        total_e += e * e
        total_o += o * o
    inten[...] = beside(total_e[:, :h] + total_e[:, h:], total_o[:, :h] + total_o[:, h:])


def waves_first_kernel(off, info, own, rows_a, rows_b, cols_b, cols_a, corners_b, probe,
                       diag, corner, mat, canvas, patch, wave, held):
    build_canvas(0, info, own, rows_a, rows_b, cols_b, cols_a, corners_b, canvas)
    extract(off, 0, canvas, patch)
    waves(probe, patch, diag, corner, mat, wave, held)


def waves_next_kernel(off, canvas, probe, diag, corner, mat, patch, wave, held):
    extract(off, 1, canvas, patch)
    waves(probe, patch, diag, corner, mat, wave, held)


def fars_first_kernel(off, info, own, rows_a, rows_b, cols_b, cols_a, corners_b, wave, tabs,
                      canvas, patch, far, inten, held):
    build_canvas(1, info, own, rows_a, rows_b, cols_b, cols_a, corners_b, canvas)
    extract(off, 0, canvas, patch)
    fars(wave, patch, tabs, far, inten, held)


def fars_next_kernel(off, canvas, wave, tabs, patch, far, inten, held):
    extract(off, 1, canvas, patch)
    fars(wave, patch, tabs, far, inten, held)


def back_last(slot, counts, mine, other, measured, far, wave, patch, tabs, grad, bar, resid, held):
    n = mine.shape[0]
    h = n // 2
    live = jnp.where(slot < counts[0], 2.0, 0.0).astype(F32)
    r = (mine[...] + other[...] - measured[slot]) * live
    resid[0] = beside(r[:, :h], r[:, :h])
    resid[1] = beside(r[:, h:], r[:, h:])
    rows = by_mode(
        held,
        far.shape[0],
        lambda m: conj_dft_left(tabs, resid[0] * far[m, 0], resid[1] * far[m, 1]),
    )
    evens, odds = mm(held[:, :n], tabs[0]), mm(held[:, n:], tabs[1])
    g_re = g_im = 0.0
    o_re, o_im = patch[0], patch[1]
    for m, at in enumerate(rows):
        e, o = evens[at], odds[at]
        b_re = beside(e[:, :h] + o[:, :h], e[:, :h] - o[:, :h])
        b_im = beside(e[:, h:] + o[:, h:], e[:, h:] - o[:, h:])
        w_re, w_im = wave[m, 0], wave[m, 1]
        g_re += w_re * b_re + w_im * b_im
        g_im += w_re * b_im - w_im * b_re
        bar[m, 0] = (o_re * b_re + o_im * b_im).astype(BF16)
        bar[m, 1] = (o_re * b_im - o_im * b_re).astype(BF16)
    grad[0] = g_re
    grad[1] = g_im


def back_last_place_kernel(slot, counts, off, info, before, mine, other, measured, far, wave, patch,
                           tabs, bar, out_a, out_c, out_b, resid, held, grad, canvas):
    back_last(
        slot, counts, mine, other, measured, far, wave, patch, tabs, grad, bar, resid, held
    )
    lay(off, (before, grad), canvas)
    n = grad.shape[-1]
    h = n // 2
    sides(info, canvas, out_a, out_b)
    out_c[...] = canvas[:, :, h : h + n]


def back_first_kernel(info, bar, probe, patch, diag, corner, mat, keep, send, part, grad, held):
    n = patch.shape[-1]
    rows = by_mode(
        held, probe.shape[1], lambda m: prop_left(diag, corner, bar[m, 0], bar[m, 1])
    )
    both = mm(held[...], mat[...])
    g_re = g_im = 0.0
    o_re, o_im = patch[0], patch[1]
    for m, at in enumerate(rows):
        b_re, b_im = both[at, :n], both[at, n:]
        p_re, p_im = probe[0, m], probe[1, m]
        g_re += p_re * b_re + p_im * b_im
        g_im += p_re * b_im - p_im * b_re
        part[0, m] = o_re * b_re + o_im * b_im
        part[1, m] = o_re * b_im - o_im * b_re
    grad[0] = g_re
    grad[1] = g_im
    mode = info[4]
    keep[0] = grad[mode]
    send[0] = grad[1 - mode]


def probe_sum_kernel(part0, part1, total):
    total[0] = part0[...] + part1[...]


def sides(info, canvas, out_a, out_b):
    h = out_a.shape[-1]
    a, b, _ = ends(info, 1, 0, 3 * h)
    out_a[...] = canvas[:, :, pl.ds(a, h)]
    out_b[...] = canvas[:, :, pl.ds(b, h)]


def lay_sums(off, parts, canvas, sums):
    for slot in range(2):
        sums[slot] = parts[2 * slot][...] + parts[2 * slot + 1][...]
    lay(off, (sums.at[0], sums.at[1]), canvas)


def place_sides_kernel(off, info, keep0, got0, keep1, got1, out_a, out_b, canvas, sums):
    lay_sums(off, (keep0, got0, keep1, got1), canvas, sums)
    sides(info, canvas, out_a, out_b)


def place_center_kernel(off, keep0, got0, keep1, got1, out_c, canvas, sums):
    lay_sums(off, (keep0, got0, keep1, got1), canvas, sums)
    h = keep0.shape[-1] // 2
    out_c[...] = canvas[:, :, h : 3 * h]


def fold_cols_kernel(info, center, got_a, got_b, out_a, mid, out_b):
    n = center.shape[-1]
    h = n // 2
    ca, cb, col_ok = ends(info, 1, 0, h)
    ra, rb, _ = ends(info, 0, 0, h + n)
    for a, out in ((ra, out_a), (rb, out_b)):
        out[:, :, pl.ds(ca, h)] = center[:, pl.ds(a, h), pl.ds(ca, h)] + got_a[:, pl.ds(a, h)]
        out[:, :, pl.ds(cb, h)] = center[:, pl.ds(a, h), pl.ds(cb, h)] + kept(
            col_ok, got_b[:, pl.ds(a, h)]
        )
    mid[:, :, pl.ds(ca, h)] = center[:, h : h + n, pl.ds(ca, h)] + got_a[:, h : h + n]
    mid[:, :, pl.ds(cb, h)] = center[:, h : h + n, pl.ds(cb, h)] + kept(
        col_ok, got_b[:, h : h + n]
    )


def fold_rows_kernel(info, mid, got_a, got_b, *outs):
    h = got_a.shape[1]
    ra, rb, row_ok = ends(info, 0, 0, h)
    for plane, out in enumerate(outs):
        out[0, pl.ds(ra, h)] = mid[plane, pl.ds(ra, h)] + got_a[plane]
        out[0, pl.ds(rb, h)] = mid[plane, pl.ds(rb, h)] + kept(row_ok, got_b[plane])


def finish_last_kernel(info, mine_first, mine_re, other_re, mine_im, other_im, out, sums, sems):
    sums[0] = mine_re[0] + other_re[0]
    sums[1] = mine_im[0] + other_im[0]
    moves = ((sums.at[0], out.at[0, 0, 1]), (sums.at[1], out.at[0, 1, 1]),
             (mine_first.at[0], out.at[0, info[4], 0]))
    copies = [pltpu.make_async_copy(a, b, sems.at[i]) for i, (a, b) in enumerate(moves)]
    for copy in copies:
        copy.start()
    for copy in copies:
        copy.wait()


def finish_kernel(info, other_first, partial, out, sems):
    copy = pltpu.make_async_copy(other_first.at[0], out.at[0, 1 - info[4], 0], sems.at[0])
    copy.start()
    copy.wait()


def pick_rows_kernel(info, own, *refs):
    *outs, sems = refs
    h = outs[0].shape[1]
    a, b, _ = ends(info, 0, 0, h)
    copies = []
    for layer in range(2):
        for i, start in enumerate((a, b)):
            k = 2 * layer + i
            copies.append(pltpu.make_async_copy(
                own.at[:, layer, pl.ds(start, h), :], outs[k], sems.at[k]))
    for copy in copies:
        copy.start()
    for copy in copies:
        copy.wait()


def pick_cols_kernel(info, own, out_b):
    h = out_b.shape[-1]
    _, b, _ = ends(info, 1, 0, h)
    out_b[...] = own[:, :, :, pl.ds(b, h)]


def pick_rest_kernel(layer, info, own, rows_a, rows_b, out_a, corners_b):
    n = own.shape[-1]
    h = n // 2
    ra, rb, row_ok = ends(info, 0, 0, h + n)
    a, b, _ = ends(info, 1, 0, h)
    a, b = pl.ds(a, h), pl.ds(b, h)
    out_a[:, h : h + n] = own[:, layer, :, a]
    out_a[:, pl.ds(ra, h)] = rows_a[:, :, a]
    out_a[:, pl.ds(rb, h)] = kept(row_ok, rows_b[:, :, a])
    corners_b[0] = rows_a[:, :, b]
    corners_b[1] = rows_b[:, :, b]


def prepare_kernel(prop_in, probe_in, tabs_in, diag, corner, right, back_diag, back_corner,
                   back_right, probe_out, tabs_out, prop, sems):
    copies = [
        pltpu.make_async_copy(prop_in, prop, sems.at[0]),
        pltpu.make_async_copy(probe_in, probe_out, sems.at[1]),
        pltpu.make_async_copy(tabs_in, tabs_out, sems.at[2]),
    ]
    for copy in copies:
        copy.start()
    copies[0].wait()
    re, im = prop[0].astype(F32), prop[1].astype(F32)
    re_t, im_t = re.T, im.T
    for out, edge, pair in ((diag, corner, (re, im)), (back_diag, back_corner, (re_t, -im_t))):
        blocks, corners = band_left(*pair)
        out[0] = blocks[0].astype(BF16)
        out[1] = blocks[1].astype(BF16)
        edge[...] = corners.astype(BF16)
    right[...] = right_form(re_t, im_t, jnp).astype(BF16)
    back_right[...] = right_form(re, -im, jnp).astype(BF16)
    copies[1].wait()
    copies[2].wait()


def reorder_kernel(measured, out):
    n = out.shape[-1]
    h = n // 2
    exact = functools.partial(
        jnp.dot, precision=lax.Precision.HIGHEST, preferred_element_type=F32
    )

    def order(to, of):
        a = lax.broadcasted_iota(jnp.int32, (n, n), to)
        b = lax.broadcasted_iota(jnp.int32, (n, n), of)
        return jnp.where(jnp.where(a < h, 2 * a, 2 * a - n + 1) == b, 1.0, 0.0).astype(F32)

    for slot in range(out.shape[0]):
        out[slot] = exact(exact(order(0, 1), measured[slot]), order(1, 0))


def swap(value, axis, second):
    count = lax.axis_size("tile")
    step, length = (GY, count // GY) if axis == 0 else (1, GY)
    pairs = []
    for i in range(count):
        at = i // step % length
        to = (at + (1 if (at % 2 == 1) == second else -1)) % length
        pairs.append((i, i + (to - at) * step))
    return lax.ppermute(value, "tile", pairs)


def swap_mode(value):
    return lax.ppermute(value, "mode", [(0, 1), (1, 0)])


def call(kernel, name, outs, args, scratch=(), smem=1, after=(), copies=0, out=None, alias=None):
    vmem = pl.BlockSpec(memory_space=pltpu.VMEM)
    held = pl.BlockSpec(memory_space=pltpu.HBM) if copies and out is None else vmem
    out = vmem if out is None else pl.BlockSpec(memory_space=out)
    scalars = pl.BlockSpec(memory_space=pltpu.SMEM)
    n_args, n_after = len(args), len(after)

    def run(*refs):
        kept_args = n_args if alias is None else n_args + n_after
        kernel(*refs[:kept_args], *refs[n_args + n_after :])

    return pl.pallas_call(
        run,
        out_shape=tuple(jax.ShapeDtypeStruct(shape, dtype) for shape, dtype in outs),
        in_specs=[scalars] * smem
        + [held] * (n_args - smem)
        + [pl.BlockSpec(memory_space=pl.ANY)] * n_after,
        out_specs=tuple(out for _ in outs),
        input_output_aliases={} if alias is None else {alias: 0},
        scratch_shapes=[pltpu.VMEM(shape, dtype) for shape, dtype in scratch]
        + [pltpu.SemaphoreType.DMA((copies,))] * (copies > 0),
        compiler_params=pltpu.CompilerParams(vmem_limit_bytes=VMEM_LIMIT),
        name=name,
    )(*args, *after)


def body(object_tiles, probe_modes, propagator, offsets, counts, measured):
    n = probe_modes.shape[-1]
    h = n // 2
    modes = probe_modes.shape[1]
    slots = measured.shape[1]
    own = object_tiles[0]
    off = offsets[0]

    tile = lax.axis_index("tile")
    row, col = tile // GY, tile % GY
    n_rows = lax.axis_size("tile") // GY
    odd_row, odd_col = row % 2 == 1, col % 2 == 1
    paired = [(row > 0) & (row < n_rows - 1), (col > 0) & (col < GY - 1)]
    info = jnp.stack([odd_row, odd_col, *paired, lax.axis_index("mode") == 1]).astype(jnp.int32)

    one, pair, mat = ((1, n, n), F32), ((2, n, n), F32), ((2 * n, 2 * n), BF16)
    plane, field, probes = ((n, n), F32), ((modes, 2, n, n), F32), ((2, modes, n, n), F32)
    band = (((2, n, n), BF16), ((4 * BAND, 4 * BAND), BF16), mat)
    held = ((modes * n, 2 * n), BF16)
    strip, tall = ((2, h, n), F32), ((2, 2 * n, h), F32)
    side_strip, quarter = ((2, 2, n, h), F32), ((2, 2, h, h), F32)

    picked = call(pick_rows_kernel, "pick_rows", (strip,) * 4, (info, own), copies=4)
    rows = [[swap(picked[2 * i + k], 0, k == 1) for k in range(2)] for i in range(2)]
    (picked,) = call(pick_cols_kernel, "pick_cols", (side_strip,), (info, own), after=())
    cols_b = swap(picked, 1, True)

    def beside_tiles(layer, after):
        picked = call(functools.partial(pick_rest_kernel, layer), f"pick_rest_{layer}",
                      (tall, quarter), (info, own, *rows[layer]), after=after)
        rest = [swap(picked[k], 1, k == 1) for k in range(2)]
        return (own, *rows[layer], cols_b, *rest, picked[0])

    first = beside_tiles(0, ())
    tabs = jnp.asarray(dft_tables(n))
    *made, probe, tabs = call(
        prepare_kernel,
        "prepare",
        band + band + (probes, (tabs.shape, BF16)),
        (propagator, probe_modes, tabs),
        scratch=(((2, n, n), BF16),),
        smem=0,
        copies=3,
        after=(first[6],),
    )
    prop, back_prop = made[:3], made[3:]
    last = beside_tiles(1, (probe, first[3], first[5]))
    canvas, patch_first0, wave0 = call(
        waves_first_kernel,
        "waves_0",
        (((2, 2 * n, 2 * n), F32), pair, field),
        (off, info, *first[:6], probe, *prop),
        scratch=(held,),
        smem=2,
        after=(),
    )
    patch_first1, wave1 = call(
        waves_next_kernel, "waves_1", (pair, field), (off, canvas, probe, *prop), scratch=(held,),
        after=()
    )
    canvas, patch_last0, far0, inten0 = call(
        fars_first_kernel,
        "fars_0",
        (((2, 2 * n, 2 * n), F32), pair, field, plane),
        (off, info, *last[:6], wave0, tabs),
        scratch=(held,),
        smem=2,
        after=(patch_first1,),
    )
    other0 = swap_mode(inten0)
    patch_last1, far1, inten1 = call(
        fars_next_kernel, "fars_1", (pair, field, plane), (off, canvas, wave1, tabs), scratch=(held,)
    )
    other1 = swap_mode(inten1)
    (measured,) = call(
        reorder_kernel,
        "reorder",
        (((slots, n, n), F32),),
        (measured[0],),
        smem=0,
        after=(),
    )

    bar_out = ((modes, 2, n, n), BF16)
    strips = (((2, 2 * n, h), F32), ((2, 2 * n, n), F32), ((2, 2 * n, h), F32))
    wide = ((2, 2 * n, 2 * n), F32)
    grad_last0, bar0 = call(
        functools.partial(back_last, 0),
        "back_last_0",
        (pair, bar_out),
        (counts, inten0, other0, measured, far0, wave0, patch_last0, tabs),
        scratch=(pair, held),
    )
    keep0, send0, part0 = call(
        back_first_kernel,
        "back_first_0",
        (one, one, probes),
        (info, bar0, probe, patch_first0, *back_prop),
        scratch=(pair, held),
    )
    got0 = swap_mode(send0)
    bar1, out_a, out_c, out_b = call(
        functools.partial(back_last_place_kernel, 1),
        "back_last_1",
        (bar_out,) + strips,
        (counts, off, info, grad_last0, inten1, other1, measured, far1, wave1, patch_last1, tabs),
        scratch=(pair, held, pair, wide),
        smem=3,
        after=(keep0,),
    )

    def fold_cols(name, out_a, out_c, out_b, after):
        got_a, got_b = swap(out_a, 1, False), swap(out_b, 1, True)
        planes = out_c.shape[0]
        half, mid = ((planes, h, n), F32), ((planes, n, n), F32)
        return call(fold_cols_kernel, name, (half, mid, half), (info, out_c, got_a, got_b),
                    after=after)

    def fold_rows(name, out_a, mid, out_b, after):
        got_a, got_b = swap(out_a, 0, False), swap(out_b, 0, True)
        return call(fold_rows_kernel, name, (one,) * mid.shape[0], (info, mid, got_a, got_b),
                    after=after)

    keep1, send1, part1 = call(
        back_first_kernel,
        "back_first_1",
        (one, one, probes),
        (info, bar1, probe, patch_first1, *back_prop),
        scratch=(pair, held),
    )
    got1 = swap_mode(send1)
    strips_last = fold_cols("cols_last", out_a, out_c, out_b, (keep1,))
    mine_re, mine_im = fold_rows("rows_last", *strips_last, ())
    other_re, other_im = swap_mode(mine_re), swap_mode(mine_im)
    strips = [((1,) + shape[1:], dtype) for shape, dtype in strips]
    wide = ((1, 2 * n, 2 * n), F32)
    parts = (keep0, got0, keep1, got1)
    out_a, out_b = call(
        place_sides_kernel,
        "place_sides",
        (strips[0], strips[2]),
        (off, info, *parts),
        scratch=(wide, ((2, 1, n, n), F32)),
        smem=2,
        after=(strips_last[0],),
    )
    (out_c,) = call(
        place_center_kernel,
        "place_center",
        (strips[1],),
        (off, *parts),
        scratch=(wide, ((2, 1, n, n), F32)),
        after=(out_a,),
    )
    strips_first = fold_cols("cols_first", out_a, out_c, out_b, ())
    (mine_first,) = fold_rows("rows_first", *strips_first, (other_re,))
    other_first = swap_mode(mine_first)
    (probe_grad,) = call(
        probe_sum_kernel,
        "probe_sum",
        (((1, 2, modes, n, n), F32),),
        (part0, part1),
        smem=0,
        after=(),
    )
    shape = ((object_tiles.shape, F32),)
    (partial,) = call(
        finish_last_kernel,
        "finish_last",
        shape,
        (info, mine_first, mine_re, other_re, mine_im, other_im),
        scratch=(pair,),
        copies=3,
        out=pl.ANY,
    )
    (object_grad,) = call(
        finish_kernel,
        "finish",
        shape,
        (info, other_first),
        after=(partial,),
        copies=1,
        out=pl.ANY,
        alias=2,
    )
    return (object_grad, probe_grad)


def solution(mesh):
    placed = (
        P("tile", None, None, None, None),
        P(None, "mode", None, None),
        P(),
        P("tile", None, None),
        P("tile"),
        P("tile", None, None, None),
    )
    return jax.shard_map(
        body,
        mesh=mesh,
        in_specs=placed,
        out_specs=(P("tile", None, None, None, None), P("tile", None, "mode", None, None)),
        check_vma=False,
    )
```

```python
import functools
import math

import jax
import jax.numpy as jnp
import ml_dtypes
import numpy as np
from jax import lax
from jax.experimental import pallas as pl
from jax.experimental.pallas import tpu as pltpu
from jax.sharding import PartitionSpec as P

GY = 8
BAND = 16
F32 = jnp.float32
BF16 = jnp.bfloat16
VMEM_LIMIT = 24 * 1024 * 1024


def dft_pair(extent):
    counter = np.arange(extent)
    angle = -2.0 * math.pi / extent * (counter[:, None] * counter[None, :] % extent)
    scale = 1.0 / math.sqrt(extent)
    return (
        (np.cos(angle) * scale).astype(ml_dtypes.bfloat16),
        (np.sin(angle) * scale).astype(ml_dtypes.bfloat16),
    )


def left_form(re, im, xp):
    return xp.concatenate(
        [xp.concatenate([re, -im], axis=1), xp.concatenate([im, re], axis=1)], axis=0
    )


def right_form(re, im, xp):
    return xp.concatenate(
        [xp.concatenate([re, im], axis=1), xp.concatenate([-im, re], axis=1)], axis=0
    )


def dft_tables(extent):
    re, im = dft_pair(extent)
    lefts = [left_form(re[b::2, : extent // 2], im[b::2, : extent // 2], np) for b in range(2)]
    return np.stack(lefts + [left.T for left in lefts])


def mm(a, b):
    return jnp.dot(a, b, preferred_element_type=F32)


def beside(a, b):
    return jnp.concatenate([a, b], axis=1)


def above(a, b):
    return jnp.concatenate([a, b], axis=0)


def band_left(re, im):
    n = re.shape[0]
    h, a, b = n // 2, n // 2 - BAND, n // 2 + BAND
    diag = [left_form(re[r, r], im[r, r], jnp) for r in (slice(0, h), slice(h, n))]
    row = lax.broadcasted_iota(jnp.int32, (2 * BAND, 2 * BAND), 0) < BAND
    col = lax.broadcasted_iota(jnp.int32, (2 * BAND, 2 * BAND), 1) < BAND
    corners = [jnp.where(row == col, 0.0, part[a:b, a:b]) for part in (re, im)]
    return diag, left_form(*corners, jnp)


def prop_left(diag, corner, re, im):
    n = re.shape[0]
    h, a, b = n // 2, n // 2 - BAND, n // 2 + BAND
    re, im = re.astype(BF16), im.astype(BF16)
    top = mm(diag[0], above(re[:h], im[:h]))
    low = mm(diag[1], above(re[h:], im[h:]))
    mid = mm(corner[...], above(re[a:b], im[a:b]))
    re = [top[:a], top[a:h] + mid[:BAND], low[:BAND] + mid[BAND : 2 * BAND], low[BAND:h]]
    mid, top, low = mid[2 * BAND :], top[h:], low[h:]
    im = [top[:a], top[a:h] + mid[:BAND], low[:BAND] + mid[BAND:], low[BAND:]]
    re, im = jnp.concatenate(re, axis=0), jnp.concatenate(im, axis=0)
    return beside(re.astype(BF16), im.astype(BF16))


def dft_left(tabs, re, im):
    h = re.shape[0] // 2
    even = mm(tabs[0], above(re[:h] + re[h:], im[:h] + im[h:]).astype(BF16))
    odd = mm(tabs[1], above(re[:h] - re[h:], im[:h] - im[h:]).astype(BF16))
    re, im = above(even[:h], odd[:h]), above(even[h:], odd[h:])
    e = beside(re[:, :h] + re[:, h:], im[:, :h] + im[:, h:])
    o = beside(re[:, :h] - re[:, h:], im[:, :h] - im[:, h:])
    return beside(e.astype(BF16), o.astype(BF16))


def conj_dft_left(tabs, e, o):
    h = e.shape[0] // 2
    e, o = e.astype(BF16), o.astype(BF16)
    even = mm(tabs[2], above(beside(e[:h, :h], o[:h, :h]), beside(e[:h, h:], o[:h, h:])))
    odd = mm(tabs[3], above(beside(e[h:, :h], o[h:, :h]), beside(e[h:, h:], o[h:, h:])))
    re = above(even[:h] + odd[:h], even[:h] - odd[:h]).astype(BF16)
    im = above(even[h:] + odd[h:], even[h:] - odd[h:]).astype(BF16)
    return beside(beside(re[:, :h], im[:, :h]), beside(re[:, h:], im[:, h:]))


def place_of(off_ref, slot, h):
    row = off_ref[slot, 0] + h
    col = off_ref[slot, 1] + h
    top = pl.multiple_of((row >> 3) * 8, 8)
    block = pl.multiple_of((col >> 7) * 128, 128)
    return top, block, row & 7, col & 127


def ends(info, axis, before, after):
    odd = info[axis]
    first = jnp.where(odd == 1, before, after)
    second = jnp.where(odd == 1, after, before)
    return pl.multiple_of(first, 128), pl.multiple_of(second, 128), info[2 + axis] == 1


def kept(good, value):
    return jnp.where(good, value, 0.0)


def build_canvas(layer, info, own, rows_a, rows_b, cols_b, cols_a, corners_b, canvas):
    n = own.shape[-1]
    h = n // 2
    ra, rb, row_ok = ends(info, 0, 0, h + n)
    ca, cb, col_ok = ends(info, 1, 0, h + n)
    canvas[:, h : h + n, h : h + n] = own[:, layer]
    canvas[:, pl.ds(ra, h), h : h + n] = rows_a[...]
    canvas[:, pl.ds(rb, h), h : h + n] = kept(row_ok, rows_b[...])
    canvas[:, :, pl.ds(ca, h)] = cols_a[...]
    canvas[:, h : h + n, pl.ds(cb, h)] = kept(col_ok, cols_b[:, layer])
    canvas[:, pl.ds(ra, h), pl.ds(cb, h)] = kept(col_ok, corners_b[0])
    canvas[:, pl.ds(rb, h), pl.ds(cb, h)] = kept(row_ok & col_ok, corners_b[1])


def extract(off_ref, slot, canvas, patch):
    n = patch.shape[-1]
    h = n // 2
    top, block, row_rest, col_rest = place_of(off_ref, slot, h)
    row_shift = jnp.where(row_rest == 0, 0, n + 8 - row_rest)
    col_shift = jnp.where(col_rest == 0, 0, n + h - col_rest)
    for part in range(2):
        window = canvas[part, pl.ds(top, n + 8), pl.ds(block, n + h)]
        window = pltpu.roll(window, col_shift, 1)[:, :n]
        patch[part] = pltpu.roll(window, row_shift, 0)[:n]


def lay(off_ref, grads, canvas):
    n = grads[0].shape[-1]
    h = n // 2
    canvas[...] = jnp.zeros_like(canvas)
    for slot, grad in enumerate(grads):
        top, block, row_rest, col_rest = place_of(off_ref, slot, h)
        for part in range(canvas.shape[0]):
            tall = above(grad[part], jnp.zeros((8, n), F32))
            tall = pltpu.roll(tall, row_rest, 0)
            wide = beside(tall, jnp.zeros((n + 8, h), F32))
            canvas[part, pl.ds(top, n + 8), pl.ds(block, n + h)] += pltpu.roll(wide, col_rest, 1)


def times(a_re, a_im, b_re, b_im):
    return a_re * b_re - a_im * b_im, a_re * b_im + a_im * b_re


def by_mode(held, modes, left):
    n = held.shape[0] // modes
    rows = [slice(m * n, (m + 1) * n) for m in range(modes)]
    for m in range(modes):
        held[rows[m]] = left(m)
    return rows


def waves(probe, patch, diag, corner, right, wave, held):
    n = patch.shape[-1]

    def left(m):
        return prop_left(diag, corner, *times(probe[0, m], probe[1, m], patch[0], patch[1]))

    rows = by_mode(held, probe.shape[1], left)
    both = mm(held[...], right[...])
    for m, at in enumerate(rows):
        wave[m, 0] = both[at, :n]
        wave[m, 1] = both[at, n:]


def fars(wave, patch, tabs, far, inten, held):
    n = patch.shape[-1]
    h = n // 2

    def left(m):
        return dft_left(tabs, *times(wave[m, 0], wave[m, 1], patch[0], patch[1]))

    rows = by_mode(held, wave.shape[0], left)
    evens, odds = mm(held[:, :n], tabs[2]), mm(held[:, n:], tabs[3])
    total_e = total_o = 0.0
    for m, at in enumerate(rows):
        e, o = evens[at], odds[at]
        far[m, 0] = e
        far[m, 1] = o
        total_e += e * e
        total_o += o * o
    inten[...] = beside(total_e[:, :h] + total_e[:, h:], total_o[:, :h] + total_o[:, h:])


def waves_first_kernel(off, info, own, rows_a, rows_b, cols_b, cols_a, corners_b, probe,
                       diag, corner, mat, canvas, patch, wave, held):
    build_canvas(0, info, own, rows_a, rows_b, cols_b, cols_a, corners_b, canvas)
    extract(off, 0, canvas, patch)
    waves(probe, patch, diag, corner, mat, wave, held)


def waves_next_kernel(off, canvas, probe, diag, corner, mat, patch, wave, held):
    extract(off, 1, canvas, patch)
    waves(probe, patch, diag, corner, mat, wave, held)


def fars_first_kernel(off, info, own, rows_a, rows_b, cols_b, cols_a, corners_b, wave, tabs,
                      canvas, patch, far, inten, held):
    build_canvas(1, info, own, rows_a, rows_b, cols_b, cols_a, corners_b, canvas)
    extract(off, 0, canvas, patch)
    fars(wave, patch, tabs, far, inten, held)


def fars_next_kernel(off, canvas, wave, tabs, patch, far, inten, held):
    extract(off, 1, canvas, patch)
    fars(wave, patch, tabs, far, inten, held)


def back_last(slot, counts, mine, other, measured, far, wave, patch, tabs, grad, bar, resid, held):
    n = mine.shape[0]
    h = n // 2
    live = jnp.where(slot < counts[0], 2.0, 0.0).astype(F32)
    r = (mine[...] + other[...] - measured[slot]) * live
    resid[0] = beside(r[:, :h], r[:, :h])
    resid[1] = beside(r[:, h:], r[:, h:])
    rows = by_mode(
        held,
        far.shape[0],
        lambda m: conj_dft_left(tabs, resid[0] * far[m, 0], resid[1] * far[m, 1]),
    )
    evens, odds = mm(held[:, :n], tabs[0]), mm(held[:, n:], tabs[1])
    g_re = g_im = 0.0
    o_re, o_im = patch[0], patch[1]
    for m, at in enumerate(rows):
        e, o = evens[at], odds[at]
        b_re = beside(e[:, :h] + o[:, :h], e[:, :h] - o[:, :h])
        b_im = beside(e[:, h:] + o[:, h:], e[:, h:] - o[:, h:])
        w_re, w_im = wave[m, 0], wave[m, 1]
        g_re += w_re * b_re + w_im * b_im
        g_im += w_re * b_im - w_im * b_re
        bar[m, 0] = (o_re * b_re + o_im * b_im).astype(BF16)
        bar[m, 1] = (o_re * b_im - o_im * b_re).astype(BF16)
    grad[0] = g_re
    grad[1] = g_im


def back_last_place_kernel(slot, counts, off, info, before, mine, other, measured, far, wave, patch,
                           tabs, bar, out_a, out_c, out_b, resid, held, grad, canvas):
    back_last(
        slot, counts, mine, other, measured, far, wave, patch, tabs, grad, bar, resid, held
    )
    lay(off, (before, grad), canvas)
    n = grad.shape[-1]
    h = n // 2
    sides(info, canvas, out_a, out_b)
    out_c[...] = canvas[:, :, h : h + n]


def back_first_kernel(info, bar, probe, patch, diag, corner, mat, keep, send, part, grad, held):
    n = patch.shape[-1]
    rows = by_mode(
        held, probe.shape[1], lambda m: prop_left(diag, corner, bar[m, 0], bar[m, 1])
    )
    both = mm(held[...], mat[...])
    g_re = g_im = 0.0
    o_re, o_im = patch[0], patch[1]
    for m, at in enumerate(rows):
        b_re, b_im = both[at, :n], both[at, n:]
        p_re, p_im = probe[0, m], probe[1, m]
        g_re += p_re * b_re + p_im * b_im
        g_im += p_re * b_im - p_im * b_re
        part[0, m] = o_re * b_re + o_im * b_im
        part[1, m] = o_re * b_im - o_im * b_re
    grad[0] = g_re
    grad[1] = g_im
    mode = info[4]
    keep[0] = grad[mode]
    send[0] = grad[1 - mode]


def probe_sum_kernel(part0, part1, total):
    total[0] = part0[...] + part1[...]


def sides(info, canvas, out_a, out_b):
    h = out_a.shape[-1]
    a, b, _ = ends(info, 1, 0, 3 * h)
    out_a[...] = canvas[:, :, pl.ds(a, h)]
    out_b[...] = canvas[:, :, pl.ds(b, h)]


def lay_sums(off, parts, canvas, sums):
    for slot in range(2):
        sums[slot] = parts[2 * slot][...] + parts[2 * slot + 1][...]
    lay(off, (sums.at[0], sums.at[1]), canvas)


def place_sides_kernel(off, info, keep0, got0, keep1, got1, out_a, out_b, canvas, sums):
    lay_sums(off, (keep0, got0, keep1, got1), canvas, sums)
    sides(info, canvas, out_a, out_b)


def place_center_kernel(off, keep0, got0, keep1, got1, out_c, canvas, sums):
    lay_sums(off, (keep0, got0, keep1, got1), canvas, sums)
    h = keep0.shape[-1] // 2
    out_c[...] = canvas[:, :, h : 3 * h]


def fold_cols_kernel(info, center, got_a, got_b, out_a, mid, out_b):
    n = center.shape[-1]
    h = n // 2
    ca, cb, col_ok = ends(info, 1, 0, h)
    ra, rb, _ = ends(info, 0, 0, h + n)
    for a, out in ((ra, out_a), (rb, out_b)):
        out[:, :, pl.ds(ca, h)] = center[:, pl.ds(a, h), pl.ds(ca, h)] + got_a[:, pl.ds(a, h)]
        out[:, :, pl.ds(cb, h)] = center[:, pl.ds(a, h), pl.ds(cb, h)] + kept(
            col_ok, got_b[:, pl.ds(a, h)]
        )
    mid[:, :, pl.ds(ca, h)] = center[:, h : h + n, pl.ds(ca, h)] + got_a[:, h : h + n]
    mid[:, :, pl.ds(cb, h)] = center[:, h : h + n, pl.ds(cb, h)] + kept(
        col_ok, got_b[:, h : h + n]
    )


def fold_rows_kernel(info, mid, got_a, got_b, *outs):
    h = got_a.shape[1]
    ra, rb, row_ok = ends(info, 0, 0, h)
    for plane, out in enumerate(outs):
        out[0, pl.ds(ra, h)] = mid[plane, pl.ds(ra, h)] + got_a[plane]
        out[0, pl.ds(rb, h)] = mid[plane, pl.ds(rb, h)] + kept(row_ok, got_b[plane])


def finish_last_kernel(info, mine_first, mine_re, other_re, mine_im, other_im, out, sums, sems):
    sums[0] = mine_re[0] + other_re[0]
    sums[1] = mine_im[0] + other_im[0]
    moves = ((sums.at[0], out.at[0, 0, 1]), (sums.at[1], out.at[0, 1, 1]),
             (mine_first.at[0], out.at[0, info[4], 0]))
    copies = [pltpu.make_async_copy(a, b, sems.at[i]) for i, (a, b) in enumerate(moves)]
    for copy in copies:
        copy.start()
    for copy in copies:
        copy.wait()


def pick_rows_kernel(info, own, *refs):
    *outs, sems = refs
    h = outs[0].shape[1]
    a, b, _ = ends(info, 0, 0, h)
    copies = []
    for layer in range(2):
        for i, start in enumerate((a, b)):
            k = 2 * layer + i
            copies.append(pltpu.make_async_copy(
                own.at[:, layer, pl.ds(start, h), :], outs[k], sems.at[k]))
    for copy in copies:
        copy.start()
    for copy in copies:
        copy.wait()


def pick_cols_kernel(info, own, out_b):
    h = out_b.shape[-1]
    _, b, _ = ends(info, 1, 0, h)
    out_b[...] = own[:, :, :, pl.ds(b, h)]


def pick_rest_kernel(layer, info, own, rows_a, rows_b, out_a, corners_b):
    n = own.shape[-1]
    h = n // 2
    ra, rb, row_ok = ends(info, 0, 0, h + n)
    a, b, _ = ends(info, 1, 0, h)
    a, b = pl.ds(a, h), pl.ds(b, h)
    out_a[:, h : h + n] = own[:, layer, :, a]
    out_a[:, pl.ds(ra, h)] = rows_a[:, :, a]
    out_a[:, pl.ds(rb, h)] = kept(row_ok, rows_b[:, :, a])
    corners_b[0] = rows_a[:, :, b]
    corners_b[1] = rows_b[:, :, b]


def prepare_kernel(prop_in, probe_in, tabs_in, diag, corner, right, back_diag, back_corner,
                   back_right, probe_out, tabs_out, prop, sems):
    copies = [
        pltpu.make_async_copy(prop_in, prop, sems.at[0]),
        pltpu.make_async_copy(probe_in, probe_out, sems.at[1]),
        pltpu.make_async_copy(tabs_in, tabs_out, sems.at[2]),
    ]
    for copy in copies:
        copy.start()
    copies[0].wait()
    re, im = prop[0].astype(F32), prop[1].astype(F32)
    re_t, im_t = re.T, im.T
    for out, edge, pair in ((diag, corner, (re, im)), (back_diag, back_corner, (re_t, -im_t))):
        blocks, corners = band_left(*pair)
        out[0] = blocks[0].astype(BF16)
        out[1] = blocks[1].astype(BF16)
        edge[...] = corners.astype(BF16)
    right[...] = right_form(re_t, im_t, jnp).astype(BF16)
    back_right[...] = right_form(re, -im, jnp).astype(BF16)
    copies[1].wait()
    copies[2].wait()


def reorder_kernel(measured, out):
    n = out.shape[-1]
    h = n // 2
    exact = functools.partial(
        jnp.dot, precision=lax.Precision.HIGHEST, preferred_element_type=F32
    )

    def order(to, of):
        a = lax.broadcasted_iota(jnp.int32, (n, n), to)
        b = lax.broadcasted_iota(jnp.int32, (n, n), of)
        return jnp.where(jnp.where(a < h, 2 * a, 2 * a - n + 1) == b, 1.0, 0.0).astype(F32)

    for slot in range(out.shape[0]):
        out[slot] = exact(exact(order(0, 1), measured[slot]), order(1, 0))


def swap(value, axis, second):
    count = lax.axis_size("tile")
    step, length = (GY, count // GY) if axis == 0 else (1, GY)
    pairs = []
    for i in range(count):
        at = i // step % length
        to = (at + (1 if (at % 2 == 1) == second else -1)) % length
        pairs.append((i, i + (to - at) * step))
    return lax.ppermute(value, "tile", pairs)


def swap_mode(value):
    return lax.ppermute(value, "mode", [(0, 1), (1, 0)])


def call(kernel, name, outs, args, scratch=(), smem=1, after=(), copies=0, out=None, alias=None):
    vmem = pl.BlockSpec(memory_space=pltpu.VMEM)
    held = pl.BlockSpec(memory_space=pltpu.HBM) if copies and out is None else vmem
    out = vmem if out is None else pl.BlockSpec(memory_space=out)
    scalars = pl.BlockSpec(memory_space=pltpu.SMEM)
    n_args, n_after = len(args), len(after)

    def run(*refs):
        kept_args = n_args if alias is None else n_args + n_after
        kernel(*refs[:kept_args], *refs[n_args + n_after :])

    return pl.pallas_call(
        run,
        out_shape=tuple(jax.ShapeDtypeStruct(shape, dtype) for shape, dtype in outs),
        in_specs=[scalars] * smem
        + [held] * (n_args - smem)
        + [pl.BlockSpec(memory_space=pl.ANY)] * n_after,
        out_specs=tuple(out for _ in outs),
        input_output_aliases={} if alias is None else {alias: 0},
        scratch_shapes=[pltpu.VMEM(shape, dtype) for shape, dtype in scratch]
        + [pltpu.SemaphoreType.DMA((copies,))] * (copies > 0),
        compiler_params=pltpu.CompilerParams(vmem_limit_bytes=VMEM_LIMIT),
        name=name,
    )(*args, *after)


def body(object_tiles, probe_modes, propagator, offsets, counts, measured):
    n = probe_modes.shape[-1]
    h = n // 2
    modes = probe_modes.shape[1]
    slots = measured.shape[1]
    own = object_tiles[0]
    off = offsets[0]

    tile = lax.axis_index("tile")
    row, col = tile // GY, tile % GY
    n_rows = lax.axis_size("tile") // GY
    odd_row, odd_col = row % 2 == 1, col % 2 == 1
    paired = [(row > 0) & (row < n_rows - 1), (col > 0) & (col < GY - 1)]
    info = jnp.stack([odd_row, odd_col, *paired, lax.axis_index("mode") == 1]).astype(jnp.int32)

    one, pair, mat = ((1, n, n), F32), ((2, n, n), F32), ((2 * n, 2 * n), BF16)
    plane, field, probes = ((n, n), F32), ((modes, 2, n, n), F32), ((2, modes, n, n), F32)
    band = (((2, n, n), BF16), ((4 * BAND, 4 * BAND), BF16), mat)
    held = ((modes * n, 2 * n), BF16)
    strip, tall = ((2, h, n), F32), ((2, 2 * n, h), F32)
    side_strip, quarter = ((2, 2, n, h), F32), ((2, 2, h, h), F32)

    picked = call(pick_rows_kernel, "pick_rows", (strip,) * 4, (info, own), copies=4)
    rows = [[swap(picked[2 * i + k], 0, k == 1) for k in range(2)] for i in range(2)]
    (picked,) = call(pick_cols_kernel, "pick_cols", (side_strip,), (info, own), after=())
    cols_b = swap(picked, 1, True)

    def beside_tiles(layer, after):
        picked = call(functools.partial(pick_rest_kernel, layer), f"pick_rest_{layer}",
                      (tall, quarter), (info, own, *rows[layer]), after=after)
        rest = [swap(picked[k], 1, k == 1) for k in range(2)]
        return (own, *rows[layer], cols_b, *rest, picked[0])

    first = beside_tiles(0, ())
    tabs = jnp.asarray(dft_tables(n))
    *made, probe, tabs = call(
        prepare_kernel,
        "prepare",
        band + band + (probes, (tabs.shape, BF16)),
        (propagator, probe_modes, tabs),
        scratch=(((2, n, n), BF16),),
        smem=0,
        copies=3,
        after=(first[6],),
    )
    prop, back_prop = made[:3], made[3:]
    last = beside_tiles(1, (probe, first[3], first[5]))
    canvas, patch_first0, wave0 = call(
        waves_first_kernel,
        "waves_0",
        (((2, 2 * n, 2 * n), F32), pair, field),
        (off, info, *first[:6], probe, *prop),
        scratch=(held,),
        smem=2,
        after=(),
    )
    patch_first1, wave1 = call(
        waves_next_kernel, "waves_1", (pair, field), (off, canvas, probe, *prop), scratch=(held,),
        after=()
    )
    canvas, patch_last0, far0, inten0 = call(
        fars_first_kernel,
        "fars_0",
        (((2, 2 * n, 2 * n), F32), pair, field, plane),
        (off, info, *last[:6], wave0, tabs),
        scratch=(held,),
        smem=2,
        after=(patch_first1,),
    )
    other0 = swap_mode(inten0)
    patch_last1, far1, inten1 = call(
        fars_next_kernel, "fars_1", (pair, field, plane), (off, canvas, wave1, tabs), scratch=(held,)
    )
    other1 = swap_mode(inten1)
    (measured,) = call(
        reorder_kernel,
        "reorder",
        (((slots, n, n), F32),),
        (measured[0],),
        smem=0,
        after=(),
    )

    bar_out = ((modes, 2, n, n), BF16)
    strips = (((2, 2 * n, h), F32), ((2, 2 * n, n), F32), ((2, 2 * n, h), F32))
    wide = ((2, 2 * n, 2 * n), F32)
    grad_last0, bar0 = call(
        functools.partial(back_last, 0),
        "back_last_0",
        (pair, bar_out),
        (counts, inten0, other0, measured, far0, wave0, patch_last0, tabs),
        scratch=(pair, held),
    )
    keep0, send0, part0 = call(
        back_first_kernel,
        "back_first_0",
        (one, one, probes),
        (info, bar0, probe, patch_first0, *back_prop),
        scratch=(pair, held),
    )
    got0 = swap_mode(send0)
    bar1, out_a, out_c, out_b = call(
        functools.partial(back_last_place_kernel, 1),
        "back_last_1",
        (bar_out,) + strips,
        (counts, off, info, grad_last0, inten1, other1, measured, far1, wave1, patch_last1, tabs),
        scratch=(pair, held, pair, wide),
        smem=3,
        after=(keep0,),
    )

    def fold_cols(name, out_a, out_c, out_b, after):
        got_a, got_b = swap(out_a, 1, False), swap(out_b, 1, True)
        planes = out_c.shape[0]
        half, mid = ((planes, h, n), F32), ((planes, n, n), F32)
        return call(fold_cols_kernel, name, (half, mid, half), (info, out_c, got_a, got_b),
                    after=after)

    def fold_rows(name, out_a, mid, out_b, after):
        got_a, got_b = swap(out_a, 0, False), swap(out_b, 0, True)
        return call(fold_rows_kernel, name, (one,) * mid.shape[0], (info, mid, got_a, got_b),
                    after=after)

    keep1, send1, part1 = call(
        back_first_kernel,
        "back_first_1",
        (one, one, probes),
        (info, bar1, probe, patch_first1, *back_prop),
        scratch=(pair, held),
    )
    got1 = swap_mode(send1)
    strips_last = fold_cols("cols_last", out_a, out_c, out_b, (keep1,))
    mine_re, mine_im = fold_rows("rows_last", *strips_last, ())
    other_re, other_im = swap_mode(mine_re), swap_mode(mine_im)
    strips = [((1,) + shape[1:], dtype) for shape, dtype in strips]
    wide = ((1, 2 * n, 2 * n), F32)
    parts = (keep0, got0, keep1, got1)
    out_a, out_b = call(
        place_sides_kernel,
        "place_sides",
        (strips[0], strips[2]),
        (off, info, *parts),
        scratch=(wide, ((2, 1, n, n), F32)),
        smem=2,
        after=(strips_last[0],),
    )
    (out_c,) = call(
        place_center_kernel,
        "place_center",
        (strips[1],),
        (off, *parts),
        scratch=(wide, ((2, 1, n, n), F32)),
        after=(out_a,),
    )
    strips_first = fold_cols("cols_first", out_a, out_c, out_b, ())
    (mine_first,) = fold_rows("rows_first", *strips_first, (other_re,))
    other_first = swap_mode(mine_first)
    (probe_grad,) = call(
        probe_sum_kernel,
        "probe_sum",
        (((1, 2, modes, n, n), F32),),
        (part0, part1),
        smem=0,
        after=(),
    )
    shape = ((object_tiles.shape, F32),)
    (partial,) = call(
        finish_last_kernel,
        "finish_last",
        shape,
        (info, mine_first, mine_re, other_re, mine_im, other_im),
        scratch=(pair,),
        copies=3,
        out=pl.ANY,
    )
    object_grad = lax.dynamic_update_slice(
        partial, other_first[:, None, None], (0, 1 - lax.axis_index("mode"), 0, 0, 0)
    )
    return (object_grad, probe_grad)


def solution(mesh):
    placed = (
        P("tile", None, None, None, None),
        P(None, "mode", None, None),
        P(),
        P("tile", None, None),
        P("tile"),
        P("tile", None, None, None),
    )
    return jax.shard_map(
        body,
        mesh=mesh,
        in_specs=placed,
        out_specs=(P("tile", None, None, None, None), P("tile", None, "mode", None, None)),
        check_vma=False,
    )
```

```python
import functools
import math

import jax
import jax.numpy as jnp
import ml_dtypes
import numpy as np
from jax import lax
from jax.experimental import pallas as pl
from jax.experimental.pallas import tpu as pltpu
from jax.sharding import PartitionSpec as P

GY = 8
BAND = 16
F32 = jnp.float32
BF16 = jnp.bfloat16
VMEM_LIMIT = 24 * 1024 * 1024


def dft_pair(extent):
    counter = np.arange(extent)
    angle = -2.0 * math.pi / extent * (counter[:, None] * counter[None, :] % extent)
    scale = 1.0 / math.sqrt(extent)
    return (
        (np.cos(angle) * scale).astype(ml_dtypes.bfloat16),
        (np.sin(angle) * scale).astype(ml_dtypes.bfloat16),
    )


def left_form(re, im, xp):
    return xp.concatenate(
        [xp.concatenate([re, -im], axis=1), xp.concatenate([im, re], axis=1)], axis=0
    )


def right_form(re, im, xp):
    return xp.concatenate(
        [xp.concatenate([re, im], axis=1), xp.concatenate([-im, re], axis=1)], axis=0
    )


def dft_tables(extent):
    re, im = dft_pair(extent)
    lefts = [left_form(re[b::2, : extent // 2], im[b::2, : extent // 2], np) for b in range(2)]
    return np.stack(lefts + [left.T for left in lefts])


def mm(a, b):
    return jnp.dot(a, b, preferred_element_type=F32)


def beside(a, b):
    return jnp.concatenate([a, b], axis=1)


def above(a, b):
    return jnp.concatenate([a, b], axis=0)


def band_left(re, im):
    n = re.shape[0]
    h, a, b = n // 2, n // 2 - BAND, n // 2 + BAND
    diag = [left_form(re[r, r], im[r, r], jnp) for r in (slice(0, h), slice(h, n))]
    row = lax.broadcasted_iota(jnp.int32, (2 * BAND, 2 * BAND), 0) < BAND
    col = lax.broadcasted_iota(jnp.int32, (2 * BAND, 2 * BAND), 1) < BAND
    corners = [jnp.where(row == col, 0.0, part[a:b, a:b]) for part in (re, im)]
    return diag, left_form(*corners, jnp)


def prop_left(diag, corner, re, im):
    n = re.shape[0]
    h, a, b = n // 2, n // 2 - BAND, n // 2 + BAND
    re, im = re.astype(BF16), im.astype(BF16)
    top = mm(diag[0], above(re[:h], im[:h]))
    low = mm(diag[1], above(re[h:], im[h:]))
    mid = mm(corner[...], above(re[a:b], im[a:b]))
    re = [top[:a], top[a:h] + mid[:BAND], low[:BAND] + mid[BAND : 2 * BAND], low[BAND:h]]
    mid, top, low = mid[2 * BAND :], top[h:], low[h:]
    im = [top[:a], top[a:h] + mid[:BAND], low[:BAND] + mid[BAND:], low[BAND:]]
    re, im = jnp.concatenate(re, axis=0), jnp.concatenate(im, axis=0)
    return beside(re.astype(BF16), im.astype(BF16))


def dft_left(tabs, re, im):
    h = re.shape[0] // 2
    even = mm(tabs[0], above(re[:h] + re[h:], im[:h] + im[h:]).astype(BF16))
    odd = mm(tabs[1], above(re[:h] - re[h:], im[:h] - im[h:]).astype(BF16))
    re, im = above(even[:h], odd[:h]), above(even[h:], odd[h:])
    e = beside(re[:, :h] + re[:, h:], im[:, :h] + im[:, h:])
    o = beside(re[:, :h] - re[:, h:], im[:, :h] - im[:, h:])
    return beside(e.astype(BF16), o.astype(BF16))


def conj_dft_left(tabs, e, o):
    h = e.shape[0] // 2
    e, o = e.astype(BF16), o.astype(BF16)
    even = mm(tabs[2], above(beside(e[:h, :h], o[:h, :h]), beside(e[:h, h:], o[:h, h:])))
    odd = mm(tabs[3], above(beside(e[h:, :h], o[h:, :h]), beside(e[h:, h:], o[h:, h:])))
    re = above(even[:h] + odd[:h], even[:h] - odd[:h]).astype(BF16)
    im = above(even[h:] + odd[h:], even[h:] - odd[h:]).astype(BF16)
    return beside(beside(re[:, :h], im[:, :h]), beside(re[:, h:], im[:, h:]))


def place_of(off_ref, slot, h):
    row = off_ref[slot, 0] + h
    col = off_ref[slot, 1] + h
    top = pl.multiple_of((row >> 3) * 8, 8)
    block = pl.multiple_of((col >> 7) * 128, 128)
    return top, block, row & 7, col & 127


def ends(info, axis, before, after):
    odd = info[axis]
    first = jnp.where(odd == 1, before, after)
    second = jnp.where(odd == 1, after, before)
    return pl.multiple_of(first, 128), pl.multiple_of(second, 128), info[2 + axis] == 1


def kept(good, value):
    return jnp.where(good, value, 0.0)


def build_canvas(layer, info, own, rows_a, rows_b, cols_b, cols_a, corners_b, canvas):
    n = own.shape[-1]
    h = n // 2
    ra, rb, row_ok = ends(info, 0, 0, h + n)
    ca, cb, col_ok = ends(info, 1, 0, h + n)
    canvas[:, h : h + n, h : h + n] = own[:, layer]
    canvas[:, pl.ds(ra, h), h : h + n] = rows_a[...]
    canvas[:, pl.ds(rb, h), h : h + n] = kept(row_ok, rows_b[...])
    canvas[:, :, pl.ds(ca, h)] = cols_a[...]
    canvas[:, h : h + n, pl.ds(cb, h)] = kept(col_ok, cols_b[:, layer])
    canvas[:, pl.ds(ra, h), pl.ds(cb, h)] = kept(col_ok, corners_b[0])
    canvas[:, pl.ds(rb, h), pl.ds(cb, h)] = kept(row_ok & col_ok, corners_b[1])


def extract(off_ref, slot, canvas, patch):
    n = patch.shape[-1]
    h = n // 2
    top, block, row_rest, col_rest = place_of(off_ref, slot, h)
    row_shift = jnp.where(row_rest == 0, 0, n + 8 - row_rest)
    col_shift = jnp.where(col_rest == 0, 0, n + h - col_rest)
    for part in range(2):
        window = canvas[part, pl.ds(top, n + 8), pl.ds(block, n + h)]
        window = pltpu.roll(window, col_shift, 1)[:, :n]
        patch[part] = pltpu.roll(window, row_shift, 0)[:n]


def lay(off_ref, grads, canvas):
    n = grads[0].shape[-1]
    h = n // 2
    canvas[...] = jnp.zeros_like(canvas)
    for slot, grad in enumerate(grads):
        top, block, row_rest, col_rest = place_of(off_ref, slot, h)
        for part in range(canvas.shape[0]):
            tall = above(grad[part], jnp.zeros((8, n), F32))
            tall = pltpu.roll(tall, row_rest, 0)
            wide = beside(tall, jnp.zeros((n + 8, h), F32))
            canvas[part, pl.ds(top, n + 8), pl.ds(block, n + h)] += pltpu.roll(wide, col_rest, 1)


def times(a_re, a_im, b_re, b_im):
    return a_re * b_re - a_im * b_im, a_re * b_im + a_im * b_re


def by_mode(held, modes, left):
    n = held.shape[0] // modes
    rows = [slice(m * n, (m + 1) * n) for m in range(modes)]
    for m in range(modes):
        held[rows[m]] = left(m)
    return rows


def waves(probe, patch, diag, corner, right, wave, held):
    n = patch.shape[-1]

    def left(m):
        return prop_left(diag, corner, *times(probe[0, m], probe[1, m], patch[0], patch[1]))

    rows = by_mode(held, probe.shape[1], left)
    both = mm(held[...], right[...])
    for m, at in enumerate(rows):
        wave[m, 0] = both[at, :n]
        wave[m, 1] = both[at, n:]


def fars(wave, patch, tabs, far, inten, held):
    n = patch.shape[-1]
    h = n // 2

    def left(m):
        return dft_left(tabs, *times(wave[m, 0], wave[m, 1], patch[0], patch[1]))

    rows = by_mode(held, wave.shape[0], left)
    evens, odds = mm(held[:, :n], tabs[2]), mm(held[:, n:], tabs[3])
    total_e = total_o = 0.0
    for m, at in enumerate(rows):
        e, o = evens[at], odds[at]
        far[m, 0] = e
        far[m, 1] = o
        total_e += e * e
        total_o += o * o
    inten[...] = beside(total_e[:, :h] + total_e[:, h:], total_o[:, :h] + total_o[:, h:])


def waves_first_kernel(off, info, own, rows_a, rows_b, cols_b, cols_a, corners_b, probe,
                       diag, corner, mat, canvas, patch, wave, held):
    build_canvas(0, info, own, rows_a, rows_b, cols_b, cols_a, corners_b, canvas)
    extract(off, 0, canvas, patch)
    waves(probe, patch, diag, corner, mat, wave, held)


def waves_next_kernel(off, canvas, probe, diag, corner, mat, patch, wave, held):
    extract(off, 1, canvas, patch)
    waves(probe, patch, diag, corner, mat, wave, held)


def fars_first_kernel(off, info, own, rows_a, rows_b, cols_b, cols_a, corners_b, wave, tabs,
                      canvas, patch, far, inten, held):
    build_canvas(1, info, own, rows_a, rows_b, cols_b, cols_a, corners_b, canvas)
    extract(off, 0, canvas, patch)
    fars(wave, patch, tabs, far, inten, held)


def fars_next_kernel(off, canvas, wave, tabs, patch, far, inten, held):
    extract(off, 1, canvas, patch)
    fars(wave, patch, tabs, far, inten, held)


def back_last(slot, counts, mine, other, measured, far, wave, patch, tabs, grad, bar, resid, held):
    n = mine.shape[0]
    h = n // 2
    live = jnp.where(slot < counts[0], 2.0, 0.0).astype(F32)
    r = (mine[...] + other[...] - measured[slot]) * live
    resid[0] = beside(r[:, :h], r[:, :h])
    resid[1] = beside(r[:, h:], r[:, h:])
    rows = by_mode(
        held,
        far.shape[0],
        lambda m: conj_dft_left(tabs, resid[0] * far[m, 0], resid[1] * far[m, 1]),
    )
    evens, odds = mm(held[:, :n], tabs[0]), mm(held[:, n:], tabs[1])
    g_re = g_im = 0.0
    o_re, o_im = patch[0], patch[1]
    for m, at in enumerate(rows):
        e, o = evens[at], odds[at]
        b_re = beside(e[:, :h] + o[:, :h], e[:, :h] - o[:, :h])
        b_im = beside(e[:, h:] + o[:, h:], e[:, h:] - o[:, h:])
        w_re, w_im = wave[m, 0], wave[m, 1]
        g_re += w_re * b_re + w_im * b_im
        g_im += w_re * b_im - w_im * b_re
        bar[m, 0] = (o_re * b_re + o_im * b_im).astype(BF16)
        bar[m, 1] = (o_re * b_im - o_im * b_re).astype(BF16)
    grad[0] = g_re
    grad[1] = g_im


def back_last_place_kernel(slot, counts, off, info, before, mine, other, measured, far, wave, patch,
                           tabs, bar, out_a, out_c, out_b, resid, held, grad, canvas):
    back_last(
        slot, counts, mine, other, measured, far, wave, patch, tabs, grad, bar, resid, held
    )
    lay(off, (before, grad), canvas)
    n = grad.shape[-1]
    h = n // 2
    sides(info, canvas, out_a, out_b)
    out_c[...] = canvas[:, :, h : h + n]


def back_first_kernel(info, bar, probe, patch, diag, corner, mat, keep, send, part, held):
    n = patch.shape[-1]
    rows = by_mode(
        held, probe.shape[1], lambda m: prop_left(diag, corner, bar[m, 0], bar[m, 1])
    )
    both = mm(held[...], mat[...])
    g_re = g_im = 0.0
    o_re, o_im = patch[0], patch[1]
    for m, at in enumerate(rows):
        b_re, b_im = both[at, :n], both[at, n:]
        p_re, p_im = probe[0, m], probe[1, m]
        g_re += p_re * b_re + p_im * b_im
        g_im += p_re * b_im - p_im * b_re
        part[0, m] = o_re * b_re + o_im * b_im
        part[1, m] = o_re * b_im - o_im * b_re
    first = info[4] == 0
    keep[0] = jnp.where(first, g_re, g_im)
    send[0] = jnp.where(first, g_im, g_re)


def probe_sum_kernel(part0, part1, total):
    total[0] = part0[...] + part1[...]


def sides(info, canvas, out_a, out_b):
    h = out_a.shape[-1]
    a, b, _ = ends(info, 1, 0, 3 * h)
    out_a[...] = canvas[:, :, pl.ds(a, h)]
    out_b[...] = canvas[:, :, pl.ds(b, h)]


def lay_sums(off, parts, canvas, sums):
    for slot in range(2):
        sums[slot] = parts[2 * slot][...] + parts[2 * slot + 1][...]
    lay(off, (sums.at[0], sums.at[1]), canvas)


def place_sides_kernel(off, info, keep0, got0, keep1, got1, out_a, out_b, canvas, sums):
    lay_sums(off, (keep0, got0, keep1, got1), canvas, sums)
    sides(info, canvas, out_a, out_b)


def place_center_kernel(off, keep0, got0, keep1, got1, out_c, canvas, sums):
    lay_sums(off, (keep0, got0, keep1, got1), canvas, sums)
    h = keep0.shape[-1] // 2
    out_c[...] = canvas[:, :, h : 3 * h]


def fold_cols_kernel(info, center, got_a, got_b, out_a, mid, out_b):
    n = center.shape[-1]
    h = n // 2
    ca, cb, col_ok = ends(info, 1, 0, h)
    ra, rb, _ = ends(info, 0, 0, h + n)
    for a, out in ((ra, out_a), (rb, out_b)):
        out[:, :, pl.ds(ca, h)] = center[:, pl.ds(a, h), pl.ds(ca, h)] + got_a[:, pl.ds(a, h)]
        out[:, :, pl.ds(cb, h)] = center[:, pl.ds(a, h), pl.ds(cb, h)] + kept(
            col_ok, got_b[:, pl.ds(a, h)]
        )
    mid[:, :, pl.ds(ca, h)] = center[:, h : h + n, pl.ds(ca, h)] + got_a[:, h : h + n]
    mid[:, :, pl.ds(cb, h)] = center[:, h : h + n, pl.ds(cb, h)] + kept(
        col_ok, got_b[:, h : h + n]
    )


def fold_rows_kernel(info, mid, got_a, got_b, *outs):
    h = got_a.shape[1]
    ra, rb, row_ok = ends(info, 0, 0, h)
    for plane, out in enumerate(outs):
        out[0, pl.ds(ra, h)] = mid[plane, pl.ds(ra, h)] + got_a[plane]
        out[0, pl.ds(rb, h)] = mid[plane, pl.ds(rb, h)] + kept(row_ok, got_b[plane])


def finish_last_kernel(info, mine_first, mine_re, other_re, mine_im, other_im, out, sums, sems):
    sums[0] = mine_re[0] + other_re[0]
    sums[1] = mine_im[0] + other_im[0]
    moves = ((sums.at[0], out.at[0, 0, 1]), (sums.at[1], out.at[0, 1, 1]),
             (mine_first.at[0], out.at[0, info[4], 0]))
    copies = [pltpu.make_async_copy(a, b, sems.at[i]) for i, (a, b) in enumerate(moves)]
    for copy in copies:
        copy.start()
    for copy in copies:
        copy.wait()


def finish_kernel(info, other_first, partial, out, sems):
    copy = pltpu.make_async_copy(other_first.at[0], out.at[0, 1 - info[4], 0], sems.at[0])
    copy.start()
    copy.wait()


def pick_rows_kernel(info, own, *refs):
    *outs, sems = refs
    h = outs[0].shape[1]
    a, b, _ = ends(info, 0, 0, h)
    copies = []
    for layer in range(2):
        for i, start in enumerate((a, b)):
            k = 2 * layer + i
            copies.append(pltpu.make_async_copy(
                own.at[:, layer, pl.ds(start, h), :], outs[k], sems.at[k]))
    for copy in copies:
        copy.start()
    for copy in copies:
        copy.wait()


def pick_cols_kernel(info, own, out_b):
    h = out_b.shape[-1]
    _, b, _ = ends(info, 1, 0, h)
    out_b[...] = own[:, :, :, pl.ds(b, h)]


def pick_rest_kernel(layer, info, own, rows_a, rows_b, out_a, corners_b):
    n = own.shape[-1]
    h = n // 2
    ra, rb, row_ok = ends(info, 0, 0, h + n)
    a, b, _ = ends(info, 1, 0, h)
    a, b = pl.ds(a, h), pl.ds(b, h)
    out_a[:, h : h + n] = own[:, layer, :, a]
    out_a[:, pl.ds(ra, h)] = rows_a[:, :, a]
    out_a[:, pl.ds(rb, h)] = kept(row_ok, rows_b[:, :, a])
    corners_b[0] = rows_a[:, :, b]
    corners_b[1] = rows_b[:, :, b]


def prepare_kernel(prop_in, probe_in, tabs_in, diag, corner, right, back_diag, back_corner,
                   back_right, probe_out, tabs_out, prop, sems):
    copies = [
        pltpu.make_async_copy(prop_in, prop, sems.at[0]),
        pltpu.make_async_copy(probe_in, probe_out, sems.at[1]),
        pltpu.make_async_copy(tabs_in, tabs_out, sems.at[2]),
    ]
    for copy in copies:
        copy.start()
    copies[0].wait()
    re, im = prop[0].astype(F32), prop[1].astype(F32)
    re_t, im_t = re.T, im.T
    for out, edge, pair in ((diag, corner, (re, im)), (back_diag, back_corner, (re_t, -im_t))):
        blocks, corners = band_left(*pair)
        out[0] = blocks[0].astype(BF16)
        out[1] = blocks[1].astype(BF16)
        edge[...] = corners.astype(BF16)
    right[...] = right_form(re_t, im_t, jnp).astype(BF16)
    back_right[...] = right_form(re, -im, jnp).astype(BF16)
    copies[1].wait()
    copies[2].wait()


def reorder_kernel(measured, out):
    n = out.shape[-1]
    h = n // 2
    exact = functools.partial(
        jnp.dot, precision=lax.Precision.HIGHEST, preferred_element_type=F32
    )

    def order(to, of):
        a = lax.broadcasted_iota(jnp.int32, (n, n), to)
        b = lax.broadcasted_iota(jnp.int32, (n, n), of)
        return jnp.where(jnp.where(a < h, 2 * a, 2 * a - n + 1) == b, 1.0, 0.0).astype(F32)

    for slot in range(out.shape[0]):
        out[slot] = exact(exact(order(0, 1), measured[slot]), order(1, 0))


def swap(value, axis, second):
    count = lax.axis_size("tile")
    step, length = (GY, count // GY) if axis == 0 else (1, GY)
    pairs = []
    for i in range(count):
        at = i // step % length
        to = (at + (1 if (at % 2 == 1) == second else -1)) % length
        pairs.append((i, i + (to - at) * step))
    return lax.ppermute(value, "tile", pairs)


def swap_mode(value):
    return lax.ppermute(value, "mode", [(0, 1), (1, 0)])


def call(kernel, name, outs, args, scratch=(), smem=1, after=(), copies=0, out=None, alias=None):
    vmem = pl.BlockSpec(memory_space=pltpu.VMEM)
    held = pl.BlockSpec(memory_space=pltpu.HBM) if copies and out is None else vmem
    out = vmem if out is None else pl.BlockSpec(memory_space=out)
    scalars = pl.BlockSpec(memory_space=pltpu.SMEM)
    n_args, n_after = len(args), len(after)

    def run(*refs):
        kept_args = n_args if alias is None else n_args + n_after
        kernel(*refs[:kept_args], *refs[n_args + n_after :])

    return pl.pallas_call(
        run,
        out_shape=tuple(jax.ShapeDtypeStruct(shape, dtype) for shape, dtype in outs),
        in_specs=[scalars] * smem
        + [held] * (n_args - smem)
        + [pl.BlockSpec(memory_space=pl.ANY)] * n_after,
        out_specs=tuple(out for _ in outs),
        input_output_aliases={} if alias is None else {alias: 0},
        scratch_shapes=[pltpu.VMEM(shape, dtype) for shape, dtype in scratch]
        + [pltpu.SemaphoreType.DMA((copies,))] * (copies > 0),
        compiler_params=pltpu.CompilerParams(vmem_limit_bytes=VMEM_LIMIT),
        name=name,
    )(*args, *after)


def body(object_tiles, probe_modes, propagator, offsets, counts, measured):
    n = probe_modes.shape[-1]
    h = n // 2
    modes = probe_modes.shape[1]
    slots = measured.shape[1]
    own = object_tiles[0]
    off = offsets[0]

    tile = lax.axis_index("tile")
    row, col = tile // GY, tile % GY
    n_rows = lax.axis_size("tile") // GY
    odd_row, odd_col = row % 2 == 1, col % 2 == 1
    paired = [(row > 0) & (row < n_rows - 1), (col > 0) & (col < GY - 1)]
    info = jnp.stack([odd_row, odd_col, *paired, lax.axis_index("mode") == 1]).astype(jnp.int32)

    one, pair, mat = ((1, n, n), F32), ((2, n, n), F32), ((2 * n, 2 * n), BF16)
    plane, field, probes = ((n, n), F32), ((modes, 2, n, n), F32), ((2, modes, n, n), F32)
    band = (((2, n, n), BF16), ((4 * BAND, 4 * BAND), BF16), mat)
    held = ((modes * n, 2 * n), BF16)
    strip, tall = ((2, h, n), F32), ((2, 2 * n, h), F32)
    side_strip, quarter = ((2, 2, n, h), F32), ((2, 2, h, h), F32)

    picked = call(pick_rows_kernel, "pick_rows", (strip,) * 4, (info, own), copies=4)
    rows = [[swap(picked[2 * i + k], 0, k == 1) for k in range(2)] for i in range(2)]
    (picked,) = call(pick_cols_kernel, "pick_cols", (side_strip,), (info, own), after=())
    cols_b = swap(picked, 1, True)

    def beside_tiles(layer, after):
        picked = call(functools.partial(pick_rest_kernel, layer), f"pick_rest_{layer}",
                      (tall, quarter), (info, own, *rows[layer]), after=after)
        rest = [swap(picked[k], 1, k == 1) for k in range(2)]
        return (own, *rows[layer], cols_b, *rest, picked[0])

    first = beside_tiles(0, ())
    tabs = jnp.asarray(dft_tables(n))
    *made, probe, tabs = call(
        prepare_kernel,
        "prepare",
        band + band + (probes, (tabs.shape, BF16)),
        (propagator, probe_modes, tabs),
        scratch=(((2, n, n), BF16),),
        smem=0,
        copies=3,
        after=(first[6],),
    )
    prop, back_prop = made[:3], made[3:]
    last = beside_tiles(1, (probe, first[3], first[5]))
    canvas, patch_first0, wave0 = call(
        waves_first_kernel,
        "waves_0",
        (((2, 2 * n, 2 * n), F32), pair, field),
        (off, info, *first[:6], probe, *prop),
        scratch=(held,),
        smem=2,
        after=(),
    )
    patch_first1, wave1 = call(
        waves_next_kernel, "waves_1", (pair, field), (off, canvas, probe, *prop), scratch=(held,),
        after=()
    )
    canvas, patch_last0, far0, inten0 = call(
        fars_first_kernel,
        "fars_0",
        (((2, 2 * n, 2 * n), F32), pair, field, plane),
        (off, info, *last[:6], wave0, tabs),
        scratch=(held,),
        smem=2,
        after=(patch_first1,),
    )
    other0 = swap_mode(inten0)
    patch_last1, far1, inten1 = call(
        fars_next_kernel, "fars_1", (pair, field, plane), (off, canvas, wave1, tabs), scratch=(held,)
    )
    other1 = swap_mode(inten1)
    (measured,) = call(
        reorder_kernel,
        "reorder",
        (((slots, n, n), F32),),
        (measured[0],),
        smem=0,
        after=(),
    )

    bar_out = ((modes, 2, n, n), BF16)
    strips = (((2, 2 * n, h), F32), ((2, 2 * n, n), F32), ((2, 2 * n, h), F32))
    wide = ((2, 2 * n, 2 * n), F32)
    grad_last0, bar0 = call(
        functools.partial(back_last, 0),
        "back_last_0",
        (pair, bar_out),
        (counts, inten0, other0, measured, far0, wave0, patch_last0, tabs),
        scratch=(pair, held),
    )
    keep0, send0, part0 = call(
        back_first_kernel,
        "back_first_0",
        (one, one, probes),
        (info, bar0, probe, patch_first0, *back_prop),
        scratch=(held,),
    )
    got0 = swap_mode(send0)
    bar1, out_a, out_c, out_b = call(
        functools.partial(back_last_place_kernel, 1),
        "back_last_1",
        (bar_out,) + strips,
        (counts, off, info, grad_last0, inten1, other1, measured, far1, wave1, patch_last1, tabs),
        scratch=(pair, held, pair, wide),
        smem=3,
        after=(keep0,),
    )

    def fold_cols(name, out_a, out_c, out_b, after):
        got_a, got_b = swap(out_a, 1, False), swap(out_b, 1, True)
        planes = out_c.shape[0]
        half, mid = ((planes, h, n), F32), ((planes, n, n), F32)
        return call(fold_cols_kernel, name, (half, mid, half), (info, out_c, got_a, got_b),
                    after=after)

    def fold_rows(name, out_a, mid, out_b, after):
        got_a, got_b = swap(out_a, 0, False), swap(out_b, 0, True)
        return call(fold_rows_kernel, name, (one,) * mid.shape[0], (info, mid, got_a, got_b),
                    after=after)

    keep1, send1, part1 = call(
        back_first_kernel,
        "back_first_1",
        (one, one, probes),
        (info, bar1, probe, patch_first1, *back_prop),
        scratch=(held,),
    )
    got1 = swap_mode(send1)
    strips_last = fold_cols("cols_last", out_a, out_c, out_b, (keep1,))
    mine_re, mine_im = fold_rows("rows_last", *strips_last, ())
    other_re, other_im = swap_mode(mine_re), swap_mode(mine_im)
    strips = [((1,) + shape[1:], dtype) for shape, dtype in strips]
    wide = ((1, 2 * n, 2 * n), F32)
    parts = (keep0, got0, keep1, got1)
    out_a, out_b = call(
        place_sides_kernel,
        "place_sides",
        (strips[0], strips[2]),
        (off, info, *parts),
        scratch=(wide, ((2, 1, n, n), F32)),
        smem=2,
        after=(strips_last[0],),
    )
    (out_c,) = call(
        place_center_kernel,
        "place_center",
        (strips[1],),
        (off, *parts),
        scratch=(wide, ((2, 1, n, n), F32)),
        after=(out_a,),
    )
    strips_first = fold_cols("cols_first", out_a, out_c, out_b, ())
    (mine_first,) = fold_rows("rows_first", *strips_first, (other_re,))
    other_first = swap_mode(mine_first)
    (probe_grad,) = call(
        probe_sum_kernel,
        "probe_sum",
        (((1, 2, modes, n, n), F32),),
        (part0, part1),
        smem=0,
        after=(),
    )
    shape = ((object_tiles.shape, F32),)
    (partial,) = call(
        finish_last_kernel,
        "finish_last",
        shape,
        (info, mine_first, mine_re, other_re, mine_im, other_im),
        scratch=(pair,),
        copies=3,
        out=pl.ANY,
    )
    (object_grad,) = call(
        finish_kernel,
        "finish",
        shape,
        (info, other_first),
        after=(partial,),
        copies=1,
        out=pl.ANY,
        alias=2,
    )
    return (object_grad, probe_grad)


def solution(mesh):
    placed = (
        P("tile", None, None, None, None),
        P(None, "mode", None, None),
        P(),
        P("tile", None, None),
        P("tile"),
        P("tile", None, None, None),
    )
    return jax.shard_map(
        body,
        mesh=mesh,
        in_specs=placed,
        out_specs=(P("tile", None, None, None, None), P("tile", None, "mode", None, None)),
        check_vma=False,
    )
```
